32 devices in a mesh: rows: 8 (over z, y), cols: 4 (over x, core).
Axes of the slice: x: 2, y: 2, z: 4, core: 2. Of those that a mesh axis runs over, the one named last changes fastest.
Arguments:
- coupling: float32 [256, 4, 2, 128, 128], P('rows', 'cols'), may hold values from 1.9 to 2120
- coupling_index: int32 [256, 4, 2], P('rows', 'cols'), may hold values from 0 to 7, as said below
- near_cost: float32 [256, 3, 128, 128], P('rows'), may hold values from 0 to 2
- near_index: int32 [256, 3], P('rows'), may hold values from 0 to 255, as said below
- source_weights: int32 [32768], P('rows'), may hold values from 1 to 98
- target_cost: float32 [4, 8, 3, 128, 128], P('cols', 'rows'), may hold values from 0 to 2
- target_index: int32 [4, 8, 3], P('cols'), may hold values from 0 to 7, as said below
- target_weights: int32 [4, 1024], P('cols', 'rows'), may hold values from 1 to 98
Outputs:
- cost_blocks: float32 [256, 4, 2, 128, 128], P('rows', 'cols')
- source_potential: float32 [32768], P('rows')
- target_potential: float32 [4, 1024], P('cols', 'rows')
The draws below stay inside these ranges and needn't reach their ends.
Inputs may be any that keep to these rules, and one draw needn't show every extreme that they name: `coupling_index`: the 2 entries of one block row and group differ; every target block of every group is named by some block row. near_index[i, 0] = i; the 3 entries of a row differ and lie in the same aligned group of 4 block rows as i. target_index[c, j, 0] = j; the 3 entries of a row differ.
All inputs are finite; a program needn't handle non-finite values.
Results may differ from the reference program's by a relative error of at most 0.0003.
Values sent between devices are 32-bit elements; how exact they have to be, the bound alone decides.
No kernel may reach another device: no remote copies, remote signals or barrier semaphores. Data moves between devices by JAX's collectives and lax.ppermute only.
A program may use at most 256 MiB of HBM per device.

```python
import jax
import jax.numpy as jnp
from jax import lax

BLK = 128
KC1 = 3
KC2 = 3
KPC = 2
SUB = 4
ITERS = 3
GROUPS = 4
KP = 8
NB = 256
NS = 32768
GB = 8
NT = 4096


def draw_coupling(key, part):
    key = jax.random.fold_in(key, 6)
    shape = (NB, GROUPS, KPC, BLK, BLK)
    spread = jax.random.truncated_normal(key, -3.5, 3.5, shape, jnp.float32)
    return 64.0 * jnp.exp(spread)


def draw_coupling_index(key, part):
    key = jax.random.fold_in(key, 1)
    first_key, second_key = jax.random.split(key)
    block_rows = jnp.arange(NB, dtype=jnp.int32)
    anchors = jax.random.randint(first_key, (NB // SUB, GROUPS), 0, GB, dtype=jnp.int32)[block_rows // SUB]
    jitter = jax.random.randint(second_key, (NB, GROUPS), 0, 2, dtype=jnp.int32)
    second = jnp.broadcast_to((block_rows % GB)[:, None], (NB, GROUPS))
    first = (anchors + jitter) % GB
    first = jnp.where(first == second, (first + 1) % GB, first)
    return jnp.stack([first, second], axis=-1)


def draw_near_index(key, part):
    key = jax.random.fold_in(key, 2)
    first_key, second_key = jax.random.split(key)
    block_rows = jnp.arange(NB, dtype=jnp.int32)
    inside = block_rows % SUB
    start = block_rows - inside
    offset_one = jax.random.randint(first_key, (NB,), 1, SUB, dtype=jnp.int32)
    turn = jax.random.randint(second_key, (NB,), 0, SUB - 2, dtype=jnp.int32)
    offset_two = (offset_one + turn) % (SUB - 1) + 1
    return jnp.stack([block_rows, start + (inside + offset_one) % SUB, start + (inside + offset_two) % SUB], axis=-1)


def draw_target_index(key, part):
    key = jax.random.fold_in(key, 3)
    first_key, second_key = jax.random.split(key)
    target_rows = jnp.broadcast_to(jnp.arange(GB, dtype=jnp.int32)[None, :], (GROUPS, GB))
    ahead = jax.random.randint(first_key, (GROUPS, GB), 1, 3, dtype=jnp.int32)
    behind = jax.random.randint(second_key, (GROUPS, GB), 1, 3, dtype=jnp.int32)
    return jnp.stack([target_rows, (target_rows + ahead) % GB, (target_rows + GB - behind) % GB], axis=-1)


def draw_source_weights(key, part):
    key = jax.random.fold_in(key, 4)
    places = jnp.arange(NS, dtype=jnp.int32)
    upper = 34 + 66 * places // NS
    return jax.random.randint(key, (NS,), 1, upper, dtype=jnp.int32)


def draw_target_weights(key, part):
    key = jax.random.fold_in(key, 5)
    places = jnp.arange(NT, dtype=jnp.int32)
    upper = 34 + 66 * places // NT
    return jax.random.randint(key, (NT,), 1, upper, dtype=jnp.int32).reshape(GROUPS, GB * BLK)


def block_scale(own_key, dims, shards, smallest, top_value):
    def one(axis_at, shards_of):
        draws = jax.random.uniform(jax.random.fold_in(jax.random.fold_in(own_key, 6), axis_at), (shards_of,), jnp.float32, smallest / len(shards), top_value / len(shards))
        return jnp.repeat(jnp.exp(draws), dims[axis_at] // shards_of).reshape((-1,) + (1,) * (len(dims) - axis_at - 1))

    level = one(*shards[0])
    for cut in shards[1:]:
        level = level * one(*cut)
    return level


def setup_inputs(seed: int = 0) -> dict:
    key_of = jax.random.split(jax.random.key(seed), 9)
    return {
        "coupling": draw_coupling(jax.random.fold_in(key_of[8], 71), 0),
        "coupling_index": draw_coupling_index(jax.random.fold_in(key_of[8], 71), 0),
        "near_cost": jnp.clip(2.0 * jax.random.uniform(key_of[2], (NB, KC1, BLK, BLK), jnp.float32) ** block_scale(key_of[2], (NB, KC1, BLK, BLK), ((0, 8),), -0.2, 0.2), 0.0, 2.0),
        "near_index": draw_near_index(jax.random.fold_in(key_of[8], 71), 0),
        "source_weights": draw_source_weights(jax.random.fold_in(key_of[8], 71), 0),
        "target_cost": jnp.clip(2.0 * jax.random.uniform(key_of[5], (GROUPS, GB, KC2, BLK, BLK), jnp.float32) ** block_scale(key_of[5], (GROUPS, GB, KC2, BLK, BLK), ((0, 4), (1, 8)), -0.2, 0.2), 0.0, 2.0),
        "target_index": draw_target_index(jax.random.fold_in(key_of[8], 71), 0),
        "target_weights": draw_target_weights(jax.random.fold_in(key_of[8], 71), 0),
    }


entropy = 0.01
full_precision = lax.Precision.HIGHEST


def reference(coupling, coupling_index, near_cost, near_index, source_weights, target_cost, target_index, target_weights):
    source_float = source_weights.astype(jnp.float32)
    source_mass = (NS * source_float / jnp.sum(source_float)).reshape(NB, BLK)
    target_float = target_weights.astype(jnp.float32)
    target_mass = (NT * target_float / jnp.sum(target_float)).reshape(GROUPS, GB, BLK)
    scale_near = 1.0 / (KC1 * BLK)
    scale_far = 1.0 / (KP * BLK)
    row_term = jnp.einsum("ikxy,iky->ix", near_cost * near_cost, source_mass[near_index], precision=full_precision) * scale_near
    spread_terms = jnp.einsum("cjw,cjmwz->cjmz", target_mass, target_cost * target_cost, precision=full_precision)
    one_hot = (target_index[..., None] == jnp.arange(GB)[None, None, None, :]).astype(jnp.float32)
    column_term = jnp.einsum("cjmz,cjmt->ctz", spread_terms, one_hot, precision=full_precision) / (KC2 * BLK)
    group_ids = jnp.arange(GROUPS)[None, :, None]

    def one_row(row_args):
        row_cost, row_near, row_slots = row_args
        far_plan = coupling[row_near]
        partial_blocks = jnp.einsum("kxy,kcqyz->kcqxz", row_cost, far_plan, precision=full_precision)
        far_slots = coupling_index[row_near]
        far_blocks = target_cost[group_ids, far_slots]
        through = jnp.einsum("kcqxy,kcqmyz->kcqmxz", partial_blocks, far_blocks, precision=full_precision)
        landing = target_index[group_ids, far_slots]
        match = (landing[..., None] == row_slots[None, :, None, None, :]).astype(jnp.float32)
        return jnp.einsum("kcqmxz,kcqml->clxz", through, match, precision=full_precision)

    product = lax.map(one_row, (near_cost, near_index, coupling_index))
    column_slots = column_term[group_ids, coupling_index]
    cost_blocks = row_term[:, None, None, :, None] + column_slots[:, :, :, None, :] - 2.0 * scale_near * scale_far * product
    log_source = jnp.log(source_mass)
    log_target = jnp.log(target_mass).reshape(GROUPS * GB, BLK)
    segment_ids = (group_ids * GB + coupling_index).reshape(-1)
    target_potential = jnp.zeros((GROUPS, GB, BLK), jnp.float32)
    source_potential = jnp.zeros((NB, BLK), jnp.float32)
    for step in range(ITERS):
        gathered = target_potential[group_ids, coupling_index]
        scores = (gathered[:, :, :, None, :] - cost_blocks) / entropy
        row_peak = jnp.max(scores, axis=(1, 2, 4))
        row_total = jnp.sum(jnp.exp(scores - row_peak[:, None, None, :, None]), axis=(1, 2, 4))
        source_potential = entropy * (log_source - (row_peak + jnp.log(row_total)))
        back_scores = (source_potential[:, None, None, :, None] - cost_blocks) / entropy
        slot_peak = jnp.max(back_scores, axis=3).reshape(-1, BLK)
        column_peak = jax.ops.segment_max(slot_peak, segment_ids, num_segments=GROUPS * GB)
        shifted = back_scores - column_peak[segment_ids].reshape(NB, GROUPS, KPC, 1, BLK)
        slot_total = jnp.sum(jnp.exp(shifted), axis=3).reshape(-1, BLK)
        column_total = jax.ops.segment_sum(slot_total, segment_ids, num_segments=GROUPS * GB)
        target_potential = (entropy * (log_target - (column_peak + jnp.log(column_total)))).reshape(GROUPS, GB, BLK)
    return cost_blocks, source_potential.reshape(NS), target_potential.reshape(GROUPS, GB * BLK)
```

```python
import functools
import math

import jax
import jax.numpy as jnp
from jax import lax
from jax.experimental import pallas as pl
from jax.experimental.pallas import tpu as pltpu
from jax.sharding import PartitionSpec as P

ITERS = 3
SUB = 4

entropy = 0.01
to_log2 = math.log2(math.e) / entropy
from_log2 = entropy * math.log(2.0)
very_low = -1e30
vmem_bytes = 40 * 1024 * 1024

SMEM = pl.BlockSpec(memory_space=pltpu.SMEM)


def whole(shape):
    return pl.BlockSpec(shape, lambda *_: (0,) * len(shape))


def split(x):
    high = x.astype(jnp.bfloat16)
    return high, (x - high.astype(jnp.float32)).astype(jnp.bfloat16)


def tree(parts, op):
    while len(parts) > 1:
        half = len(parts) // 2
        parts = [op(parts[s], parts[s + half]) for s in range(half)]
    return parts[0]


def log_sum(parts):
    peak = tree(parts, jnp.maximum)
    return peak + jnp.log2(tree([jnp.exp2(p - peak) for p in parts], jnp.add))


def send(x, axis, mask):
    size = lax.axis_size(axis)
    return lax.ppermute(x, axis, [(d, d ^ mask) for d in range(size)])


def exchange(x, axis):
    return [x] + [send(x, axis, s) for s in range(1, lax.axis_size(axis))]


def pack_kernel(source_ref, target_ref, out_ref):
    out_ref[...] = jnp.zeros_like(out_ref)
    for place, ref in enumerate((source_ref, target_ref)):
        total = jnp.sum(ref[...].astype(jnp.float32), axis=(0, 1), keepdims=True)
        out_ref[place : place + 1, :] = jnp.broadcast_to(total, (1, out_ref.shape[1]))
    out_ref[2 : 2 + target_ref.shape[0], :] = target_ref[...].astype(jnp.float32)


def near_kernel(near_index_ref, cost_ref, plan_ref, mass_ref, high_ref, low_ref, term_ref, plan_scr):
    g = pl.program_id(0)
    near_count = cost_ref.shape[1]
    width = cost_ref.shape[2]
    slots = plan_ref.shape[2]
    wide = slots * width
    for a in range(SUB):
        plan = jnp.concatenate([plan_ref[a, 0, q] for q in range(slots)], axis=1)
        high, low = split(plan)
        plan_scr[a, 0:width, :] = high
        plan_scr[a, width : 2 * width, :] = low
        plan_scr[a, 2 * width : 3 * width, :] = high
    lanes = lax.broadcasted_iota(jnp.int32, (width, SUB), 1)
    terms = jnp.zeros((width, SUB), jnp.float32)
    for i in range(SUB):
        acc = None
        for k in range(near_count):
            a = near_index_ref[k, g * SUB + i] & (SUB - 1)
            cost = cost_ref[i, k]
            high, low = split(cost)
            x = jnp.dot(
                jnp.concatenate([high, high, low], axis=1),
                plan_scr[a],
                preferred_element_type=jnp.float32,
            )
            x_high, x_low = split(x)
            high_ref[i, :, k * wide : (k + 1) * wide] = x_high
            low_ref[i, :, k * wide : (k + 1) * wide] = x_low
            weighted = cost * cost * mass_ref[pl.ds(g * SUB + a, 1), :].astype(jnp.float32)
            acc = weighted if acc is None else acc + weighted
        terms = jnp.where(lanes == i, jnp.sum(acc, axis=1, keepdims=True), terms)
    term_ref[0] = terms


def far_kernel(counts, row_axis, *refs):
    row_devices, target_here, source_count, target_count, group_blocks, link_count = counts
    near_index_ref, slot_ref, link_ref, high_ref, low_ref, term_ref, mass_ref = refs[:7]
    cost_parts = refs[7 : 7 + row_devices]
    packs = refs[7 + row_devices : 7 + 2 * row_devices]
    out_ref, peak_ref, log_source_ref, log_target_ref = refs[7 + 2 * row_devices : 11 + 2 * row_devices]
    far_high, far_low, table, column_scr, scale_scr, peak_scr, sum_scr = refs[11 + 2 * row_devices :]
    g = pl.program_id(0)
    steps = pl.num_programs(0)
    near_count = near_index_ref.shape[0]
    slots = slot_ref.shape[0]
    rows = high_ref.shape[0]
    width = high_ref.shape[1]
    zero_block = group_blocks * link_count

    @pl.when(g == 0)
    def _():
        me = lax.axis_index(row_axis)
        far_high[zero_block] = jnp.zeros((width, width), jnp.bfloat16)
        far_low[zero_block] = jnp.zeros((width, width), jnp.bfloat16)

        def clear(e, _):
            table[e] = zero_block
            return 0

        lax.fori_loop(0, group_blocks * group_blocks, clear, 0)

        def mark(j, _):
            for m in range(link_count):
                table[j * group_blocks + link_ref[m, 0, j]] = j * link_count + m
            return 0

        lax.fori_loop(0, group_blocks, mark, 0)
        total_source = tree([p[0:1, :] for p in packs], jnp.add)
        total_target = tree([p[1:2, :] for p in packs], jnp.add)
        log_source_ref[...] = jnp.log2(source_count * mass_ref[...].astype(jnp.float32) / total_source)
        scale_scr[...] = source_count / (total_source * (near_count * width))
        column_scr[...] = jnp.zeros_like(column_scr)
        for s in range(row_devices):
            for h in range(target_here):
                j = (me ^ s) * target_here + h
                mass = target_count * packs[s][2 + h : 3 + h, :] / total_target
                log_target_ref[pl.ds(j, 1), :] = jnp.log2(mass)
                tall = jnp.broadcast_to(mass, (width, width)).T
                for m in range(link_count):
                    block = cost_parts[s][0, h, m]
                    high, low = split(block)
                    far_high[j * link_count + m] = high
                    far_low[j * link_count + m] = low
                    spread = jnp.sum(tall * (block * block), axis=0, keepdims=True)
                    t = link_ref[m, 0, j]
                    column_scr[pl.ds(t, 1), :] += spread * (1.0 / (link_count * width))

    group_devices = target_count // (group_blocks * width)
    coef = 2.0 * (1.0 / (near_count * width)) * (1.0 / (slots * group_devices * width))
    lanes = lax.broadcasted_iota(jnp.int32, peak_scr.shape, 1)
    scale = scale_scr[0:1, 0:1]
    for i in range(rows):
        row = g * rows + i
        group = row - lax.rem(row, SUB)
        targets = [slot_ref[l, row] for l in range(slots)]
        far_rows = []
        for k in range(near_count):
            a = group + (near_index_ref[k, row] & (SUB - 1))
            for q in range(slots):
                j = slot_ref[q, a]
                far_rows.append([table[j * group_blocks + t] for t in targets])
        right_high = jnp.concatenate(
            [jnp.concatenate([far_high[e] for e in r], axis=1) for r in far_rows], axis=0
        )
        right_low = jnp.concatenate(
            [jnp.concatenate([far_low[e] for e in r], axis=1) for r in far_rows], axis=0
        )
        high = high_ref[i]
        product = jnp.dot(high, right_high, preferred_element_type=jnp.float32)
        product += jnp.dot(high, right_low, preferred_element_type=jnp.float32)
        product += jnp.dot(low_ref[i], right_high, preferred_element_type=jnp.float32)
        tall = term_ref[i // SUB, :, i % SUB : i % SUB + 1] * scale
        scores = []
        for l in range(slots):
            cost = tall + column_scr[pl.ds(targets[l], 1), :] - coef * product[:, l * width : (l + 1) * width]
            out_ref[i, 0, l] = cost
            scores.append(cost * -to_log2)
        row_pass(scores, row, lanes, peak_scr, sum_scr)

    @pl.when(g == steps - 1)
    def _():
        finish_rows(peak_ref, peak_scr, sum_scr)


def row_pass(scores, row, lanes, peak_scr, sum_scr):
    peak = jnp.max(functools.reduce(jnp.maximum, scores), axis=1, keepdims=True)
    total = functools.reduce(jnp.add, [jnp.exp2(s - peak) for s in scores])
    total = jnp.sum(total, axis=1, keepdims=True)
    peak_scr[...] = jnp.where(lanes == row, peak, peak_scr[...])
    sum_scr[...] = jnp.where(lanes == row, total, sum_scr[...])


def finish_rows(out_ref, peak_scr, sum_scr):
    rows = out_ref.shape[0]
    score = peak_scr[...] + jnp.log2(sum_scr[...])
    out_ref[...] = score.T[:rows, :]


def column_kernel(col_devices, *refs):
    cost_ref, select_ref, log_mass_ref = refs[:3]
    parts = refs[3 : 3 + col_devices]
    out_ref, potential_ref = refs[3 + col_devices : 5 + col_devices]
    potential_scr, peak_scr, sum_scr = refs[5 + col_devices :]
    g = pl.program_id(0)
    rows, _, slots, width, _ = cost_ref.shape

    @pl.when(g == 0)
    def _():
        scaled = log_mass_ref[...] - log_sum([p[...] for p in parts])
        potential_scr[...] = scaled
        potential_ref[...] = scaled * from_log2

    tall = potential_scr[pl.ds(pl.multiple_of(g * rows, rows), rows), :].T
    for i in range(rows):
        for l in range(slots):
            score = tall[:, i : i + 1] - cost_ref[i, 0, l] * to_log2
            peak = jnp.max(score, axis=0, keepdims=True)
            total = jnp.sum(jnp.exp2(score - peak), axis=0, keepdims=True)
            place = g * (rows * slots) + i * slots + l
            peak_scr[pl.ds(place, 1), :] = peak
            sum_scr[pl.ds(place, 1), :] = total

    @pl.when(g == pl.num_programs(0) - 1)
    def _():
        select = select_ref[...]
        peaks = peak_scr[...]
        sums = sum_scr[...]
        for t in range(out_ref.shape[0]):
            chosen = select == t
            peak = jnp.max(jnp.where(chosen, peaks, very_low), axis=0, keepdims=True)
            shifted = jnp.where(chosen, sums * jnp.exp2(jnp.minimum(peaks - peak, 0.0)), 0.0)
            total = jnp.sum(shifted, axis=0, keepdims=True)
            some = total > 0.0
            out_ref[t : t + 1, :] = jnp.where(
                some, peak + jnp.log2(jnp.where(some, total, 1.0)), very_low
            )


def row_kernel(row_devices, *refs):
    slot_ref, cost_ref, log_mass_ref = refs[:3]
    parts = refs[3 : 3 + row_devices]
    out_ref = refs[3 + row_devices]
    potential_scr, peak_scr, sum_scr = refs[4 + row_devices :]
    g = pl.program_id(0)
    rows, _, slots, _, _ = cost_ref.shape

    @pl.when(g == 0)
    def _():
        potential_scr[...] = log_mass_ref[...] - log_sum([p[...] for p in parts])

    lanes = lax.broadcasted_iota(jnp.int32, peak_scr.shape, 1)
    for i in range(rows):
        row = g * rows + i
        scores = [
            potential_scr[pl.ds(slot_ref[l, row], 1), :] - cost_ref[i, 0, l] * to_log2
            for l in range(slots)
        ]
        row_pass(scores, row, lanes, peak_scr, sum_scr)

    @pl.when(g == pl.num_programs(0) - 1)
    def _():
        finish_rows(out_ref, peak_scr, sum_scr)


def last_kernel(row_devices, target_here, row_axis, *refs):
    log_mass_ref = refs[0]
    parts = refs[1 : 1 + row_devices]
    out_ref, scr = refs[1 + row_devices :]
    scr[...] = (log_mass_ref[...] - log_sum([p[...] for p in parts])) * from_log2
    me = lax.axis_index(row_axis)
    for h in range(target_here):
        out_ref[h : h + 1, :] = scr[pl.ds(me * target_here + h, 1), :]


def per_device(
    coupling,
    coupling_index,
    near_cost,
    near_index,
    source_weights,
    target_cost,
    target_index,
    target_weights,
):
    rows_here = coupling.shape[0]
    slots = coupling.shape[2]
    width = coupling.shape[3]
    near_count = near_cost.shape[1]
    group_blocks = target_index.shape[1]
    link_count = target_index.shape[2]
    target_here = target_cost.shape[1]
    row_devices = lax.axis_size("rows")
    col_devices = lax.axis_size("cols")
    source_count = rows_here * row_devices * width
    target_count = group_blocks * width * col_devices
    f32 = jnp.float32
    params = pltpu.CompilerParams(vmem_limit_bytes=vmem_bytes)

    arrived = {0: target_cost}
    arrived[1] = send(target_cost, "rows", 1)
    for mask in range(2, row_devices, 2):
        arrived[mask] = send(target_cost, "rows", mask)
    for mask in range(2, row_devices, 2):
        arrived[mask + 1] = send(arrived[mask], "rows", 1)
    cost_parts = [arrived[s] for s in range(row_devices)]

    near_t = near_index.T
    slot_t = coupling_index[:, 0, :].T
    link_t = jnp.transpose(target_index, (2, 0, 1))
    mass = source_weights.reshape(rows_here, width)
    select = jnp.broadcast_to(
        coupling_index.reshape(rows_here * slots, 1), (rows_here * slots, width)
    )

    pack_rows = 8 * pl.cdiv(2 + target_here, 8)
    pack = pl.pallas_call(
        pack_kernel,
        out_shape=jax.ShapeDtypeStruct((pack_rows, width), f32),
        name="pack",
    )(mass, target_weights.reshape(target_here, width))
    target_sum = tree([p[1:2] for p in exchange(pack, "cols")], jnp.add)
    pack = jnp.concatenate([pack[0:1], target_sum, pack[2:]], axis=0)
    packs = exchange(pack, "rows")

    wide = near_count * slots * width
    groups = rows_here // SUB
    high, low, term = pl.pallas_call(
        near_kernel,
        grid=(groups,),
        in_specs=[
            SMEM,
            pl.BlockSpec((SUB, near_count, width, width), lambda g: (g, 0, 0, 0)),
            pl.BlockSpec((SUB, 1, slots, width, width), lambda g: (g, 0, 0, 0, 0)),
            whole((rows_here, width)),
        ],
        out_specs=[
            pl.BlockSpec((SUB, width, wide), lambda g: (g, 0, 0)),
            pl.BlockSpec((SUB, width, wide), lambda g: (g, 0, 0)),
            pl.BlockSpec((1, width, SUB), lambda g: (g, 0, 0)),
        ],
        out_shape=[
            jax.ShapeDtypeStruct((rows_here, width, wide), jnp.bfloat16),
            jax.ShapeDtypeStruct((rows_here, width, wide), jnp.bfloat16),
            jax.ShapeDtypeStruct((groups, width, SUB), f32),
        ],
        scratch_shapes=[pltpu.VMEM((SUB, 3 * width, slots * width), jnp.bfloat16)],
        compiler_params=params,
        cost_estimate=pl.CostEstimate(
            flops=6 * rows_here * wide * width * width,
            bytes_accessed=rows_here * width * (4 * near_count * width + 4 * slots * width + 4 * wide),
            transcendentals=0,
        ),
        name="near_product",
    )(near_t, near_cost, coupling, mass)

    step_rows = SUB
    steps = rows_here // step_rows
    cost_block = pl.BlockSpec((step_rows, 1, slots, width, width), lambda g: (g, 0, 0, 0, 0))
    cost_blocks, row_part, log_source, log_target = pl.pallas_call(
        functools.partial(
            far_kernel,
            (row_devices, target_here, source_count, target_count, group_blocks, link_count),
            "rows",
        ),
        grid=(steps,),
        in_specs=[
            SMEM,
            SMEM,
            SMEM,
            pl.BlockSpec((step_rows, width, wide), lambda g: (g, 0, 0)),
            pl.BlockSpec((step_rows, width, wide), lambda g: (g, 0, 0)),
            pl.BlockSpec((step_rows // SUB, width, SUB), lambda g: (g, 0, 0)),
            whole((rows_here, width)),
        ]
        + [whole(target_cost.shape)] * row_devices
        + [whole((pack_rows, width))] * row_devices,
        out_specs=[
            cost_block,
            whole((rows_here, width)),
            whole((rows_here, width)),
            whole((group_blocks, width)),
        ],
        out_shape=[
            jax.ShapeDtypeStruct(coupling.shape, f32),
            jax.ShapeDtypeStruct((rows_here, width), f32),
            jax.ShapeDtypeStruct((rows_here, width), f32),
            jax.ShapeDtypeStruct((group_blocks, width), f32),
        ],
        scratch_shapes=[
            pltpu.VMEM((group_blocks * link_count + 1, width, width), jnp.bfloat16),
            pltpu.VMEM((group_blocks * link_count + 1, width, width), jnp.bfloat16),
            pltpu.SMEM((group_blocks * group_blocks,), jnp.int32),
            pltpu.VMEM((group_blocks, width), f32),
            pltpu.VMEM((1, width), f32),
            pltpu.VMEM((width, width), f32),
            pltpu.VMEM((width, width), f32),
        ],
        compiler_params=params,
        name="far_product",
    )(near_t, slot_t, link_t, high, low, term, mass, *cost_parts, *packs)

    pass_rows = 8
    passes = rows_here // pass_rows
    pass_block = pl.BlockSpec((pass_rows, 1, slots, width, width), lambda g: (g, 0, 0, 0, 0))

    def column_step(row_parts):
        return pl.pallas_call(
            functools.partial(column_kernel, col_devices),
            grid=(passes,),
            in_specs=[pass_block, whole((rows_here * slots, width)), whole((rows_here, width))]
            + [whole((rows_here, width))] * col_devices,
            out_specs=[whole((group_blocks, width)), whole((rows_here, width))],
            out_shape=[
                jax.ShapeDtypeStruct((group_blocks, width), f32),
                jax.ShapeDtypeStruct((rows_here, width), f32),
            ],
            scratch_shapes=[
                pltpu.VMEM((rows_here, width), f32),
                pltpu.VMEM((rows_here * slots, width), f32),
                pltpu.VMEM((rows_here * slots, width), f32),
            ],
            compiler_params=params,
            name="column_pass",
        )(cost_blocks, select, log_source, *row_parts)

    def row_step(column_parts):
        return pl.pallas_call(
            functools.partial(row_kernel, row_devices),
            grid=(passes,),
            in_specs=[SMEM, pass_block, whole((group_blocks, width))]
            + [whole((group_blocks, width))] * row_devices,
            out_specs=whole((rows_here, width)),
            out_shape=jax.ShapeDtypeStruct((rows_here, width), f32),
            scratch_shapes=[
                pltpu.VMEM((group_blocks, width), f32),
                pltpu.VMEM((width, width), f32),
                pltpu.VMEM((width, width), f32),
            ],
            compiler_params=params,
            name="row_pass",
        )(slot_t, cost_blocks, log_target, *column_parts)

    for step in range(ITERS):
        column_part, source_potential = column_step(exchange(row_part, "cols"))
        column_parts = exchange(column_part, "rows")
        if step < ITERS - 1:
            row_part = row_step(column_parts)
    own_target = pl.pallas_call(
        functools.partial(last_kernel, row_devices, target_here, "rows"),
        out_shape=jax.ShapeDtypeStruct((target_here, width), f32),
        scratch_shapes=[pltpu.VMEM((group_blocks, width), f32)],
        name="last_potential",
    )(log_target, *column_parts)
    return (
        cost_blocks,
        source_potential.reshape(rows_here * width),
        own_target.reshape(1, target_here * width),
    )


def solution(mesh):
    placed = (
        P("rows", "cols", None, None, None),
        P("rows", "cols", None),
        P("rows", None, None, None),
        P("rows", None),
        P("rows"),
        P("cols", "rows", None, None, None),
        P("cols", None, None),
        P("cols", "rows"),
    )
    return jax.shard_map(
        per_device,
        mesh=mesh,
        in_specs=placed,
        out_specs=(P("rows", "cols", None, None, None), P("rows"), P("cols", "rows")),
        check_vma=False,
    )
```

```python
import functools
import math

import jax
import jax.numpy as jnp
from jax import lax
from jax.experimental import pallas as pl
from jax.experimental.pallas import tpu as pltpu
from jax.sharding import PartitionSpec as P

ITERS = 3
SUB = 4

entropy = 0.01
to_log2 = math.log2(math.e) / entropy
from_log2 = entropy * math.log(2.0)
very_low = -1e30
vmem_bytes = 40 * 1024 * 1024

SMEM = pl.BlockSpec(memory_space=pltpu.SMEM)


def whole(shape):
    return pl.BlockSpec(shape, lambda *_: (0,) * len(shape))


def split(x):
    high = x.astype(jnp.bfloat16)
    return high, (x - high.astype(jnp.float32)).astype(jnp.bfloat16)


def log_sum(parts):
    peak = functools.reduce(jnp.maximum, parts)
    return peak + jnp.log2(functools.reduce(jnp.add, [jnp.exp2(p - peak) for p in parts]))


def parts_of(ref, devices):
    rows = ref.shape[0] // devices
    return [ref[d * rows : (d + 1) * rows, :] for d in range(devices)]


def put_copies(ref, devices, value):
    rows = value.shape[0]
    for d in range(devices):
        ref[d * rows : (d + 1) * rows, :] = value


def send(x, axis, mask):
    size = lax.axis_size(axis)
    return lax.ppermute(x, axis, [(d, d ^ mask) for d in range(size)])


def exchange(copies, axis):
    return lax.all_to_all(copies, axis, 0, 0, tiled=True)


def pack_kernel(devices, source_ref, target_ref, out_ref):
    rows = out_ref.shape[0] // devices
    total = jnp.sum(source_ref[...].astype(jnp.float32), axis=(0, 1), keepdims=True)
    target = target_ref[...].astype(jnp.float32)
    out_ref[...] = jnp.zeros_like(out_ref)
    for d in range(devices):
        out_ref[d * rows : d * rows + 1, :] = jnp.broadcast_to(total, (1, out_ref.shape[1]))
        out_ref[d * rows + 1 : d * rows + 1 + target.shape[0], :] = target


def near_kernel(near_index_ref, cost_ref, plan_ref, mass_ref, high_ref, low_ref, term_ref, plan_scr):
    g = pl.program_id(0)
    near_count = cost_ref.shape[1]
    width = cost_ref.shape[2]
    slots = plan_ref.shape[2]
    wide = slots * width
    for a in range(SUB):
        plan = jnp.concatenate([plan_ref[a, 0, q] for q in range(slots)], axis=1)
        high, low = split(plan)
        plan_scr[a, 0:width, :] = high
        plan_scr[a, width : 2 * width, :] = low
        plan_scr[a, 2 * width : 3 * width, :] = high
    lanes = lax.broadcasted_iota(jnp.int32, (width, SUB), 1)
    terms = jnp.zeros((width, SUB), jnp.float32)
    for i in range(SUB):
        acc = None
        for k in range(near_count):
            a = near_index_ref[k, g * SUB + i] & (SUB - 1)
            cost = cost_ref[i, k]
            high, low = split(cost)
            x = jnp.dot(
                jnp.concatenate([high, high, low], axis=1),
                plan_scr[a],
                preferred_element_type=jnp.float32,
            )
            x_high, x_low = split(x)
            high_ref[i, :, k * wide : (k + 1) * wide] = x_high
            low_ref[i, :, k * wide : (k + 1) * wide] = x_low
            weighted = cost * cost * mass_ref[pl.ds(g * SUB + a, 1), :].astype(jnp.float32)
            acc = weighted if acc is None else acc + weighted
        terms = jnp.where(lanes == i, jnp.sum(acc, axis=1, keepdims=True), terms)
    term_ref[0] = terms


def far_kernel(counts, row_axis, *refs):
    row_devices, col_devices, target_here, source_count, target_count, group_blocks, link_count = counts
    near_index_ref, slot_ref, link_ref, high_ref, low_ref, term_ref, mass_ref = refs[:7]
    cost_parts = refs[7 : 7 + row_devices]
    pack_ref, out_ref, peak_ref, log_source_ref, log_target_ref = refs[7 + row_devices : 12 + row_devices]
    far_high, far_low, table, column_scr, scale_scr, peak_scr, sum_scr = refs[12 + row_devices :]
    g = pl.program_id(0)
    steps = pl.num_programs(0)
    near_count = near_index_ref.shape[0]
    slots = slot_ref.shape[0]
    rows = high_ref.shape[0]
    width = high_ref.shape[1]
    zero_block = group_blocks * link_count

    @pl.when(g == 0)
    def _():
        me = lax.axis_index(row_axis)
        far_high[zero_block] = jnp.zeros((width, width), jnp.bfloat16)
        far_low[zero_block] = jnp.zeros((width, width), jnp.bfloat16)

        def clear(e, _):
            table[e] = zero_block
            return 0

        lax.fori_loop(0, group_blocks * group_blocks, clear, 0)

        def mark(j, _):
            for m in range(link_count):
                table[j * group_blocks + link_ref[m, 0, j]] = j * link_count + m
            return 0

        lax.fori_loop(0, group_blocks, mark, 0)
        pack_rows = pack_ref.shape[0] // (row_devices * col_devices)
        total_source = functools.reduce(
            jnp.add,
            [pack_ref[r * col_devices * pack_rows : r * col_devices * pack_rows + 1, :] for r in range(row_devices)],
        )
        targets = functools.reduce(
            jnp.add,
            [
                pack_ref[d * pack_rows + 1 + h : d * pack_rows + 2 + h, :]
                for d in range(row_devices * col_devices)
                for h in range(target_here)
            ],
        )
        total_target = jnp.sum(targets, axis=1, keepdims=True)
        col = lax.axis_index("cols")
        log_source_ref[...] = jnp.log2(source_count * mass_ref[...].astype(jnp.float32) / total_source)
        scale_scr[...] = source_count / (total_source * (near_count * width))
        column_scr[...] = jnp.zeros_like(column_scr)
        for s in range(row_devices):
            for h in range(target_here):
                j = (me ^ s) * target_here + h
                place = ((me ^ s) * col_devices + col) * pack_rows + 1 + h
                mass = target_count * pack_ref[pl.ds(place, 1), :] / total_target
                log_target_ref[pl.ds(j, 1), :] = jnp.log2(mass)
                tall = jnp.broadcast_to(mass, (width, width)).T
                for m in range(link_count):
                    block = cost_parts[s][0, h, m]
                    high, low = split(block)
                    far_high[j * link_count + m] = high
                    far_low[j * link_count + m] = low
                    spread = jnp.sum(tall * (block * block), axis=0, keepdims=True)
                    t = link_ref[m, 0, j]
                    column_scr[pl.ds(t, 1), :] += spread * (1.0 / (link_count * width))

    group_devices = target_count // (group_blocks * width)
    coef = 2.0 * (1.0 / (near_count * width)) * (1.0 / (slots * group_devices * width))
    lanes = lax.broadcasted_iota(jnp.int32, peak_scr.shape, 1)
    scale = scale_scr[0:1, 0:1]
    for i in range(rows):
        row = g * rows + i
        group = row - lax.rem(row, SUB)
        targets = [slot_ref[l, row] for l in range(slots)]
        far_rows = []
        for k in range(near_count):
            a = group + (near_index_ref[k, row] & (SUB - 1))
            for q in range(slots):
                j = slot_ref[q, a]
                far_rows.append([table[j * group_blocks + t] for t in targets])
        right_high = jnp.concatenate(
            [jnp.concatenate([far_high[e] for e in r], axis=1) for r in far_rows], axis=0
        )
        right_low = jnp.concatenate(
            [jnp.concatenate([far_low[e] for e in r], axis=1) for r in far_rows], axis=0
        )
        high = high_ref[i]
        product = jnp.dot(high, right_high, preferred_element_type=jnp.float32)
        product += jnp.dot(high, right_low, preferred_element_type=jnp.float32)
        product += jnp.dot(low_ref[i], right_high, preferred_element_type=jnp.float32)
        tall = term_ref[i // SUB, :, i % SUB : i % SUB + 1] * scale
        scores = []
        for l in range(slots):
            cost = tall + column_scr[pl.ds(targets[l], 1), :] - coef * product[:, l * width : (l + 1) * width]
            out_ref[i, 0, l] = cost
            scores.append(cost * -to_log2)
        row_pass(scores, row, lanes, peak_scr, sum_scr)

    @pl.when(g == steps - 1)
    def _():
        finish_rows(col_devices, peak_ref, peak_scr, sum_scr)


def row_pass(scores, row, lanes, peak_scr, sum_scr):
    peak = jnp.max(functools.reduce(jnp.maximum, scores), axis=1, keepdims=True)
    total = functools.reduce(jnp.add, [jnp.exp2(s - peak) for s in scores])
    total = jnp.sum(total, axis=1, keepdims=True)
    peak_scr[...] = jnp.where(lanes == row, peak, peak_scr[...])
    sum_scr[...] = jnp.where(lanes == row, total, sum_scr[...])


def finish_rows(col_devices, out_ref, peak_scr, sum_scr):
    rows = out_ref.shape[0] // col_devices
    score = peak_scr[...] + jnp.log2(sum_scr[...])
    put_copies(out_ref, col_devices, score.T[:rows, :])


def column_kernel(
    col_devices,
    copies,
    cost_ref,
    select_ref,
    log_mass_ref,
    parts_ref,
    out_ref,
    potential_ref,
    potential_scr,
    peak_scr,
    sum_scr,
):
    g = pl.program_id(0)
    rows, _, slots, width, _ = cost_ref.shape

    @pl.when(g == 0)
    def _():
        scaled = log_mass_ref[...] - log_sum(parts_of(parts_ref, col_devices))
        potential_scr[...] = scaled
        potential_ref[...] = scaled * from_log2

    tall = potential_scr[pl.ds(pl.multiple_of(g * rows, rows), rows), :].T
    for i in range(rows):
        for l in range(slots):
            score = tall[:, i : i + 1] - cost_ref[i, 0, l] * to_log2
            peak = jnp.max(score, axis=0, keepdims=True)
            total = jnp.sum(jnp.exp2(score - peak), axis=0, keepdims=True)
            place = g * (rows * slots) + i * slots + l
            peak_scr[pl.ds(place, 1), :] = peak
            sum_scr[pl.ds(place, 1), :] = total

    @pl.when(g == pl.num_programs(0) - 1)
    def _():
        select = select_ref[...]
        peaks = peak_scr[...]
        sums = sum_scr[...]
        blocks = out_ref.shape[0] // copies
        for t in range(blocks):
            chosen = select == t
            peak = jnp.max(jnp.where(chosen, peaks, very_low), axis=0, keepdims=True)
            shifted = jnp.where(chosen, sums * jnp.exp2(jnp.minimum(peaks - peak, 0.0)), 0.0)
            total = jnp.sum(shifted, axis=0, keepdims=True)
            some = total > 0.0
            out_ref[t : t + 1, :] = jnp.where(
                some, peak + jnp.log2(jnp.where(some, total, 1.0)), very_low
            )
        if copies > 1:
            put_copies(out_ref, copies, out_ref[0:blocks, :])


def row_kernel(
    row_devices,
    col_devices,
    slot_ref,
    cost_ref,
    log_mass_ref,
    parts_ref,
    out_ref,
    potential_scr,
    peak_scr,
    sum_scr,
):
    g = pl.program_id(0)
    rows, _, slots, _, _ = cost_ref.shape

    @pl.when(g == 0)
    def _():
        potential_scr[...] = log_mass_ref[...] - log_sum(parts_of(parts_ref, row_devices))

    lanes = lax.broadcasted_iota(jnp.int32, peak_scr.shape, 1)
    for i in range(rows):
        row = g * rows + i
        scores = [
            potential_scr[pl.ds(slot_ref[l, row], 1), :] - cost_ref[i, 0, l] * to_log2
            for l in range(slots)
        ]
        row_pass(scores, row, lanes, peak_scr, sum_scr)

    @pl.when(g == pl.num_programs(0) - 1)
    def _():
        finish_rows(col_devices, out_ref, peak_scr, sum_scr)


def last_kernel(row_devices, row_axis, log_mass_ref, parts_ref, out_ref):
    here = out_ref.shape[0]
    start = lax.axis_index(row_axis) * here
    log_mass = log_mass_ref[pl.ds(start, here), :]
    out_ref[...] = (log_mass - log_sum(parts_of(parts_ref, row_devices))) * from_log2


def per_device(
    coupling,
    coupling_index,
    near_cost,
    near_index,
    source_weights,
    target_cost,
    target_index,
    target_weights,
):
    rows_here = coupling.shape[0]
    slots = coupling.shape[2]
    width = coupling.shape[3]
    near_count = near_cost.shape[1]
    group_blocks = target_index.shape[1]
    link_count = target_index.shape[2]
    target_here = target_cost.shape[1]
    row_devices = lax.axis_size("rows")
    col_devices = lax.axis_size("cols")
    source_count = rows_here * row_devices * width
    target_count = group_blocks * width * col_devices
    f32 = jnp.float32
    params = pltpu.CompilerParams(vmem_limit_bytes=vmem_bytes)

    arrived = {0: target_cost}
    arrived[1] = send(target_cost, "rows", 1)
    for mask in range(2, row_devices, 2):
        arrived[mask] = send(target_cost, "rows", mask)
    for mask in range(2, row_devices, 2):
        arrived[mask + 1] = send(arrived[mask], "rows", 1)
    cost_parts = [arrived[s] for s in range(row_devices)]

    near_t = near_index.T
    slot_t = coupling_index[:, 0, :].T
    link_t = jnp.transpose(target_index, (2, 0, 1))
    mass = source_weights.reshape(rows_here, width)
    select = jnp.broadcast_to(
        coupling_index.reshape(rows_here * slots, 1), (rows_here * slots, width)
    )

    pack_rows = 8 * pl.cdiv(1 + target_here, 8)
    devices = row_devices * col_devices
    pack = pl.pallas_call(
        functools.partial(pack_kernel, devices),
        out_shape=jax.ShapeDtypeStruct((devices * pack_rows, width), f32),
        name="pack",
    )(mass, target_weights.reshape(target_here, width))
    packs = exchange(pack, ("rows", "cols"))

    wide = near_count * slots * width
    groups = rows_here // SUB
    high, low, term = pl.pallas_call(
        near_kernel,
        grid=(groups,),
        in_specs=[
            SMEM,
            pl.BlockSpec((SUB, near_count, width, width), lambda g: (g, 0, 0, 0)),
            pl.BlockSpec((SUB, 1, slots, width, width), lambda g: (g, 0, 0, 0, 0)),
            whole((rows_here, width)),
        ],
        out_specs=[
            pl.BlockSpec((SUB, width, wide), lambda g: (g, 0, 0)),
            pl.BlockSpec((SUB, width, wide), lambda g: (g, 0, 0)),
            pl.BlockSpec((1, width, SUB), lambda g: (g, 0, 0)),
        ],
        out_shape=[
            jax.ShapeDtypeStruct((rows_here, width, wide), jnp.bfloat16),
            jax.ShapeDtypeStruct((rows_here, width, wide), jnp.bfloat16),
            jax.ShapeDtypeStruct((groups, width, SUB), f32),
        ],
        scratch_shapes=[pltpu.VMEM((SUB, 3 * width, slots * width), jnp.bfloat16)],
        compiler_params=params,
        cost_estimate=pl.CostEstimate(
            flops=6 * rows_here * wide * width * width,
            bytes_accessed=rows_here * width * (4 * near_count * width + 4 * slots * width + 4 * wide),
            transcendentals=0,
        ),
        name="near_product",
    )(near_t, near_cost, coupling, mass)

    step_rows = SUB
    steps = rows_here // step_rows
    cost_block = pl.BlockSpec((step_rows, 1, slots, width, width), lambda g: (g, 0, 0, 0, 0))
    cost_blocks, row_part, log_source, log_target = pl.pallas_call(
        functools.partial(
            far_kernel,
            (row_devices, col_devices, target_here, source_count, target_count, group_blocks, link_count),
            "rows",
        ),
        grid=(steps,),
        in_specs=[
            SMEM,
            SMEM,
            SMEM,
            pl.BlockSpec((step_rows, width, wide), lambda g: (g, 0, 0)),
            pl.BlockSpec((step_rows, width, wide), lambda g: (g, 0, 0)),
            pl.BlockSpec((step_rows // SUB, width, SUB), lambda g: (g, 0, 0)),
            whole((rows_here, width)),
        ]
        + [whole(target_cost.shape)] * row_devices
        + [whole(packs.shape)],
        out_specs=[
            cost_block,
            whole((col_devices * rows_here, width)),
            whole((rows_here, width)),
            whole((group_blocks, width)),
        ],
        out_shape=[
            jax.ShapeDtypeStruct(coupling.shape, f32),
            jax.ShapeDtypeStruct((col_devices * rows_here, width), f32),
            jax.ShapeDtypeStruct((rows_here, width), f32),
            jax.ShapeDtypeStruct((group_blocks, width), f32),
        ],
        scratch_shapes=[
            pltpu.VMEM((group_blocks * link_count + 1, width, width), jnp.bfloat16),
            pltpu.VMEM((group_blocks * link_count + 1, width, width), jnp.bfloat16),
            pltpu.SMEM((group_blocks * group_blocks,), jnp.int32),
            pltpu.VMEM((group_blocks, width), f32),
            pltpu.VMEM((1, width), f32),
            pltpu.VMEM((width, width), f32),
            pltpu.VMEM((width, width), f32),
        ],
        compiler_params=params,
        name="far_product",
    )(near_t, slot_t, link_t, high, low, term, mass, *cost_parts, packs)

    pass_rows = 8
    passes = rows_here // pass_rows
    pass_block = pl.BlockSpec((pass_rows, 1, slots, width, width), lambda g: (g, 0, 0, 0, 0))

    def column_step(row_parts, copies):
        return pl.pallas_call(
            functools.partial(column_kernel, col_devices, copies),
            grid=(passes,),
            in_specs=[
                pass_block,
                whole((rows_here * slots, width)),
                whole((rows_here, width)),
                whole(row_parts.shape),
            ],
            out_specs=[whole((copies * group_blocks, width)), whole((rows_here, width))],
            out_shape=[
                jax.ShapeDtypeStruct((copies * group_blocks, width), f32),
                jax.ShapeDtypeStruct((rows_here, width), f32),
            ],
            scratch_shapes=[
                pltpu.VMEM((rows_here, width), f32),
                pltpu.VMEM((rows_here * slots, width), f32),
                pltpu.VMEM((rows_here * slots, width), f32),
            ],
            compiler_params=params,
            name="column_pass",
        )(cost_blocks, select, log_source, row_parts)

    def row_step(column_parts):
        return pl.pallas_call(
            functools.partial(row_kernel, row_devices, col_devices),
            grid=(passes,),
            in_specs=[SMEM, pass_block, whole((group_blocks, width)), whole(column_parts.shape)],
            out_specs=whole((col_devices * rows_here, width)),
            out_shape=jax.ShapeDtypeStruct((col_devices * rows_here, width), f32),
            scratch_shapes=[
                pltpu.VMEM((group_blocks, width), f32),
                pltpu.VMEM((width, width), f32),
                pltpu.VMEM((width, width), f32),
            ],
            compiler_params=params,
            name="row_pass",
        )(slot_t, cost_blocks, log_target, column_parts)

    for step in range(ITERS):
        last = step == ITERS - 1
        column_part, source_potential = column_step(
            exchange(row_part, "cols"), 1 if last else row_devices
        )
        column_parts = exchange(column_part, "rows")
        if not last:
            row_part = row_step(column_parts)
    own_target = pl.pallas_call(
        functools.partial(last_kernel, row_devices, "rows"),
        out_shape=jax.ShapeDtypeStruct((target_here, width), f32),
        name="last_potential",
    )(log_target, column_parts)
    return (
        cost_blocks,
        source_potential.reshape(rows_here * width),
        own_target.reshape(1, target_here * width),
    )


def solution(mesh):
    placed = (
        P("rows", "cols", None, None, None),
        P("rows", "cols", None),
        P("rows", None, None, None),
        P("rows", None),
        P("rows"),
        P("cols", "rows", None, None, None),
        P("cols", None, None),
        P("cols", "rows"),
    )
    return jax.shard_map(
        per_device,
        mesh=mesh,
        in_specs=placed,
        out_specs=(P("rows", "cols", None, None, None), P("rows"), P("cols", "rows")),
        check_vma=False,
    )
```

```python
import functools
import math

import jax
import jax.numpy as jnp
from jax import lax
from jax.experimental import pallas as pl
from jax.experimental.pallas import tpu as pltpu
from jax.sharding import PartitionSpec as P

ITERS = 3
SUB = 4

entropy = 0.01
to_log2 = math.log2(math.e) / entropy
from_log2 = entropy * math.log(2.0)
very_low = -1e30
mib = 1024 * 1024

SMEM = pl.BlockSpec(memory_space=pltpu.SMEM)
VMEM = pl.BlockSpec(memory_space=pltpu.VMEM)
ANY = pl.BlockSpec(memory_space=pl.ANY)


def in_vmem(x):
    return pltpu.with_memory_space_constraint(x, pltpu.VMEM)


def whole(shape):
    return pl.BlockSpec(shape, lambda *_: (0,) * len(shape))


def split(x):
    high = x.astype(jnp.bfloat16)
    return high, (x - high.astype(jnp.float32)).astype(jnp.bfloat16)


def tree(parts, op):
    while len(parts) > 1:
        half = len(parts) // 2
        parts = [op(parts[s], parts[s + half]) for s in range(half)]
    return parts[0]


def log_sum(parts):
    peak = tree(parts, jnp.maximum)
    return peak + jnp.log2(tree([jnp.exp2(p - peak) for p in parts], jnp.add))


def parts_of(ref, devices):
    rows = ref.shape[0] // devices
    return [ref[d * rows : (d + 1) * rows, :] for d in range(devices)]


def put_copies(ref, devices, value):
    rows = value.shape[0]
    for d in range(devices):
        ref[d * rows : (d + 1) * rows, :] = value


def send(x, axis, mask):
    size = lax.axis_size(axis)
    return lax.ppermute(x, axis, [(d, d ^ mask) for d in range(size)])


def from_all(x, axis):
    return [x] + [send(x, axis, s) for s in range(1, lax.axis_size(axis))]


def exchange(copies, axis):
    return lax.all_to_all(copies, axis, 0, 0, tiled=True)


def pack_kernel(devices, source_ref, target_ref, out_ref):
    rows = out_ref.shape[0] // devices
    total = jnp.sum(source_ref[...].astype(jnp.float32), axis=(0, 1), keepdims=True)
    target = target_ref[...].astype(jnp.float32)
    out_ref[...] = jnp.zeros_like(out_ref)
    for d in range(devices):
        out_ref[d * rows : d * rows + 1, :] = jnp.broadcast_to(total, (1, out_ref.shape[1]))
        out_ref[d * rows + 1 : d * rows + 1 + target.shape[0], :] = target


def near_kernel(first, near_index_ref, cost_ref, plan_ref, mass_ref, *refs):
    x_ref, term_ref, plan_scr = refs[-3:]
    g = first + pl.program_id(0)
    near_count = cost_ref.shape[1]
    width = cost_ref.shape[2]
    slots = plan_ref.shape[2]
    wide = slots * width
    for a in range(SUB):
        plan = jnp.concatenate([plan_ref[a, 0, q] for q in range(slots)], axis=1)
        high, low = split(plan)
        plan_scr[a, 0:width, :] = high
        plan_scr[a, width : 2 * width, :] = low
        plan_scr[a, 2 * width : 3 * width, :] = high
    lanes = lax.broadcasted_iota(jnp.int32, (width, SUB), 1)
    terms = jnp.zeros((width, SUB), jnp.float32)
    for i in range(SUB):
        row = g * SUB + i
        acc = None
        for k in range(near_count):
            a = near_index_ref[k, row] & (SUB - 1)
            cost = cost_ref[i, k]
            high, low = split(cost)
            x = jnp.dot(
                jnp.concatenate([high, high, low], axis=1),
                plan_scr[a],
                preferred_element_type=jnp.float32,
            )
            x_high, x_low = split(x)
            x_ref[row, 0:width, k * wide : (k + 1) * wide] = x_high
            x_ref[row, width : 2 * width, k * wide : (k + 1) * wide] = x_low
            weighted = cost * cost * mass_ref[pl.ds(g * SUB + a, 1), :].astype(jnp.float32)
            acc = weighted if acc is None else acc + weighted
        terms = jnp.where(lanes == i, jnp.sum(acc, axis=1, keepdims=True), terms)
    term_ref[g] = terms


def relay_kernel(*refs):
    pass


def far_kernel(counts, row_axis, col_axis, *refs):
    row_devices, col_devices, target_here, source_count, target_count, group_blocks, link_count = counts
    near_index_ref, slot_ref, link_ref, x_ref, term_ref, mass_ref = refs[:6]
    cost_parts = refs[6 : 6 + row_devices]
    pack_ref, out_ref, work_ref, tall_ref, part_ref, log_source_ref, log_target_ref = refs[
        6 + row_devices : 13 + row_devices
    ]
    far_high, far_low, table, column_scr, scale_scr, peak_scr, sum_scr = refs[13 + row_devices :]
    g = pl.program_id(0)
    near_count = near_index_ref.shape[0]
    slots = slot_ref.shape[0]
    rows = out_ref.shape[0]
    width = out_ref.shape[3]
    zero_block = group_blocks * link_count

    @pl.when(g == 0)
    def _():
        me = lax.axis_index(row_axis)
        col = lax.axis_index(col_axis)
        far_high[zero_block] = jnp.zeros((width, width), jnp.bfloat16)
        far_low[zero_block] = jnp.zeros((width, width), jnp.bfloat16)

        def clear(e, _):
            table[e] = zero_block
            return 0

        lax.fori_loop(0, group_blocks * group_blocks, clear, 0)

        def mark(j, _):
            for m in range(link_count):
                table[j * group_blocks + link_ref[m, 0, j]] = j * link_count + m
            return 0

        lax.fori_loop(0, group_blocks, mark, 0)
        pack_rows = pack_ref.shape[0] // (row_devices * col_devices)
        total_source = functools.reduce(
            jnp.add,
            [pack_ref[r * col_devices * pack_rows : r * col_devices * pack_rows + 1, :] for r in range(row_devices)],
        )
        targets = functools.reduce(
            jnp.add,
            [
                pack_ref[d * pack_rows + 1 + h : d * pack_rows + 2 + h, :]
                for d in range(row_devices * col_devices)
                for h in range(target_here)
            ],
        )
        total_target = jnp.sum(targets, axis=1, keepdims=True)
        log_source_ref[...] = jnp.log2(source_count * mass_ref[...].astype(jnp.float32) / total_source)
        scale_scr[...] = source_count / (total_source * (near_count * width))
        column_scr[...] = jnp.zeros_like(column_scr)
        for s in range(row_devices):
            for h in range(target_here):
                j = (me ^ s) * target_here + h
                place = ((me ^ s) * col_devices + col) * pack_rows + 1 + h
                mass = target_count * pack_ref[pl.ds(place, 1), :] / total_target
                log_target_ref[pl.ds(j, 1), :] = jnp.log2(mass)
                tall = jnp.broadcast_to(mass, (width, width)).T
                for m in range(link_count):
                    block = cost_parts[s][0, h, m]
                    high, low = split(block)
                    far_high[j * link_count + m] = high
                    far_low[j * link_count + m] = low
                    spread = jnp.sum(tall * (block * block), axis=0, keepdims=True)
                    t = link_ref[m, 0, j]
                    column_scr[pl.ds(t, 1), :] += spread * (1.0 / (link_count * width))

    group_devices = target_count // (group_blocks * width)
    coef = 2.0 * (1.0 / (near_count * width)) * (1.0 / (slots * group_devices * width))
    scale = scale_scr[0:1, 0:1]
    for i in range(rows):
        row = g * rows + i
        group = row - lax.rem(row, SUB)
        targets = [slot_ref[l, row] for l in range(slots)]
        far_rows = []
        for k in range(near_count):
            a = group + (near_index_ref[k, row] & (SUB - 1))
            for q in range(slots):
                j = slot_ref[q, a]
                far_rows.append([table[j * group_blocks + t] for t in targets])
        right_high = jnp.concatenate(
            [jnp.concatenate([far_high[e] for e in r], axis=1) for r in far_rows], axis=0
        )
        right_low = jnp.concatenate(
            [jnp.concatenate([far_low[e] for e in r], axis=1) for r in far_rows], axis=0
        )
        both = jnp.dot(x_ref[row], right_high, preferred_element_type=jnp.float32)
        rest = jnp.dot(x_ref[row, 0:width, :], right_low, preferred_element_type=jnp.float32)
        product = both[0:width] + (both[width:] + rest)
        tall = term_ref[row // SUB, :, i % SUB : i % SUB + 1] * scale
        scores = []
        for l in range(slots):
            cost = tall + column_scr[pl.ds(targets[l], 1), :] - coef * product[:, l * width : (l + 1) * width]
            out_ref[i, 0, l] = cost
            scaled = cost * -to_log2
            work_ref[row, l] = scaled
            turned = scaled.T
            tall_ref[row, l] = turned
            scores.append(turned)
        row_pass(scores, row, peak_scr, sum_scr)

    @pl.when(g == pl.num_programs(0) - 1)
    def _():
        part_ref[...] = peak_scr[...] + jnp.log2(sum_scr[...])


def row_pass(scores, row, peak_scr, sum_scr):
    peak = jnp.max(functools.reduce(jnp.maximum, scores), axis=0, keepdims=True)
    total = functools.reduce(jnp.add, [jnp.exp2(s - peak) for s in scores])
    peak_scr[pl.ds(row, 1), :] = peak
    sum_scr[pl.ds(row, 1), :] = jnp.sum(total, axis=0, keepdims=True)


def column_kernel(col_devices, copies, work_ref, select_ref, log_mass_ref, *refs):
    parts = refs[:col_devices]
    out_ref, potential_ref, potential_scr, peak_scr, sum_scr = refs[col_devices:]
    rows, slots, width, _ = work_ref.shape
    together = math.gcd(rows, 8)
    scaled = log_mass_ref[...] - log_sum([p[...] for p in parts])
    potential_scr[...] = scaled
    potential_ref[...] = scaled * from_log2

    def some_rows(g, _):
        first = pl.multiple_of(g * together, together)
        tall = potential_scr[pl.ds(first, together), :].T
        for i in range(together):
            for l in range(slots):
                score = tall[:, i : i + 1] + work_ref[first + i, l]
                peak = jnp.max(score, axis=0, keepdims=True)
                total = jnp.sum(jnp.exp2(score - peak), axis=0, keepdims=True)
                place = (first + i) * slots + l
                peak_scr[pl.ds(place, 1), :] = peak
                sum_scr[pl.ds(place, 1), :] = total
        return 0

    lax.fori_loop(0, rows // together, some_rows, 0)
    select = select_ref[...]
    peaks = peak_scr[...]
    sums = sum_scr[...]
    blocks = out_ref.shape[0] // copies
    for t in range(blocks):
        chosen = select == t
        peak = jnp.max(jnp.where(chosen, peaks, very_low), axis=0, keepdims=True)
        shifted = jnp.where(chosen, sums * jnp.exp2(jnp.minimum(peaks - peak, 0.0)), 0.0)
        total = jnp.sum(shifted, axis=0, keepdims=True)
        some = total > 0.0
        out_ref[t : t + 1, :] = jnp.where(
            some, peak + jnp.log2(jnp.where(some, total, 1.0)), very_low
        )
    if copies > 1:
        put_copies(out_ref, copies, out_ref[0:blocks, :])


def row_kernel(
    row_devices, slot_ref, tall_ref, log_mass_ref, parts_ref, out_ref, wide_scr, peak_scr, sum_scr
):
    rows, slots, width, _ = tall_ref.shape
    together = math.gcd(rows, 8)
    potential = (log_mass_ref[...] - log_sum(parts_of(parts_ref, row_devices))).T
    for t in range(wide_scr.shape[0]):
        wide_scr[t] = jnp.broadcast_to(potential[:, t : t + 1], (width, width))

    def some_rows(g, _):
        for i in range(together):
            row = g * together + i
            scores = [wide_scr[slot_ref[l, row]] + tall_ref[row, l] for l in range(slots)]
            row_pass(scores, row, peak_scr, sum_scr)
        return 0

    lax.fori_loop(0, rows // together, some_rows, 0)
    out_ref[...] = peak_scr[...] + jnp.log2(sum_scr[...])


def last_kernel(row_devices, row_axis, log_mass_ref, parts_ref, out_ref):
    here = out_ref.shape[0]
    start = lax.axis_index(row_axis) * here
    log_mass = log_mass_ref[pl.ds(start, here), :]
    out_ref[...] = (log_mass - log_sum(parts_of(parts_ref, row_devices))) * from_log2


def per_device(
    coupling,
    coupling_index,
    near_cost,
    near_index,
    source_weights,
    target_cost,
    target_index,
    target_weights,
):
    rows_here = coupling.shape[0]
    slots = coupling.shape[2]
    width = coupling.shape[3]
    near_count = near_cost.shape[1]
    group_blocks = target_index.shape[1]
    link_count = target_index.shape[2]
    target_here = target_cost.shape[1]
    row_devices = lax.axis_size("rows")
    col_devices = lax.axis_size("cols")
    source_count = rows_here * row_devices * width
    target_count = group_blocks * width * col_devices
    f32 = jnp.float32
    arrived = {0: target_cost}
    late = [mask for mask in range(5, row_devices, 2)]
    for mask in range(1, row_devices):
        if mask not in late:
            arrived[mask] = send(target_cost, "rows", mask)

    near_t = near_index.T
    slot_t = coupling_index[:, 0, :].T
    link_t = jnp.transpose(target_index, (2, 0, 1))
    mass = source_weights.reshape(rows_here, width)
    select = jnp.broadcast_to(
        coupling_index.reshape(rows_here * slots, 1), (rows_here * slots, width)
    )

    pack_rows = 8 * pl.cdiv(1 + target_here, 8)
    devices = row_devices * col_devices
    pack = pl.pallas_call(
        functools.partial(pack_kernel, devices),
        out_shape=jax.ShapeDtypeStruct((devices * pack_rows, width), f32),
        name="pack",
    )(mass, target_weights.reshape(target_here, width))
    packs = exchange(pack, ("rows", "cols"))

    wide = near_count * slots * width
    groups = rows_here // SUB
    x_shape = pltpu.VMEM((rows_here, 2 * width, wide), jnp.bfloat16)
    term_shape = pltpu.VMEM((groups, width, SUB), f32)
    near_cost = pltpu.with_memory_space_constraint(near_cost, pltpu.HBM)
    coupling = pltpu.with_memory_space_constraint(coupling, pltpu.HBM)

    def near_product(first, count, *held):
        return pl.pallas_call(
            functools.partial(near_kernel, first),
            grid=(count,),
            in_specs=[
                SMEM,
                pl.BlockSpec((SUB, near_count, width, width), lambda g: (first + g, 0, 0, 0)),
                pl.BlockSpec((SUB, 1, slots, width, width), lambda g: (first + g, 0, 0, 0, 0)),
                whole((rows_here, width)),
            ]
            + [VMEM] * len(held),
            out_specs=[VMEM, VMEM],
            out_shape=[x_shape, term_shape],
            input_output_aliases={4: 0, 5: 1} if held else {},
            scratch_shapes=[pltpu.VMEM((SUB, 3 * width, slots * width), jnp.bfloat16)],
            compiler_params=pltpu.CompilerParams(vmem_limit_bytes=12 * mib),
            cost_estimate=pl.CostEstimate(
                flops=6 * count * SUB * wide * width * width,
                bytes_accessed=4 * count * SUB * width * (near_count + slots) * width,
                transcendentals=0,
            ),
            name="near_product",
        )(near_t, near_cost, coupling, mass, *map(in_vmem, held))

    held = near_product(0, (groups + 1) // 2)
    if late:
        sources = [mask - 1 for mask in late]
        passed = pl.pallas_call(
            relay_kernel,
            in_specs=[ANY] * (2 + len(sources)),
            out_specs=[ANY] * len(sources),
            out_shape=[jax.ShapeDtypeStruct(target_cost.shape, f32)] * len(sources),
            input_output_aliases={2 + e: e for e in range(len(sources))},
            name="relay",
        )(held[1], packs, *[arrived[mask] for mask in sources])
        for mask, block in zip(sources, passed):
            arrived[mask] = block
            arrived[mask + 1] = send(block, "rows", 1)
    cost_parts = [arrived[s] for s in range(row_devices)]
    x, term = near_product((groups + 1) // 2, groups // 2, *held)

    far_bytes = group_blocks * link_count * width * width * 4
    step_rows = SUB
    steps = rows_here // step_rows
    cost_block = pl.BlockSpec((step_rows, 1, slots, width, width), lambda g: (g, 0, 0, 0, 0))
    work_shape = pltpu.VMEM((rows_here, slots, width, width), f32)
    cost_blocks, work, tall, row_part, log_source, log_target = pl.pallas_call(
        functools.partial(
            far_kernel,
            (row_devices, col_devices, target_here, source_count, target_count, group_blocks, link_count),
            "rows",
            "cols",
        ),
        grid=(steps,),
        in_specs=[SMEM, SMEM, SMEM, VMEM, VMEM, whole((rows_here, width))]
        + [VMEM] * row_devices
        + [whole(packs.shape)],
        out_specs=[
            cost_block,
            VMEM,
            VMEM,
            whole((rows_here, width)),
            whole((rows_here, width)),
            whole((group_blocks, width)),
        ],
        out_shape=[
            jax.ShapeDtypeStruct(coupling.shape, f32),
            work_shape,
            work_shape,
            jax.ShapeDtypeStruct((rows_here, width), f32),
            jax.ShapeDtypeStruct((rows_here, width), f32),
            jax.ShapeDtypeStruct((group_blocks, width), f32),
        ],
        scratch_shapes=[
            pltpu.VMEM((group_blocks * link_count + 1, width, width), jnp.bfloat16),
            pltpu.VMEM((group_blocks * link_count + 1, width, width), jnp.bfloat16),
            pltpu.SMEM((group_blocks * group_blocks,), jnp.int32),
            pltpu.VMEM((group_blocks, width), f32),
            pltpu.VMEM((1, width), f32),
            pltpu.VMEM((rows_here, width), f32),
            pltpu.VMEM((rows_here, width), f32),
        ],
        compiler_params=pltpu.CompilerParams(vmem_limit_bytes=12 * mib + 2 * far_bytes),
        name="far_product",
    )(near_t, slot_t, link_t, in_vmem(x), in_vmem(term), mass, *cost_parts, packs)

    pass_params = pltpu.CompilerParams(vmem_limit_bytes=12 * mib)

    def column_step(row_parts, copies):
        return pl.pallas_call(
            functools.partial(column_kernel, col_devices, copies),
            in_specs=[VMEM] * (3 + col_devices),
            out_specs=[VMEM, VMEM],
            out_shape=[
                jax.ShapeDtypeStruct((copies * group_blocks, width), f32),
                jax.ShapeDtypeStruct((rows_here, width), f32),
            ],
            scratch_shapes=[
                pltpu.VMEM((rows_here, width), f32),
                pltpu.VMEM((rows_here * slots, width), f32),
                pltpu.VMEM((rows_here * slots, width), f32),
            ],
            compiler_params=pass_params,
            name="column_pass",
        )(in_vmem(work), select, log_source, *row_parts)

    def row_step(column_parts):
        return pl.pallas_call(
            functools.partial(row_kernel, row_devices),
            in_specs=[SMEM, VMEM, VMEM, VMEM],
            out_specs=VMEM,
            out_shape=jax.ShapeDtypeStruct((rows_here, width), f32),
            scratch_shapes=[
                pltpu.VMEM((group_blocks, width, width), f32),
                pltpu.VMEM((rows_here, width), f32),
                pltpu.VMEM((rows_here, width), f32),
            ],
            compiler_params=pass_params,
            name="row_pass",
        )(slot_t, in_vmem(tall), log_target, column_parts)

    for step in range(ITERS):
        last = step == ITERS - 1
        column_part, source_potential = column_step(
            from_all(row_part, "cols"), 1 if last else row_devices
        )
        column_parts = exchange(column_part, "rows")
        if not last:
            row_part = row_step(column_parts)
    own_target = pl.pallas_call(
        functools.partial(last_kernel, row_devices, "rows"),
        out_shape=jax.ShapeDtypeStruct((target_here, width), f32),
        name="last_potential",
    )(log_target, column_parts)
    return (
        cost_blocks,
        source_potential.reshape(rows_here * width),
        own_target.reshape(1, target_here * width),
    )


def solution(mesh):
    placed = (
        P("rows", "cols", None, None, None),
        P("rows", "cols", None),
        P("rows", None, None, None),
        P("rows", None),
        P("rows"),
        P("cols", "rows", None, None, None),
        P("cols", None, None),
        P("cols", "rows"),
    )
    return jax.shard_map(
        per_device,
        mesh=mesh,
        in_specs=placed,
        out_specs=(P("rows", "cols", None, None, None), P("rows"), P("cols", "rows")),
        check_vma=False,
    )
```

```python
import functools
import math

import jax
import jax.numpy as jnp
from jax import lax
from jax.experimental import pallas as pl
from jax.experimental.pallas import tpu as pltpu
from jax.sharding import PartitionSpec as P

ITERS = 3
SUB = 4

entropy = 0.01
to_log2 = math.log2(math.e) / entropy
from_log2 = entropy * math.log(2.0)
very_low = -1e30
mib = 1024 * 1024

SMEM = pl.BlockSpec(memory_space=pltpu.SMEM)
VMEM = pl.BlockSpec(memory_space=pltpu.VMEM)
ANY = pl.BlockSpec(memory_space=pl.ANY)


def in_hbm(x):
    return pltpu.with_memory_space_constraint(x, pltpu.HBM)


def whole(shape):
    return pl.BlockSpec(shape, lambda *_: (0,) * len(shape))


def split(x):
    high = x.astype(jnp.bfloat16)
    return high, (x - high.astype(jnp.float32)).astype(jnp.bfloat16)


def tree(parts, op):
    while len(parts) > 1:
        half = len(parts) // 2
        parts = [op(parts[s], parts[s + half]) for s in range(half)]
    return parts[0]


def log_sum(parts):
    peak = tree(parts, jnp.maximum)
    return peak + jnp.log2(tree([jnp.exp2(p - peak) for p in parts], jnp.add))


def parts_of(ref, devices):
    rows = ref.shape[0] // devices
    return [ref[d * rows : (d + 1) * rows, :] for d in range(devices)]


def put_copies(ref, devices, value):
    rows = value.shape[0]
    for d in range(devices):
        ref[d * rows : (d + 1) * rows, :] = value


def send(x, axis, mask):
    size = lax.axis_size(axis)
    return lax.ppermute(x, axis, [(d, d ^ mask) for d in range(size)])


def from_all(x, axis):
    return [x] + [send(x, axis, s) for s in range(1, lax.axis_size(axis))]


def exchange(copies, axis):
    return lax.all_to_all(copies, axis, 0, 0, tiled=True)


def pack_kernel(devices, after_ref, source_ref, target_ref, out_ref):
    rows = out_ref.shape[0] // devices
    total = jnp.sum(source_ref[...].astype(jnp.float32), axis=(0, 1), keepdims=True)
    target = target_ref[...].astype(jnp.float32)
    out_ref[...] = jnp.zeros_like(out_ref)
    for d in range(devices):
        out_ref[d * rows : d * rows + 1, :] = jnp.broadcast_to(total, (1, out_ref.shape[1]))
        out_ref[d * rows + 1 : d * rows + 1 + target.shape[0], :] = target


def near_kernel(first, near_index_ref, cost_ref, plan_ref, mass_ref, *refs):
    x_ref, term_ref, plan_scr = refs[-3:]
    g = first + pl.program_id(0)
    near_count = cost_ref.shape[1]
    width = cost_ref.shape[2]
    slots = plan_ref.shape[2]
    wide = slots * width
    for a in range(SUB):
        plan = jnp.concatenate([plan_ref[a, 0, q] for q in range(slots)], axis=1)
        high, low = split(plan)
        plan_scr[a, 0:width, :] = high
        plan_scr[a, width : 2 * width, :] = low
        plan_scr[a, 2 * width : 3 * width, :] = high
    lanes = lax.broadcasted_iota(jnp.int32, (width, SUB), 1)
    terms = jnp.zeros((width, SUB), jnp.float32)
    for i in range(SUB):
        row = g * SUB + i
        acc = None
        for k in range(near_count):
            a = near_index_ref[k, row] & (SUB - 1)
            cost = cost_ref[i, k]
            high, low = split(cost)
            x = jnp.dot(
                jnp.concatenate([high, high, low], axis=1),
                plan_scr[a],
                preferred_element_type=jnp.float32,
            )
            x_high, x_low = split(x)
            x_ref[i, 0:width, k * wide : (k + 1) * wide] = x_high
            x_ref[i, width : 2 * width, k * wide : (k + 1) * wide] = x_low
            weighted = cost * cost * mass_ref[pl.ds(g * SUB + a, 1), :].astype(jnp.float32)
            acc = weighted if acc is None else acc + weighted
        terms = jnp.where(lanes == i, jnp.sum(acc, axis=1, keepdims=True), terms)
    term_ref[0] = terms


def relay_kernel(*refs):
    pass


def far_kernel(counts, row_axis, col_axis, *refs):
    row_devices, col_devices, target_here, source_count, target_count, group_blocks, link_count = counts
    near_index_ref, slot_ref, link_ref, x_ref, term_ref, mass_ref = refs[:6]
    cost_parts = refs[6 : 6 + row_devices]
    pack_ref, out_ref, tall_ref, part_ref, log_source_ref, log_target_ref = refs[
        6 + row_devices : 12 + row_devices
    ]
    far_high, far_low, table, column_scr, scale_scr, peak_scr, sum_scr = refs[12 + row_devices :]
    g = pl.program_id(0)
    near_count = near_index_ref.shape[0]
    slots = slot_ref.shape[0]
    rows = out_ref.shape[0]
    width = out_ref.shape[3]
    zero_block = group_blocks * link_count

    @pl.when(g == 0)
    def _():
        me = lax.axis_index(row_axis)
        col = lax.axis_index(col_axis)
        far_high[zero_block] = jnp.zeros((width, width), jnp.bfloat16)
        far_low[zero_block] = jnp.zeros((width, width), jnp.bfloat16)

        def clear(e, _):
            table[e] = zero_block
            return 0

        lax.fori_loop(0, group_blocks * group_blocks, clear, 0)

        def mark(j, _):
            for m in range(link_count):
                table[j * group_blocks + link_ref[m, 0, j]] = j * link_count + m
            return 0

        lax.fori_loop(0, group_blocks, mark, 0)
        pack_rows = pack_ref.shape[0] // (row_devices * col_devices)
        total_source = functools.reduce(
            jnp.add,
            [pack_ref[r * col_devices * pack_rows : r * col_devices * pack_rows + 1, :] for r in range(row_devices)],
        )
        targets = functools.reduce(
            jnp.add,
            [
                pack_ref[d * pack_rows + 1 + h : d * pack_rows + 2 + h, :]
                for d in range(row_devices * col_devices)
                for h in range(target_here)
            ],
        )
        total_target = jnp.sum(targets, axis=1, keepdims=True)
        log_source_ref[...] = jnp.log2(source_count * mass_ref[...].astype(jnp.float32) / total_source)
        scale_scr[...] = source_count / (total_source * (near_count * width))
        column_scr[...] = jnp.zeros_like(column_scr)
        for s in range(row_devices):
            for h in range(target_here):
                j = (me ^ s) * target_here + h
                place = ((me ^ s) * col_devices + col) * pack_rows + 1 + h
                mass = target_count * pack_ref[pl.ds(place, 1), :] / total_target
                log_target_ref[pl.ds(j, 1), :] = jnp.log2(mass)
                tall = jnp.broadcast_to(mass, (width, width)).T
                for m in range(link_count):
                    block = cost_parts[s][0, h, m]
                    high, low = split(block)
                    far_high[j * link_count + m] = high
                    far_low[j * link_count + m] = low
                    spread = jnp.sum(tall * (block * block), axis=0, keepdims=True)
                    t = link_ref[m, 0, j]
                    column_scr[pl.ds(t, 1), :] += spread * (1.0 / (link_count * width))

    group_devices = target_count // (group_blocks * width)
    coef = 2.0 * (1.0 / (near_count * width)) * (1.0 / (slots * group_devices * width))
    scale = scale_scr[0:1, 0:1]
    for i in range(rows):
        row = g * rows + i
        group = row - lax.rem(row, SUB)
        targets = [slot_ref[l, row] for l in range(slots)]
        far_rows = []
        for k in range(near_count):
            a = group + (near_index_ref[k, row] & (SUB - 1))
            for q in range(slots):
                j = slot_ref[q, a]
                far_rows.append([table[j * group_blocks + t] for t in targets])
        right_high = jnp.concatenate(
            [jnp.concatenate([far_high[e] for e in r], axis=1) for r in far_rows], axis=0
        )
        right_low = jnp.concatenate(
            [jnp.concatenate([far_low[e] for e in r], axis=1) for r in far_rows], axis=0
        )
        both = jnp.dot(x_ref[i], right_high, preferred_element_type=jnp.float32)
        rest = jnp.dot(x_ref[i, 0:width, :], right_low, preferred_element_type=jnp.float32)
        product = both[0:width] + (both[width:] + rest)
        tall = term_ref[i // SUB, :, i % SUB : i % SUB + 1] * scale
        scores = []
        for l in range(slots):
            cost = tall + column_scr[pl.ds(targets[l], 1), :] - coef * product[:, l * width : (l + 1) * width]
            out_ref[i, 0, l] = cost
            turned = (cost * -to_log2).T
            tall_ref[i, l] = turned
            scores.append(turned)
        row_pass(scores, row, peak_scr, sum_scr)

    @pl.when(g == pl.num_programs(0) - 1)
    def _():
        part_ref[...] = peak_scr[...] + jnp.log2(sum_scr[...])


def row_pass(scores, row, peak_scr, sum_scr):
    peak = jnp.max(functools.reduce(jnp.maximum, scores), axis=0, keepdims=True)
    total = functools.reduce(jnp.add, [jnp.exp2(s - peak) for s in scores])
    peak_scr[pl.ds(row, 1), :] = peak
    sum_scr[pl.ds(row, 1), :] = jnp.sum(total, axis=0, keepdims=True)


def column_kernel(col_devices, copies, cost_ref, select_ref, log_mass_ref, *refs):
    parts = refs[:col_devices]
    out_ref, potential_ref, potential_scr, peak_scr, sum_scr = refs[col_devices:]
    rows, _, slots, _, _ = cost_ref.shape
    g = pl.program_id(0)

    @pl.when(g == 0)
    def _():
        scaled = log_mass_ref[...] - log_sum([p[...] for p in parts])
        potential_scr[...] = scaled
        potential_ref[...] = scaled * from_log2

    first = pl.multiple_of(g * rows, rows)
    tall = potential_scr[pl.ds(first, rows), :].T
    for i in range(rows):
        for l in range(slots):
            score = tall[:, i : i + 1] - cost_ref[i, 0, l] * to_log2
            peak = jnp.max(score, axis=0, keepdims=True)
            total = jnp.sum(jnp.exp2(score - peak), axis=0, keepdims=True)
            place = (first + i) * slots + l
            peak_scr[pl.ds(place, 1), :] = peak
            sum_scr[pl.ds(place, 1), :] = total

    @pl.when(g == pl.num_programs(0) - 1)
    def _():
        select = select_ref[...]
        peaks = peak_scr[...]
        sums = sum_scr[...]
        blocks = out_ref.shape[0] // copies
        for t in range(blocks):
            chosen = select == t
            peak = jnp.max(jnp.where(chosen, peaks, very_low), axis=0, keepdims=True)
            shifted = jnp.where(chosen, sums * jnp.exp2(jnp.minimum(peaks - peak, 0.0)), 0.0)
            total = jnp.sum(shifted, axis=0, keepdims=True)
            some = total > 0.0
            out_ref[t : t + 1, :] = jnp.where(
                some, peak + jnp.log2(jnp.where(some, total, 1.0)), very_low
            )
        if copies > 1:
            put_copies(out_ref, copies, out_ref[0:blocks, :])


def row_kernel(
    row_devices, slot_ref, tall_ref, log_mass_ref, parts_ref, out_ref, wide_scr, peak_scr, sum_scr
):
    rows, slots, width, _ = tall_ref.shape
    g = pl.program_id(0)

    @pl.when(g == 0)
    def _():
        potential = (log_mass_ref[...] - log_sum(parts_of(parts_ref, row_devices))).T
        for t in range(wide_scr.shape[0]):
            wide_scr[t] = jnp.broadcast_to(potential[:, t : t + 1], (width, width))

    for i in range(rows):
        row = g * rows + i
        scores = [wide_scr[slot_ref[l, row]] + tall_ref[i, l] for l in range(slots)]
        row_pass(scores, row, peak_scr, sum_scr)

    @pl.when(g == pl.num_programs(0) - 1)
    def _():
        out_ref[...] = peak_scr[...] + jnp.log2(sum_scr[...])


def last_kernel(row_devices, row_axis, log_mass_ref, parts_ref, out_ref):
    here = out_ref.shape[0]
    start = lax.axis_index(row_axis) * here
    log_mass = log_mass_ref[pl.ds(start, here), :]
    out_ref[...] = (log_mass - log_sum(parts_of(parts_ref, row_devices))) * from_log2


def per_device(
    coupling,
    coupling_index,
    near_cost,
    near_index,
    source_weights,
    target_cost,
    target_index,
    target_weights,
):
    rows_here = coupling.shape[0]
    slots = coupling.shape[2]
    width = coupling.shape[3]
    near_count = near_cost.shape[1]
    group_blocks = target_index.shape[1]
    link_count = target_index.shape[2]
    target_here = target_cost.shape[1]
    row_devices = lax.axis_size("rows")
    col_devices = lax.axis_size("cols")
    source_count = rows_here * row_devices * width
    target_count = group_blocks * width * col_devices
    f32 = jnp.float32
    arrived = {0: target_cost}
    late = [mask for mask in range(5, row_devices, 2)]
    for mask in range(1, row_devices):
        if mask not in late:
            arrived[mask] = send(target_cost, "rows", mask)

    near_t = in_hbm(near_index.T)
    slot_t = in_hbm(coupling_index[:, 0, :].T)
    link_t = in_hbm(jnp.transpose(target_index, (2, 0, 1)))
    mass = in_hbm(source_weights.reshape(rows_here, width))
    near_cost = in_hbm(near_cost)
    coupling = in_hbm(coupling)
    select = jnp.broadcast_to(
        coupling_index.reshape(rows_here * slots, 1), (rows_here * slots, width)
    )

    wide = near_count * slots * width
    groups = rows_here // SUB
    x_shape = pltpu.HBM((rows_here, 2 * width, wide), jnp.bfloat16)
    term_shape = pltpu.HBM((groups, width, SUB), f32)

    def near_product(first, count, *held):
        return pl.pallas_call(
            functools.partial(near_kernel, first),
            grid=(count,),
            in_specs=[
                SMEM,
                pl.BlockSpec((SUB, near_count, width, width), lambda g: (first + g, 0, 0, 0)),
                pl.BlockSpec((SUB, 1, slots, width, width), lambda g: (first + g, 0, 0, 0, 0)),
                whole((rows_here, width)),
            ]
            + [ANY] * len(held),
            out_specs=[
                pl.BlockSpec((SUB, 2 * width, wide), lambda g: (first + g, 0, 0)),
                pl.BlockSpec((1, width, SUB), lambda g: (first + g, 0, 0)),
            ],
            out_shape=[x_shape, term_shape],
            input_output_aliases={4: 0, 5: 1} if held else {},
            scratch_shapes=[pltpu.VMEM((SUB, 3 * width, slots * width), jnp.bfloat16)],
            compiler_params=pltpu.CompilerParams(vmem_limit_bytes=32 * mib),
            cost_estimate=pl.CostEstimate(
                flops=6 * count * SUB * wide * width * width,
                bytes_accessed=4 * count * SUB * width * (near_count + slots) * width,
                transcendentals=0,
            ),
            name="near_product",
        )(near_t, near_cost, coupling, mass, *map(in_hbm, held))

    held = near_product(0, (groups + 1) // 2)

    pack_rows = 8 * pl.cdiv(1 + target_here, 8)
    devices = row_devices * col_devices
    pack = pl.pallas_call(
        functools.partial(pack_kernel, devices),
        in_specs=[ANY, VMEM, VMEM],
        out_shape=jax.ShapeDtypeStruct((devices * pack_rows, width), f32),
        name="pack",
    )(in_hbm(held[1]), mass, in_hbm(target_weights.reshape(target_here, width)))
    packs = exchange(pack, ("rows", "cols"))

    if late:
        sources = [mask - 1 for mask in late]
        passed = pl.pallas_call(
            relay_kernel,
            in_specs=[ANY] * (1 + len(sources)),
            out_specs=[ANY] * len(sources),
            out_shape=[jax.ShapeDtypeStruct(target_cost.shape, f32)] * len(sources),
            input_output_aliases={1 + e: e for e in range(len(sources))},
            name="relay",
        )(packs, *[arrived[mask] for mask in sources])
        for mask, block in zip(sources, passed):
            arrived[mask] = block
            arrived[mask + 1] = send(block, "rows", 1)
    cost_parts = [arrived[s] for s in range(row_devices)]
    x, term = near_product((groups + 1) // 2, groups // 2, *held)

    far_bytes = group_blocks * link_count * width * width * 4
    step_rows = SUB
    steps = rows_here // step_rows
    cost_block = pl.BlockSpec((step_rows, 1, slots, width, width), lambda g: (g, 0, 0, 0, 0))
    tall_block = pl.BlockSpec((step_rows, slots, width, width), lambda g: (g, 0, 0, 0))
    cost_blocks, tall, row_part, log_source, log_target = pl.pallas_call(
        functools.partial(
            far_kernel,
            (row_devices, col_devices, target_here, source_count, target_count, group_blocks, link_count),
            "rows",
            "cols",
        ),
        grid=(steps,),
        in_specs=[
            SMEM,
            SMEM,
            SMEM,
            pl.BlockSpec((step_rows, 2 * width, wide), lambda g: (g, 0, 0)),
            pl.BlockSpec((step_rows // SUB, width, SUB), lambda g: (g, 0, 0)),
            whole((rows_here, width)),
        ]
        + [VMEM] * row_devices
        + [whole(packs.shape)],
        out_specs=[
            cost_block,
            tall_block,
            whole((rows_here, width)),
            whole((rows_here, width)),
            whole((group_blocks, width)),
        ],
        out_shape=[
            pltpu.HBM(coupling.shape, f32),
            pltpu.HBM((rows_here, slots, width, width), f32),
            jax.ShapeDtypeStruct((rows_here, width), f32),
            jax.ShapeDtypeStruct((rows_here, width), f32),
            jax.ShapeDtypeStruct((group_blocks, width), f32),
        ],
        scratch_shapes=[
            pltpu.VMEM((group_blocks * link_count + 1, width, width), jnp.bfloat16),
            pltpu.VMEM((group_blocks * link_count + 1, width, width), jnp.bfloat16),
            pltpu.SMEM((group_blocks * group_blocks,), jnp.int32),
            pltpu.VMEM((group_blocks, width), f32),
            pltpu.VMEM((1, width), f32),
            pltpu.VMEM((rows_here, width), f32),
            pltpu.VMEM((rows_here, width), f32),
        ],
        compiler_params=pltpu.CompilerParams(vmem_limit_bytes=20 * mib + 2 * far_bytes),
        name="far_product",
    )(near_t, slot_t, link_t, in_hbm(x), in_hbm(term), mass, *cost_parts, packs)

    pass_params = pltpu.CompilerParams(vmem_limit_bytes=32 * mib)
    pass_rows = math.gcd(rows_here, 8)
    passes = rows_here // pass_rows

    def column_step(row_parts, copies):
        return pl.pallas_call(
            functools.partial(column_kernel, col_devices, copies),
            grid=(passes,),
            in_specs=[
                pl.BlockSpec((pass_rows, 1, slots, width, width), lambda g: (g, 0, 0, 0, 0)),
                whole((rows_here * slots, width)),
            ]
            + [whole((rows_here, width))] * (1 + col_devices),
            out_specs=[whole((copies * group_blocks, width)), whole((rows_here, width))],
            out_shape=[
                jax.ShapeDtypeStruct((copies * group_blocks, width), f32),
                jax.ShapeDtypeStruct((rows_here, width), f32),
            ],
            scratch_shapes=[
                pltpu.VMEM((rows_here, width), f32),
                pltpu.VMEM((rows_here * slots, width), f32),
                pltpu.VMEM((rows_here * slots, width), f32),
            ],
            compiler_params=pass_params,
            name="column_pass",
        )(in_hbm(cost_blocks), select, log_source, *row_parts)

    def row_step(column_parts):
        return pl.pallas_call(
            functools.partial(row_kernel, row_devices),
            grid=(passes,),
            in_specs=[
                SMEM,
                pl.BlockSpec((pass_rows, slots, width, width), lambda g: (g, 0, 0, 0)),
                whole((group_blocks, width)),
                whole(column_parts.shape),
            ],
            out_specs=whole((rows_here, width)),
            out_shape=jax.ShapeDtypeStruct((rows_here, width), f32),
            scratch_shapes=[
                pltpu.VMEM((group_blocks, width, width), f32),
                pltpu.VMEM((rows_here, width), f32),
                pltpu.VMEM((rows_here, width), f32),
            ],
            compiler_params=pass_params,
            name="row_pass",
        )(slot_t, in_hbm(tall), log_target, column_parts)

    for step in range(ITERS):
        last = step == ITERS - 1
        column_part, source_potential = column_step(
            from_all(row_part, "cols"), 1 if last else row_devices
        )
        column_parts = exchange(column_part, "rows")
        if not last:
            row_part = row_step(column_parts)
    own_target = pl.pallas_call(
        functools.partial(last_kernel, row_devices, "rows"),
        out_shape=jax.ShapeDtypeStruct((target_here, width), f32),
        name="last_potential",
    )(log_target, column_parts)
    return (
        cost_blocks,
        source_potential.reshape(rows_here * width),
        own_target.reshape(1, target_here * width),
    )


def solution(mesh):
    placed = (
        P("rows", "cols", None, None, None),
        P("rows", "cols", None),
        P("rows", None, None, None),
        P("rows", None),
        P("rows"),
        P("cols", "rows", None, None, None),
        P("cols", None, None),
        P("cols", "rows"),
    )
    return jax.shard_map(
        per_device,
        mesh=mesh,
        in_specs=placed,
        out_specs=(P("rows", "cols", None, None, None), P("rows"), P("cols", "rows")),
        check_vma=False,
    )
```

```python
import functools
import math

import jax
import jax.numpy as jnp
from jax import lax
from jax.experimental import pallas as pl
from jax.experimental.pallas import tpu as pltpu
from jax.sharding import PartitionSpec as P

ITERS = 3
SUB = 4

entropy = 0.01
to_log2 = math.log2(math.e) / entropy
from_log2 = entropy * math.log(2.0)
very_low = -1e30
mib = 1024 * 1024

SMEM = pl.BlockSpec(memory_space=pltpu.SMEM)
VMEM = pl.BlockSpec(memory_space=pltpu.VMEM)
ANY = pl.BlockSpec(memory_space=pl.ANY)


def in_hbm(x):
    return pltpu.with_memory_space_constraint(x, pltpu.HBM)


def in_vmem(x):
    return pltpu.with_memory_space_constraint(x, pltpu.VMEM)


def whole(shape):
    return pl.BlockSpec(shape, lambda *_: (0,) * len(shape))


def split(x):
    high = x.astype(jnp.bfloat16)
    return high, (x - high.astype(jnp.float32)).astype(jnp.bfloat16)


def tree(parts, op):
    while len(parts) > 1:
        half = len(parts) // 2
        parts = [op(parts[s], parts[s + half]) for s in range(half)]
    return parts[0]


def log_sum(parts):
    peak = tree(parts, jnp.maximum)
    return peak + jnp.log2(tree([jnp.exp2(p - peak) for p in parts], jnp.add))


def parts_of(ref, devices):
    rows = ref.shape[0] // devices
    return [ref[d * rows : (d + 1) * rows, :] for d in range(devices)]


def put_copies(ref, devices, value):
    rows = value.shape[0]
    for d in range(devices):
        ref[d * rows : (d + 1) * rows, :] = value


def send(x, axis, mask):
    size = lax.axis_size(axis)
    return lax.ppermute(x, axis, [(d, d ^ mask) for d in range(size)])


def from_all(x, axis):
    return [x] + [send(x, axis, s) for s in range(1, lax.axis_size(axis))]


def exchange(copies, axis):
    return lax.all_to_all(copies, axis, 0, 0, tiled=True)


def pack_kernel(devices, after_ref, source_ref, target_ref, out_ref):
    rows = out_ref.shape[0] // devices
    total = jnp.sum(source_ref[...].astype(jnp.float32), axis=(0, 1), keepdims=True)
    target = target_ref[...].astype(jnp.float32)
    out_ref[...] = jnp.zeros_like(out_ref)
    for d in range(devices):
        out_ref[d * rows : d * rows + 1, :] = jnp.broadcast_to(total, (1, out_ref.shape[1]))
        out_ref[d * rows + 1 : d * rows + 1 + target.shape[0], :] = target


def near_kernel(near_index_ref, cost_ref, plan_ref, mass_ref, x_ref, term_ref, plan_scr):
    g = pl.program_id(0)
    near_count = cost_ref.shape[1]
    width = cost_ref.shape[2]
    slots = plan_ref.shape[2]
    wide = slots * width
    for a in range(SUB):
        plan = jnp.concatenate([plan_ref[a, 0, q] for q in range(slots)], axis=1)
        high, low = split(plan)
        plan_scr[a, 0:width, :] = high
        plan_scr[a, width : 2 * width, :] = low
        plan_scr[a, 2 * width : 3 * width, :] = high
    lanes = lax.broadcasted_iota(jnp.int32, (width, SUB), 1)
    terms = jnp.zeros((width, SUB), jnp.float32)
    for i in range(SUB):
        row = g * SUB + i
        acc = None
        for k in range(near_count):
            a = near_index_ref[k, row] & (SUB - 1)
            cost = cost_ref[i, k]
            high, low = split(cost)
            x = jnp.dot(
                jnp.concatenate([high, high, low], axis=1),
                plan_scr[a],
                preferred_element_type=jnp.float32,
            )
            x_high, x_low = split(x)
            x_ref[row, 0:width, k * wide : (k + 1) * wide] = x_high
            x_ref[row, width : 2 * width, k * wide : (k + 1) * wide] = x_low
            weighted = cost * cost * mass_ref[pl.ds(g * SUB + a, 1), :].astype(jnp.float32)
            acc = weighted if acc is None else acc + weighted
        terms = jnp.where(lanes == i, jnp.sum(acc, axis=1, keepdims=True), terms)
    term_ref[g] = terms


def relay_kernel(*refs):
    pass


def far_kernel(counts, row_axis, col_axis, *refs):
    row_devices, col_devices, target_here, source_count, target_count, group_blocks, link_count = counts
    near_index_ref, slot_ref, link_ref, x_ref, term_ref, mass_ref = refs[:6]
    cost_parts = refs[6 : 6 + row_devices]
    pack_ref, out_ref, work_ref, tall_ref, part_ref, log_source_ref, log_target_ref, select_ref = refs[
        6 + row_devices : 14 + row_devices
    ]
    far_high, far_low, table, column_scr, scale_scr, peak_scr, sum_scr = refs[14 + row_devices :]
    g = pl.program_id(0)
    near_count = near_index_ref.shape[0]
    slots = slot_ref.shape[0]
    rows = out_ref.shape[0]
    width = out_ref.shape[3]
    zero_block = group_blocks * link_count

    @pl.when(g == 0)
    def _():
        me = lax.axis_index(row_axis)
        col = lax.axis_index(col_axis)
        far_high[zero_block] = jnp.zeros((width, width), jnp.bfloat16)
        far_low[zero_block] = jnp.zeros((width, width), jnp.bfloat16)

        def clear(e, _):
            table[e] = zero_block
            return 0

        lax.fori_loop(0, group_blocks * group_blocks, clear, 0)

        def mark(j, _):
            for m in range(link_count):
                table[j * group_blocks + link_ref[m, 0, j]] = j * link_count + m
            return 0

        lax.fori_loop(0, group_blocks, mark, 0)
        pack_rows = pack_ref.shape[0] // (row_devices * col_devices)
        total_source = functools.reduce(
            jnp.add,
            [pack_ref[r * col_devices * pack_rows : r * col_devices * pack_rows + 1, :] for r in range(row_devices)],
        )
        targets = functools.reduce(
            jnp.add,
            [
                pack_ref[d * pack_rows + 1 + h : d * pack_rows + 2 + h, :]
                for d in range(row_devices * col_devices)
                for h in range(target_here)
            ],
        )
        total_target = jnp.sum(targets, axis=1, keepdims=True)
        log_source_ref[...] = jnp.log2(source_count * mass_ref[...].astype(jnp.float32) / total_source)
        scale_scr[...] = source_count / (total_source * (near_count * width))
        column_scr[...] = jnp.zeros_like(column_scr)
        for s in range(row_devices):
            for h in range(target_here):
                j = (me ^ s) * target_here + h
                place = ((me ^ s) * col_devices + col) * pack_rows + 1 + h
                mass = target_count * pack_ref[pl.ds(place, 1), :] / total_target
                log_target_ref[pl.ds(j, 1), :] = jnp.log2(mass)
                tall = jnp.broadcast_to(mass, (width, width)).T
                for m in range(link_count):
                    block = cost_parts[s][0, h, m]
                    high, low = split(block)
                    far_high[j * link_count + m] = high
                    far_low[j * link_count + m] = low
                    spread = jnp.sum(tall * (block * block), axis=0, keepdims=True)
                    t = link_ref[m, 0, j]
                    column_scr[pl.ds(t, 1), :] += spread * (1.0 / (link_count * width))

    group_devices = target_count // (group_blocks * width)
    coef = 2.0 * (1.0 / (near_count * width)) * (1.0 / (slots * group_devices * width))
    scale = scale_scr[0:1, 0:1]
    for i in range(rows):
        row = g * rows + i
        group = row - lax.rem(row, SUB)
        targets = [slot_ref[l, row] for l in range(slots)]
        far_rows = []
        for k in range(near_count):
            a = group + (near_index_ref[k, row] & (SUB - 1))
            for q in range(slots):
                j = slot_ref[q, a]
                far_rows.append([table[j * group_blocks + t] for t in targets])
        right_high = jnp.concatenate(
            [jnp.concatenate([far_high[e] for e in r], axis=1) for r in far_rows], axis=0
        )
        right_low = jnp.concatenate(
            [jnp.concatenate([far_low[e] for e in r], axis=1) for r in far_rows], axis=0
        )
        both = jnp.dot(x_ref[row], right_high, preferred_element_type=jnp.float32)
        rest = jnp.dot(x_ref[row, 0:width, :], right_low, preferred_element_type=jnp.float32)
        product = both[0:width] + (both[width:] + rest)
        tall = term_ref[row // SUB, :, i % SUB : i % SUB + 1] * scale
        scores = []
        for l in range(slots):
            cost = tall + column_scr[pl.ds(targets[l], 1), :] - coef * product[:, l * width : (l + 1) * width]
            out_ref[i, 0, l] = cost
            select_ref[pl.ds(row * slots + l, 1), :] = jnp.full((1, width), targets[l], jnp.int32)
            scaled = cost * -to_log2
            work_ref[row, l] = scaled
            turned = scaled.T
            tall_ref[row, l] = turned
            scores.append(turned)
        row_pass(scores, row, peak_scr, sum_scr)

    @pl.when(g == pl.num_programs(0) - 1)
    def _():
        part_ref[...] = peak_scr[...] + jnp.log2(sum_scr[...])


def row_pass(scores, row, peak_scr, sum_scr):
    peak = jnp.max(functools.reduce(jnp.maximum, scores), axis=0, keepdims=True)
    total = functools.reduce(jnp.add, [jnp.exp2(s - peak) for s in scores])
    peak_scr[pl.ds(row, 1), :] = peak
    sum_scr[pl.ds(row, 1), :] = jnp.sum(total, axis=0, keepdims=True)


def column_kernel(col_devices, copies, work_ref, select_ref, log_mass_ref, *refs):
    parts = refs[:col_devices]
    out_ref, potential_ref, potential_scr, peak_scr, sum_scr = refs[col_devices:]
    rows, slots, width, _ = work_ref.shape
    together = math.gcd(rows, 8)
    scaled = log_mass_ref[...] - log_sum([p[...] for p in parts])
    potential_scr[...] = scaled
    potential_ref[...] = scaled * from_log2

    def some_rows(g, _):
        first = pl.multiple_of(g * together, together)
        tall = potential_scr[pl.ds(first, together), :].T
        for i in range(together):
            for l in range(slots):
                score = tall[:, i : i + 1] + work_ref[first + i, l]
                peak = jnp.max(score, axis=0, keepdims=True)
                total = jnp.sum(jnp.exp2(score - peak), axis=0, keepdims=True)
                place = (first + i) * slots + l
                peak_scr[pl.ds(place, 1), :] = peak
                sum_scr[pl.ds(place, 1), :] = total
        return 0

    lax.fori_loop(0, rows // together, some_rows, 0)
    select = select_ref[...]
    peaks = peak_scr[...]
    sums = sum_scr[...]
    blocks = out_ref.shape[0] // copies
    for t in range(blocks):
        chosen = select == t
        peak = jnp.max(jnp.where(chosen, peaks, very_low), axis=0, keepdims=True)
        shifted = jnp.where(chosen, sums * jnp.exp2(jnp.minimum(peaks - peak, 0.0)), 0.0)
        total = jnp.sum(shifted, axis=0, keepdims=True)
        some = total > 0.0
        out_ref[t : t + 1, :] = jnp.where(
            some, peak + jnp.log2(jnp.where(some, total, 1.0)), very_low
        )
    if copies > 1:
        put_copies(out_ref, copies, out_ref[0:blocks, :])


def row_kernel(
    row_devices, slot_ref, tall_ref, log_mass_ref, parts_ref, out_ref, wide_scr, peak_scr, sum_scr
):
    rows, slots, width, _ = tall_ref.shape
    together = math.gcd(rows, 8)
    potential = (log_mass_ref[...] - log_sum(parts_of(parts_ref, row_devices))).T
    for t in range(wide_scr.shape[0]):
        wide_scr[t] = jnp.broadcast_to(potential[:, t : t + 1], (width, width))

    def some_rows(g, _):
        for i in range(together):
            row = g * together + i
            scores = [wide_scr[slot_ref[l, row]] + tall_ref[row, l] for l in range(slots)]
            row_pass(scores, row, peak_scr, sum_scr)
        return 0

    lax.fori_loop(0, rows // together, some_rows, 0)
    out_ref[...] = peak_scr[...] + jnp.log2(sum_scr[...])


def last_kernel(row_devices, row_axis, log_mass_ref, parts_ref, out_ref):
    here = out_ref.shape[0]
    start = lax.axis_index(row_axis) * here
    log_mass = log_mass_ref[pl.ds(start, here), :]
    out_ref[...] = (log_mass - log_sum(parts_of(parts_ref, row_devices))) * from_log2


def per_device(
    coupling,
    coupling_index,
    near_cost,
    near_index,
    source_weights,
    target_cost,
    target_index,
    target_weights,
):
    rows_here = coupling.shape[0]
    slots = coupling.shape[2]
    width = coupling.shape[3]
    near_count = near_cost.shape[1]
    group_blocks = target_index.shape[1]
    link_count = target_index.shape[2]
    target_here = target_cost.shape[1]
    row_devices = lax.axis_size("rows")
    col_devices = lax.axis_size("cols")
    source_count = rows_here * row_devices * width
    target_count = group_blocks * width * col_devices
    f32 = jnp.float32
    arrived = {0: target_cost}
    late = [mask for mask in range(5, row_devices, 2)]
    for mask in range(1, row_devices):
        if mask not in late:
            arrived[mask] = send(target_cost, "rows", mask)

    near_t = in_hbm(near_index.T)
    slot_t = in_hbm(coupling_index[:, 0, :].T)
    link_t = in_hbm(jnp.transpose(target_index, (2, 0, 1)))
    mass = in_hbm(source_weights.reshape(rows_here, width))
    small = pltpu.CompilerParams(vmem_limit_bytes=4 * mib)

    wide = near_count * slots * width
    groups = rows_here // SUB
    x, term = pl.pallas_call(
        near_kernel,
        grid=(groups,),
        in_specs=[
            SMEM,
            pl.BlockSpec((SUB, near_count, width, width), lambda g: (g, 0, 0, 0)),
            pl.BlockSpec((SUB, 1, slots, width, width), lambda g: (g, 0, 0, 0, 0)),
            whole((rows_here, width)),
        ],
        out_specs=[VMEM, VMEM],
        out_shape=[
            pltpu.VMEM((rows_here, 2 * width, wide), jnp.bfloat16),
            pltpu.VMEM((groups, width, SUB), f32),
        ],
        scratch_shapes=[pltpu.VMEM((SUB, 3 * width, slots * width), jnp.bfloat16)],
        compiler_params=pltpu.CompilerParams(vmem_limit_bytes=12 * mib),
        cost_estimate=pl.CostEstimate(
            flops=6 * rows_here * wide * width * width,
            bytes_accessed=4 * rows_here * width * (near_count + slots) * width,
            transcendentals=0,
        ),
        name="near_product",
    )(near_t, in_hbm(near_cost), in_hbm(coupling), mass)

    sources = [mask - 1 for mask in late] or [0]
    passed = pl.pallas_call(
        relay_kernel,
        in_specs=[ANY] * (1 + len(sources)),
        out_specs=[ANY] * len(sources),
        out_shape=[jax.ShapeDtypeStruct(target_cost.shape, f32)] * len(sources),
        input_output_aliases={1 + e: e for e in range(len(sources))},
        compiler_params=small,
        name="relay",
    )(in_vmem(term), *[arrived[mask] for mask in sources])
    for mask, block in zip(sources, passed):
        arrived[mask] = block
    for mask in late:
        arrived[mask] = send(arrived[mask - 1], "rows", 1)
    cost_parts = [arrived[s] for s in range(row_devices)]

    pack_rows = 8 * pl.cdiv(1 + target_here, 8)
    devices = row_devices * col_devices
    pack = pl.pallas_call(
        functools.partial(pack_kernel, devices),
        in_specs=[ANY, VMEM, VMEM],
        out_shape=jax.ShapeDtypeStruct((devices * pack_rows, width), f32),
        compiler_params=small,
        name="pack",
    )(passed[0], mass, in_hbm(target_weights.reshape(target_here, width)))
    packs = exchange(pack, ("rows", "cols"))

    far_bytes = group_blocks * link_count * width * width * 4
    step_rows = SUB
    steps = rows_here // step_rows
    cost_block = pl.BlockSpec((step_rows, 1, slots, width, width), lambda g: (g, 0, 0, 0, 0))
    work_shape = pltpu.VMEM((rows_here, slots, width, width), f32)
    cost_blocks, work, tall, row_part, log_source, log_target, select = pl.pallas_call(
        functools.partial(
            far_kernel,
            (row_devices, col_devices, target_here, source_count, target_count, group_blocks, link_count),
            "rows",
            "cols",
        ),
        grid=(steps,),
        in_specs=[SMEM, SMEM, SMEM, VMEM, VMEM, whole((rows_here, width))]
        + [VMEM] * row_devices
        + [whole(packs.shape)],
        out_specs=[
            cost_block,
            VMEM,
            VMEM,
            whole((rows_here, width)),
            whole((rows_here, width)),
            whole((group_blocks, width)),
            whole((rows_here * slots, width)),
        ],
        out_shape=[
            jax.ShapeDtypeStruct(coupling.shape, f32),
            work_shape,
            work_shape,
            jax.ShapeDtypeStruct((rows_here, width), f32),
            jax.ShapeDtypeStruct((rows_here, width), f32),
            jax.ShapeDtypeStruct((group_blocks, width), f32),
            jax.ShapeDtypeStruct((rows_here * slots, width), jnp.int32),
        ],
        scratch_shapes=[
            pltpu.VMEM((group_blocks * link_count + 1, width, width), jnp.bfloat16),
            pltpu.VMEM((group_blocks * link_count + 1, width, width), jnp.bfloat16),
            pltpu.SMEM((group_blocks * group_blocks,), jnp.int32),
            pltpu.VMEM((group_blocks, width), f32),
            pltpu.VMEM((1, width), f32),
            pltpu.VMEM((rows_here, width), f32),
            pltpu.VMEM((rows_here, width), f32),
        ],
        compiler_params=pltpu.CompilerParams(vmem_limit_bytes=12 * mib + 2 * far_bytes),
        name="far_product",
    )(near_t, slot_t, link_t, in_vmem(x), in_vmem(term), mass, *cost_parts, packs)

    pass_params = pltpu.CompilerParams(vmem_limit_bytes=12 * mib)

    def column_step(row_parts, copies):
        return pl.pallas_call(
            functools.partial(column_kernel, col_devices, copies),
            in_specs=[VMEM] * (3 + col_devices),
            out_specs=[VMEM, VMEM],
            out_shape=[
                jax.ShapeDtypeStruct((copies * group_blocks, width), f32),
                jax.ShapeDtypeStruct((rows_here, width), f32),
            ],
            scratch_shapes=[
                pltpu.VMEM((rows_here, width), f32),
                pltpu.VMEM((rows_here * slots, width), f32),
                pltpu.VMEM((rows_here * slots, width), f32),
            ],
            compiler_params=pass_params,
            name="column_pass",
        )(in_vmem(work), select, log_source, *row_parts)

    def row_step(column_parts):
        return pl.pallas_call(
            functools.partial(row_kernel, row_devices),
            in_specs=[SMEM, VMEM, VMEM, VMEM],
            out_specs=VMEM,
            out_shape=jax.ShapeDtypeStruct((rows_here, width), f32),
            scratch_shapes=[
                pltpu.VMEM((group_blocks, width, width), f32),
                pltpu.VMEM((rows_here, width), f32),
                pltpu.VMEM((rows_here, width), f32),
            ],
            compiler_params=pass_params,
            name="row_pass",
        )(slot_t, in_vmem(tall), log_target, column_parts)

    for step in range(ITERS):
        last = step == ITERS - 1
        column_part, source_potential = column_step(
            from_all(row_part, "cols"), 1 if last else row_devices
        )
        column_parts = exchange(column_part, "rows")
        if not last:
            row_part = row_step(column_parts)
    own_target = pl.pallas_call(
        functools.partial(last_kernel, row_devices, "rows"),
        out_shape=jax.ShapeDtypeStruct((target_here, width), f32),
        compiler_params=small,
        name="last_potential",
    )(log_target, column_parts)
    return (
        cost_blocks,
        source_potential.reshape(rows_here * width),
        own_target.reshape(1, target_here * width),
    )


def solution(mesh):
    placed = (
        P("rows", "cols", None, None, None),
        P("rows", "cols", None),
        P("rows", None, None, None),
        P("rows", None),
        P("rows"),
        P("cols", "rows", None, None, None),
        P("cols", None, None),
        P("cols", "rows"),
    )
    return jax.shard_map(
        per_device,
        mesh=mesh,
        in_specs=placed,
        out_specs=(P("rows", "cols", None, None, None), P("rows"), P("cols", "rows")),
        check_vma=False,
    )
```

```python
import functools
import math

import jax
import jax.numpy as jnp
from jax import lax
from jax.experimental import pallas as pl
from jax.experimental.pallas import tpu as pltpu
from jax.sharding import PartitionSpec as P

ITERS = 3
SUB = 4

entropy = 0.01
to_log2 = math.log2(math.e) / entropy
from_log2 = entropy * math.log(2.0)
very_low = -1e30
mib = 1024 * 1024

SMEM = pl.BlockSpec(memory_space=pltpu.SMEM)
VMEM = pl.BlockSpec(memory_space=pltpu.VMEM)
ANY = pl.BlockSpec(memory_space=pl.ANY)


def in_hbm(x):
    return pltpu.with_memory_space_constraint(x, pltpu.HBM)


def in_vmem(x):
    return pltpu.with_memory_space_constraint(x, pltpu.VMEM)


def whole(shape):
    return pl.BlockSpec(shape, lambda *_: (0,) * len(shape))


def split(x):
    high = x.astype(jnp.bfloat16)
    return high, (x - high.astype(jnp.float32)).astype(jnp.bfloat16)


def tree(parts, op):
    while len(parts) > 1:
        half = len(parts) // 2
        parts = [op(parts[s], parts[s + half]) for s in range(half)]
    return parts[0]


def log_sum(parts):
    peak = tree(parts, jnp.maximum)
    return peak + jnp.log2(tree([jnp.exp2(p - peak) for p in parts], jnp.add))


def parts_of(ref, devices):
    rows = ref.shape[0] // devices
    return [ref[d * rows : (d + 1) * rows, :] for d in range(devices)]


def put_copies(ref, devices, value):
    rows = value.shape[0]
    for d in range(devices):
        ref[d * rows : (d + 1) * rows, :] = value


def send(x, axis, mask):
    size = lax.axis_size(axis)
    return lax.ppermute(x, axis, [(d, d ^ mask) for d in range(size)])


def from_all(x, axis):
    return [x] + [send(x, axis, s) for s in range(1, lax.axis_size(axis))]


def exchange(copies, axis):
    return lax.all_to_all(copies, axis, 0, 0, tiled=True)


def pack_kernel(devices, source_ref, target_ref, out_ref):
    rows = out_ref.shape[0] // devices
    total = jnp.sum(source_ref[...].astype(jnp.float32), axis=(0, 1), keepdims=True)
    target = target_ref[...].astype(jnp.float32)
    out_ref[...] = jnp.zeros_like(out_ref)
    for d in range(devices):
        out_ref[d * rows : d * rows + 1, :] = jnp.broadcast_to(total, (1, out_ref.shape[1]))
        out_ref[d * rows + 1 : d * rows + 1 + target.shape[0], :] = target


def near_kernel(near_index_ref, cost_ref, plan_ref, mass_ref, totals_ref, x_ref, term_ref, plan_scr):
    g = pl.program_id(0)
    near_count = cost_ref.shape[1]
    width = cost_ref.shape[2]
    slots = plan_ref.shape[2]
    wide = slots * width
    for a in range(SUB):
        plan = jnp.concatenate([plan_ref[a, 0, q] for q in range(slots)], axis=1)
        high, low = split(plan)
        plan_scr[a, 0:width, :] = high
        plan_scr[a, width : 2 * width, :] = low
        plan_scr[a, 2 * width : 3 * width, :] = high
    lanes = lax.broadcasted_iota(jnp.int32, (width, SUB), 1)
    terms = jnp.zeros((width, SUB), jnp.float32)
    for i in range(SUB):
        row = g * SUB + i
        acc = None
        for k in range(near_count):
            a = near_index_ref[k, row] & (SUB - 1)
            cost = cost_ref[i, k]
            high, low = split(cost)
            x = jnp.dot(
                jnp.concatenate([high, high, low], axis=1),
                plan_scr[a],
                preferred_element_type=jnp.float32,
            )
            x_high, x_low = split(x)
            x_ref[row, 0:width, k * wide : (k + 1) * wide] = x_high
            x_ref[row, width : 2 * width, k * wide : (k + 1) * wide] = x_low
            weighted = cost * cost * mass_ref[pl.ds(g * SUB + a, 1), :].astype(jnp.float32)
            acc = weighted if acc is None else acc + weighted
        terms = jnp.where(lanes == i, jnp.sum(acc, axis=1, keepdims=True), terms)
    term_ref[g] = terms


def relay_kernel(*refs):
    pass


def far_kernel(counts, row_axis, col_axis, *refs):
    row_devices, col_devices, target_here, source_count, target_count, group_blocks, link_count = counts
    near_index_ref, slot_ref, link_ref, x_ref, term_ref, mass_ref = refs[:6]
    cost_parts = refs[6 : 6 + row_devices]
    pack_ref, out_ref, work_ref, tall_ref, part_ref, log_source_ref, log_target_ref, select_ref = refs[
        6 + row_devices : 14 + row_devices
    ]
    far_high, far_low, table, column_scr, scale_scr, peak_scr, sum_scr = refs[14 + row_devices :]
    g = pl.program_id(0)
    near_count = near_index_ref.shape[0]
    slots = slot_ref.shape[0]
    rows = out_ref.shape[0]
    width = out_ref.shape[3]
    zero_block = group_blocks * link_count

    @pl.when(g == 0)
    def _():
        me = lax.axis_index(row_axis)
        col = lax.axis_index(col_axis)
        far_high[zero_block] = jnp.zeros((width, width), jnp.bfloat16)
        far_low[zero_block] = jnp.zeros((width, width), jnp.bfloat16)

        def clear(e, _):
            table[e] = zero_block
            return 0

        lax.fori_loop(0, group_blocks * group_blocks, clear, 0)

        def mark(j, _):
            for m in range(link_count):
                table[j * group_blocks + link_ref[m, 0, j]] = j * link_count + m
            return 0

        lax.fori_loop(0, group_blocks, mark, 0)
        pack_rows = pack_ref.shape[0] // (row_devices * col_devices)
        total_source = functools.reduce(
            jnp.add,
            [pack_ref[r * col_devices * pack_rows : r * col_devices * pack_rows + 1, :] for r in range(row_devices)],
        )
        targets = functools.reduce(
            jnp.add,
            [
                pack_ref[d * pack_rows + 1 + h : d * pack_rows + 2 + h, :]
                for d in range(row_devices * col_devices)
                for h in range(target_here)
            ],
        )
        total_target = jnp.sum(targets, axis=1, keepdims=True)
        log_source_ref[...] = jnp.log2(source_count * mass_ref[...].astype(jnp.float32) / total_source)
        scale_scr[...] = source_count / (total_source * (near_count * width))
        column_scr[...] = jnp.zeros_like(column_scr)
        for s in range(row_devices):
            for h in range(target_here):
                j = (me ^ s) * target_here + h
                place = ((me ^ s) * col_devices + col) * pack_rows + 1 + h
                mass = target_count * pack_ref[pl.ds(place, 1), :] / total_target
                log_target_ref[pl.ds(j, 1), :] = jnp.log2(mass)
                tall = jnp.broadcast_to(mass, (width, width)).T
                for m in range(link_count):
                    block = cost_parts[s][0, h, m]
                    high, low = split(block)
                    far_high[j * link_count + m] = high
                    far_low[j * link_count + m] = low
                    spread = jnp.sum(tall * (block * block), axis=0, keepdims=True)
                    t = link_ref[m, 0, j]
                    column_scr[pl.ds(t, 1), :] += spread * (1.0 / (link_count * width))

    group_devices = target_count // (group_blocks * width)
    coef = 2.0 * (1.0 / (near_count * width)) * (1.0 / (slots * group_devices * width))
    scale = scale_scr[0:1, 0:1]
    for i in range(rows):
        row = g * rows + i
        group = row - lax.rem(row, SUB)
        targets = [slot_ref[l, row] for l in range(slots)]
        far_rows = []
        for k in range(near_count):
            a = group + (near_index_ref[k, row] & (SUB - 1))
            for q in range(slots):
                j = slot_ref[q, a]
                far_rows.append([table[j * group_blocks + t] for t in targets])
        right_high = jnp.concatenate(
            [jnp.concatenate([far_high[e] for e in r], axis=1) for r in far_rows], axis=0
        )
        right_low = jnp.concatenate(
            [jnp.concatenate([far_low[e] for e in r], axis=1) for r in far_rows], axis=0
        )
        both = jnp.dot(x_ref[row], right_high, preferred_element_type=jnp.float32)
        rest = jnp.dot(x_ref[row, 0:width, :], right_low, preferred_element_type=jnp.float32)
        product = both[0:width] + (both[width:] + rest)
        tall = term_ref[row // SUB, :, i % SUB : i % SUB + 1] * scale
        scores = []
        for l in range(slots):
            cost = tall + column_scr[pl.ds(targets[l], 1), :] - coef * product[:, l * width : (l + 1) * width]
            out_ref[i, 0, l] = cost
            select_ref[pl.ds(row * slots + l, 1), :] = jnp.full((1, width), targets[l], jnp.int32)
            scaled = cost * -to_log2
            work_ref[row, l] = scaled
            turned = scaled.T
            tall_ref[row, l] = turned
            scores.append(turned)
        row_pass(scores, row, peak_scr, sum_scr)

    @pl.when(g == pl.num_programs(0) - 1)
    def _():
        part_ref[...] = peak_scr[...] + jnp.log2(sum_scr[...])


def row_pass(scores, row, peak_scr, sum_scr):
    peak = jnp.max(functools.reduce(jnp.maximum, scores), axis=0, keepdims=True)
    total = functools.reduce(jnp.add, [jnp.exp2(s - peak) for s in scores])
    peak_scr[pl.ds(row, 1), :] = peak
    sum_scr[pl.ds(row, 1), :] = jnp.sum(total, axis=0, keepdims=True)


def column_kernel(col_devices, copies, work_ref, select_ref, log_mass_ref, *refs):
    parts = refs[:col_devices]
    out_ref, potential_ref, potential_scr, peak_scr, sum_scr = refs[col_devices:]
    rows, slots, width, _ = work_ref.shape
    together = math.gcd(rows, 8)
    scaled = log_mass_ref[...] - log_sum([p[...] for p in parts])
    potential_scr[...] = scaled
    potential_ref[...] = scaled * from_log2

    def some_rows(g, _):
        first = pl.multiple_of(g * together, together)
        tall = potential_scr[pl.ds(first, together), :].T
        for i in range(together):
            for l in range(slots):
                score = tall[:, i : i + 1] + work_ref[first + i, l]
                peak = jnp.max(score, axis=0, keepdims=True)
                total = jnp.sum(jnp.exp2(score - peak), axis=0, keepdims=True)
                place = (first + i) * slots + l
                peak_scr[pl.ds(place, 1), :] = peak
                sum_scr[pl.ds(place, 1), :] = total
        return 0

    lax.fori_loop(0, rows // together, some_rows, 0)
    select = select_ref[...]
    peaks = peak_scr[...]
    sums = sum_scr[...]
    blocks = out_ref.shape[0] // copies
    for t in range(blocks):
        chosen = select == t
        peak = jnp.max(jnp.where(chosen, peaks, very_low), axis=0, keepdims=True)
        shifted = jnp.where(chosen, sums * jnp.exp2(jnp.minimum(peaks - peak, 0.0)), 0.0)
        total = jnp.sum(shifted, axis=0, keepdims=True)
        some = total > 0.0
        out_ref[t : t + 1, :] = jnp.where(
            some, peak + jnp.log2(jnp.where(some, total, 1.0)), very_low
        )
    if copies > 1:
        put_copies(out_ref, copies, out_ref[0:blocks, :])


def row_kernel(
    row_devices, slot_ref, tall_ref, log_mass_ref, parts_ref, out_ref, wide_scr, peak_scr, sum_scr
):
    rows, slots, width, _ = tall_ref.shape
    together = math.gcd(rows, 8)
    potential = (log_mass_ref[...] - log_sum(parts_of(parts_ref, row_devices))).T
    for t in range(wide_scr.shape[0]):
        wide_scr[t] = jnp.broadcast_to(potential[:, t : t + 1], (width, width))

    def some_rows(g, _):
        for i in range(together):
            row = g * together + i
            scores = [wide_scr[slot_ref[l, row]] + tall_ref[row, l] for l in range(slots)]
            row_pass(scores, row, peak_scr, sum_scr)
        return 0

    lax.fori_loop(0, rows // together, some_rows, 0)
    out_ref[...] = peak_scr[...] + jnp.log2(sum_scr[...])


def last_kernel(row_devices, row_axis, log_mass_ref, parts_ref, out_ref):
    here = out_ref.shape[0]
    start = lax.axis_index(row_axis) * here
    log_mass = log_mass_ref[pl.ds(start, here), :]
    out_ref[...] = (log_mass - log_sum(parts_of(parts_ref, row_devices))) * from_log2


def per_device(
    coupling,
    coupling_index,
    near_cost,
    near_index,
    source_weights,
    target_cost,
    target_index,
    target_weights,
):
    rows_here = coupling.shape[0]
    slots = coupling.shape[2]
    width = coupling.shape[3]
    near_count = near_cost.shape[1]
    group_blocks = target_index.shape[1]
    link_count = target_index.shape[2]
    target_here = target_cost.shape[1]
    row_devices = lax.axis_size("rows")
    col_devices = lax.axis_size("cols")
    source_count = rows_here * row_devices * width
    target_count = group_blocks * width * col_devices
    f32 = jnp.float32
    half = row_devices // 2
    arrived = {0: target_cost}
    for mask in range(1, half + 1):
        arrived[mask] = send(target_cost, "rows", mask)

    near_t = in_hbm(near_index.T)
    slot_t = in_hbm(coupling_index[:, 0, :].T)
    link_t = in_hbm(jnp.transpose(target_index, (2, 0, 1)))
    mass = in_hbm(source_weights.reshape(rows_here, width))
    small = pltpu.CompilerParams(vmem_limit_bytes=4 * mib)

    pack_rows = 8 * pl.cdiv(1 + target_here, 8)
    devices = row_devices * col_devices
    pack = pl.pallas_call(
        functools.partial(pack_kernel, devices),
        in_specs=[VMEM, VMEM],
        out_shape=jax.ShapeDtypeStruct((devices * pack_rows, width), f32),
        compiler_params=small,
        name="pack",
    )(mass, in_hbm(target_weights.reshape(target_here, width)))
    packs = exchange(pack, ("rows", "cols"))

    direct = list(range(1, half + 1))
    passed = pl.pallas_call(
        relay_kernel,
        in_specs=[ANY] * half,
        out_specs=[ANY] * half,
        out_shape=[jax.ShapeDtypeStruct(target_cost.shape, f32)] * half,
        input_output_aliases={e: e for e in range(half)},
        compiler_params=small,
        name="relay",
    )(*[arrived[mask] for mask in direct])
    arrived.update(zip(direct, passed))
    for mask in range(half + 1, row_devices):
        arrived[mask] = send(arrived[half], "rows", mask - half)
    cost_parts = [arrived[s] for s in range(row_devices)]

    wide = near_count * slots * width
    groups = rows_here // SUB
    x, term = pl.pallas_call(
        near_kernel,
        grid=(groups,),
        in_specs=[
            SMEM,
            pl.BlockSpec((SUB, near_count, width, width), lambda g: (g, 0, 0, 0)),
            pl.BlockSpec((SUB, 1, slots, width, width), lambda g: (g, 0, 0, 0, 0)),
            whole((rows_here, width)),
            ANY,
        ],
        out_specs=[VMEM, VMEM],
        out_shape=[
            pltpu.VMEM((rows_here, 2 * width, wide), jnp.bfloat16),
            pltpu.VMEM((groups, width, SUB), f32),
        ],
        scratch_shapes=[pltpu.VMEM((SUB, 3 * width, slots * width), jnp.bfloat16)],
        compiler_params=pltpu.CompilerParams(vmem_limit_bytes=12 * mib),
        cost_estimate=pl.CostEstimate(
            flops=6 * rows_here * wide * width * width,
            bytes_accessed=4 * rows_here * width * (near_count + slots) * width,
            transcendentals=0,
        ),
        name="near_product",
    )(near_t, in_hbm(near_cost), in_hbm(coupling), mass, packs)

    far_bytes = group_blocks * link_count * width * width * 4
    step_rows = SUB
    steps = rows_here // step_rows
    cost_block = pl.BlockSpec((step_rows, 1, slots, width, width), lambda g: (g, 0, 0, 0, 0))
    work_shape = pltpu.VMEM((rows_here, slots, width, width), f32)
    cost_blocks, work, tall, row_part, log_source, log_target, select = pl.pallas_call(
        functools.partial(
            far_kernel,
            (row_devices, col_devices, target_here, source_count, target_count, group_blocks, link_count),
            "rows",
            "cols",
        ),
        grid=(steps,),
        in_specs=[SMEM, SMEM, SMEM, VMEM, VMEM, whole((rows_here, width))]
        + [VMEM] * row_devices
        + [whole(packs.shape)],
        out_specs=[
            cost_block,
            VMEM,
            VMEM,
            whole((rows_here, width)),
            whole((rows_here, width)),
            whole((group_blocks, width)),
            whole((rows_here * slots, width)),
        ],
        out_shape=[
            jax.ShapeDtypeStruct(coupling.shape, f32),
            work_shape,
            work_shape,
            jax.ShapeDtypeStruct((rows_here, width), f32),
            jax.ShapeDtypeStruct((rows_here, width), f32),
            jax.ShapeDtypeStruct((group_blocks, width), f32),
            jax.ShapeDtypeStruct((rows_here * slots, width), jnp.int32),
        ],
        scratch_shapes=[
            pltpu.VMEM((group_blocks * link_count + 1, width, width), jnp.bfloat16),
            pltpu.VMEM((group_blocks * link_count + 1, width, width), jnp.bfloat16),
            pltpu.SMEM((group_blocks * group_blocks,), jnp.int32),
            pltpu.VMEM((group_blocks, width), f32),
            pltpu.VMEM((1, width), f32),
            pltpu.VMEM((rows_here, width), f32),
            pltpu.VMEM((rows_here, width), f32),
        ],
        compiler_params=pltpu.CompilerParams(vmem_limit_bytes=12 * mib + 2 * far_bytes),
        name="far_product",
    )(near_t, slot_t, link_t, in_vmem(x), in_vmem(term), mass, *cost_parts, packs)

    pass_params = pltpu.CompilerParams(vmem_limit_bytes=12 * mib)

    def column_step(row_parts, copies):
        return pl.pallas_call(
            functools.partial(column_kernel, col_devices, copies),
            in_specs=[VMEM] * (3 + col_devices),
            out_specs=[VMEM, VMEM],
            out_shape=[
                jax.ShapeDtypeStruct((copies * group_blocks, width), f32),
                jax.ShapeDtypeStruct((rows_here, width), f32),
            ],
            scratch_shapes=[
                pltpu.VMEM((rows_here, width), f32),
                pltpu.VMEM((rows_here * slots, width), f32),
                pltpu.VMEM((rows_here * slots, width), f32),
            ],
            compiler_params=pass_params,
            name="column_pass",
        )(in_vmem(work), select, log_source, *row_parts)

    def row_step(column_parts):
        return pl.pallas_call(
            functools.partial(row_kernel, row_devices),
            in_specs=[SMEM, VMEM, VMEM, VMEM],
            out_specs=VMEM,
            out_shape=jax.ShapeDtypeStruct((rows_here, width), f32),
            scratch_shapes=[
                pltpu.VMEM((group_blocks, width, width), f32),
                pltpu.VMEM((rows_here, width), f32),
                pltpu.VMEM((rows_here, width), f32),
            ],
            compiler_params=pass_params,
            name="row_pass",
        )(slot_t, in_vmem(tall), log_target, column_parts)

    for step in range(ITERS):
        last = step == ITERS - 1
        column_part, source_potential = column_step(
            from_all(row_part, "cols"), 1 if last else row_devices
        )
        column_parts = exchange(column_part, "rows")
        if not last:
            row_part = row_step(column_parts)
    own_target = pl.pallas_call(
        functools.partial(last_kernel, row_devices, "rows"),
        out_shape=jax.ShapeDtypeStruct((target_here, width), f32),
        compiler_params=small,
        name="last_potential",
    )(log_target, column_parts)
    return (
        cost_blocks,
        source_potential.reshape(rows_here * width),
        own_target.reshape(1, target_here * width),
    )


def solution(mesh):
    placed = (
        P("rows", "cols", None, None, None),
        P("rows", "cols", None),
        P("rows", None, None, None),
        P("rows", None),
        P("rows"),
        P("cols", "rows", None, None, None),
        P("cols", None, None),
        P("cols", "rows"),
    )
    return jax.shard_map(
        per_device,
        mesh=mesh,
        in_specs=placed,
        out_specs=(P("rows", "cols", None, None, None), P("rows"), P("cols", "rows")),
        check_vma=False,
    )
```

```python
import functools
import math

import jax
import jax.numpy as jnp
from jax import lax
from jax.experimental import pallas as pl
from jax.experimental.pallas import tpu as pltpu
from jax.sharding import PartitionSpec as P

ITERS = 3
SUB = 4

entropy = 0.01
to_log2 = math.log2(math.e) / entropy
from_log2 = entropy * math.log(2.0)
very_low = -1e30
mib = 1024 * 1024

SMEM = pl.BlockSpec(memory_space=pltpu.SMEM)
VMEM = pl.BlockSpec(memory_space=pltpu.VMEM)
ANY = pl.BlockSpec(memory_space=pl.ANY)


def in_hbm(x):
    return pltpu.with_memory_space_constraint(x, pltpu.HBM)


def in_vmem(x):
    return pltpu.with_memory_space_constraint(x, pltpu.VMEM)


def whole(shape):
    return pl.BlockSpec(shape, lambda *_: (0,) * len(shape))


def split(x):
    high = x.astype(jnp.bfloat16)
    return high, (x - high.astype(jnp.float32)).astype(jnp.bfloat16)


def tree(parts, op):
    while len(parts) > 1:
        half = len(parts) // 2
        parts = [op(parts[s], parts[s + half]) for s in range(half)]
    return parts[0]


def log_sum(parts):
    peak = tree(parts, jnp.maximum)
    return peak + jnp.log2(tree([jnp.exp2(p - peak) for p in parts], jnp.add))


def parts_of(ref, devices):
    rows = ref.shape[0] // devices
    return [ref[d * rows : (d + 1) * rows, :] for d in range(devices)]


def put_copies(ref, devices, value):
    rows = value.shape[0]
    for d in range(devices):
        ref[d * rows : (d + 1) * rows, :] = value


def send(x, axis, mask):
    size = lax.axis_size(axis)
    return lax.ppermute(x, axis, [(d, d ^ mask) for d in range(size)])


def from_all(x, axis):
    return [x] + [send(x, axis, s) for s in range(1, lax.axis_size(axis))]


def exchange(copies, axis):
    return lax.all_to_all(copies, axis, 0, 0, tiled=True)


def pack_kernel(devices, source_ref, target_ref, out_ref):
    rows = out_ref.shape[0] // devices
    total = jnp.sum(source_ref[...].astype(jnp.float32), axis=(0, 1), keepdims=True)
    target = target_ref[...].astype(jnp.float32)
    out_ref[...] = jnp.zeros_like(out_ref)
    for d in range(devices):
        out_ref[d * rows : d * rows + 1, :] = jnp.broadcast_to(total, (1, out_ref.shape[1]))
        out_ref[d * rows + 1 : d * rows + 1 + target.shape[0], :] = target


def near_kernel(near_index_ref, cost_ref, plan_ref, mass_ref, totals_ref, x_ref, term_ref, plan_scr):
    rows = cost_ref.shape[0]
    first = pl.program_id(0) * rows
    near_count = cost_ref.shape[1]
    width = cost_ref.shape[2]
    slots = plan_ref.shape[2]
    wide = slots * width
    for a in range(rows):
        plan = jnp.concatenate([plan_ref[a, 0, q] for q in range(slots)], axis=1)
        high, low = split(plan)
        plan_scr[a, 0:width, :] = high
        plan_scr[a, width : 2 * width, :] = low
        plan_scr[a, 2 * width : 3 * width, :] = high
    lanes = lax.broadcasted_iota(jnp.int32, (width, SUB), 1)
    for group in range(rows // SUB):
        terms = jnp.zeros((width, SUB), jnp.float32)
        for i in range(group * SUB, (group + 1) * SUB):
            acc = None
            for k in range(near_count):
                a = group * SUB + (near_index_ref[k, first + i] & (SUB - 1))
                cost = cost_ref[i, k]
                high, low = split(cost)
                x = jnp.dot(
                    jnp.concatenate([high, high, low], axis=1),
                    plan_scr[a],
                    preferred_element_type=jnp.float32,
                )
                x_high, x_low = split(x)
                x_ref[first + i, 0:width, k * wide : (k + 1) * wide] = x_high
                x_ref[first + i, width : 2 * width, k * wide : (k + 1) * wide] = x_low
                weighted = cost * cost * mass_ref[pl.ds(first + a, 1), :].astype(jnp.float32)
                acc = weighted if acc is None else acc + weighted
            terms = jnp.where(lanes == i % SUB, jnp.sum(acc, axis=1, keepdims=True), terms)
        term_ref[first // SUB + group] = terms


def relay_kernel(*refs):
    pass


def far_kernel(counts, row_axis, col_axis, *refs):
    row_devices, col_devices, target_here, source_count, target_count, group_blocks, link_count = counts
    near_index_ref, slot_ref, link_ref, x_ref, term_ref, mass_ref = refs[:6]
    cost_parts = refs[6 : 6 + row_devices]
    pack_ref, out_ref, work_ref, tall_ref, part_ref, log_source_ref, log_target_ref, select_ref = refs[
        6 + row_devices : 14 + row_devices
    ]
    far_high, far_low, table, column_scr, scale_scr, peak_scr, sum_scr = refs[14 + row_devices :]
    g = pl.program_id(0)
    near_count = near_index_ref.shape[0]
    slots = slot_ref.shape[0]
    rows = out_ref.shape[0]
    width = out_ref.shape[3]
    zero_block = group_blocks * link_count

    @pl.when(g == 0)
    def _():
        me = lax.axis_index(row_axis)
        col = lax.axis_index(col_axis)
        far_high[zero_block] = jnp.zeros((width, width), jnp.bfloat16)
        far_low[zero_block] = jnp.zeros((width, width), jnp.bfloat16)

        def clear(e, _):
            table[e] = zero_block
            return 0

        lax.fori_loop(0, group_blocks * group_blocks, clear, 0)

        def mark(j, _):
            for m in range(link_count):
                table[j * group_blocks + link_ref[m, 0, j]] = j * link_count + m
            return 0

        lax.fori_loop(0, group_blocks, mark, 0)
        pack_rows = pack_ref.shape[0] // (row_devices * col_devices)
        total_source = functools.reduce(
            jnp.add,
            [pack_ref[r * col_devices * pack_rows : r * col_devices * pack_rows + 1, :] for r in range(row_devices)],
        )
        targets = functools.reduce(
            jnp.add,
            [
                pack_ref[d * pack_rows + 1 + h : d * pack_rows + 2 + h, :]
                for d in range(row_devices * col_devices)
                for h in range(target_here)
            ],
        )
        total_target = jnp.sum(targets, axis=1, keepdims=True)
        log_source_ref[...] = jnp.log2(source_count * mass_ref[...].astype(jnp.float32) / total_source)
        scale_scr[...] = source_count / (total_source * (near_count * width))
        column_scr[...] = jnp.zeros_like(column_scr)
        for s in range(row_devices):
            for h in range(target_here):
                j = (me ^ s) * target_here + h
                place = ((me ^ s) * col_devices + col) * pack_rows + 1 + h
                mass = target_count * pack_ref[pl.ds(place, 1), :] / total_target
                log_target_ref[pl.ds(j, 1), :] = jnp.log2(mass)
                tall = jnp.broadcast_to(mass, (width, width)).T
                for m in range(link_count):
                    block = cost_parts[s][0, h, m]
                    high, low = split(block)
                    far_high[j * link_count + m] = high
                    far_low[j * link_count + m] = low
                    spread = jnp.sum(tall * (block * block), axis=0, keepdims=True)
                    t = link_ref[m, 0, j]
                    column_scr[pl.ds(t, 1), :] += spread * (1.0 / (link_count * width))

    group_devices = target_count // (group_blocks * width)
    coef = 2.0 * (1.0 / (near_count * width)) * (1.0 / (slots * group_devices * width))
    scale = scale_scr[0:1, 0:1]
    for i in range(rows):
        row = g * rows + i
        group = row - lax.rem(row, SUB)
        targets = [slot_ref[l, row] for l in range(slots)]
        far_rows = []
        for k in range(near_count):
            a = group + (near_index_ref[k, row] & (SUB - 1))
            for q in range(slots):
                j = slot_ref[q, a]
                far_rows.append([table[j * group_blocks + t] for t in targets])
        right_high = jnp.concatenate(
            [jnp.concatenate([far_high[e] for e in r], axis=1) for r in far_rows], axis=0
        )
        right_low = jnp.concatenate(
            [jnp.concatenate([far_low[e] for e in r], axis=1) for r in far_rows], axis=0
        )
        both = jnp.dot(x_ref[row], right_high, preferred_element_type=jnp.float32)
        rest = jnp.dot(x_ref[row, 0:width, :], right_low, preferred_element_type=jnp.float32)
        product = both[0:width] + (both[width:] + rest)
        tall = term_ref[row // SUB, :, i % SUB : i % SUB + 1] * scale
        scores = []
        for l in range(slots):
            cost = tall + column_scr[pl.ds(targets[l], 1), :] - coef * product[:, l * width : (l + 1) * width]
            out_ref[i, 0, l] = cost
            select_ref[pl.ds(row * slots + l, 1), :] = jnp.full((1, width), targets[l], jnp.int32)
            scaled = cost * -to_log2
            work_ref[row, l] = scaled
            turned = scaled.T
            tall_ref[row, l] = turned
            scores.append(turned)
        row_pass(scores, row, peak_scr, sum_scr)

    @pl.when(g == pl.num_programs(0) - 1)
    def _():
        part_ref[...] = peak_scr[...] + jnp.log2(sum_scr[...])


def row_pass(scores, row, peak_scr, sum_scr):
    peak = jnp.max(functools.reduce(jnp.maximum, scores), axis=0, keepdims=True)
    total = functools.reduce(jnp.add, [jnp.exp2(s - peak) for s in scores])
    peak_scr[pl.ds(row, 1), :] = peak
    sum_scr[pl.ds(row, 1), :] = jnp.sum(total, axis=0, keepdims=True)


def column_kernel(col_devices, copies, work_ref, select_ref, log_mass_ref, *refs):
    parts = refs[:col_devices]
    out_ref, potential_ref, potential_scr, peak_scr, sum_scr = refs[col_devices:]
    rows, slots, width, _ = work_ref.shape
    together = math.gcd(rows, 8)
    scaled = log_mass_ref[...] - log_sum([p[...] for p in parts])
    potential_scr[...] = scaled
    potential_ref[...] = scaled * from_log2

    for first in range(0, rows, together):
        tall = potential_scr[first : first + together, :].T
        for i in range(together):
            for l in range(slots):
                score = tall[:, i : i + 1] + work_ref[first + i, l]
                peak = jnp.max(score, axis=0, keepdims=True)
                total = jnp.sum(jnp.exp2(score - peak), axis=0, keepdims=True)
                place = (first + i) * slots + l
                peak_scr[place : place + 1, :] = peak
                sum_scr[place : place + 1, :] = total
    select = select_ref[...]
    peaks = peak_scr[...]
    sums = sum_scr[...]
    blocks = out_ref.shape[0] // copies
    for t in range(blocks):
        chosen = select == t
        peak = jnp.max(jnp.where(chosen, peaks, very_low), axis=0, keepdims=True)
        shifted = jnp.where(chosen, sums * jnp.exp2(jnp.minimum(peaks - peak, 0.0)), 0.0)
        total = jnp.sum(shifted, axis=0, keepdims=True)
        some = total > 0.0
        out_ref[t : t + 1, :] = jnp.where(
            some, peak + jnp.log2(jnp.where(some, total, 1.0)), very_low
        )
    if copies > 1:
        put_copies(out_ref, copies, out_ref[0:blocks, :])


def row_kernel(
    row_devices, slot_ref, tall_ref, log_mass_ref, parts_ref, out_ref, wide_scr, peak_scr, sum_scr
):
    rows, slots, width, _ = tall_ref.shape
    potential = (log_mass_ref[...] - log_sum(parts_of(parts_ref, row_devices))).T
    for t in range(wide_scr.shape[0]):
        wide_scr[t] = jnp.broadcast_to(potential[:, t : t + 1], (width, width))

    for row in range(rows):
        scores = [wide_scr[slot_ref[l, row]] + tall_ref[row, l] for l in range(slots)]
        row_pass(scores, row, peak_scr, sum_scr)
    out_ref[...] = peak_scr[...] + jnp.log2(sum_scr[...])


def last_kernel(row_devices, row_axis, log_mass_ref, parts_ref, out_ref):
    here = out_ref.shape[0]
    start = lax.axis_index(row_axis) * here
    log_mass = log_mass_ref[pl.ds(start, here), :]
    out_ref[...] = (log_mass - log_sum(parts_of(parts_ref, row_devices))) * from_log2


def per_device(
    coupling,
    coupling_index,
    near_cost,
    near_index,
    source_weights,
    target_cost,
    target_index,
    target_weights,
):
    rows_here = coupling.shape[0]
    slots = coupling.shape[2]
    width = coupling.shape[3]
    near_count = near_cost.shape[1]
    group_blocks = target_index.shape[1]
    link_count = target_index.shape[2]
    target_here = target_cost.shape[1]
    row_devices = lax.axis_size("rows")
    col_devices = lax.axis_size("cols")
    source_count = rows_here * row_devices * width
    target_count = group_blocks * width * col_devices
    f32 = jnp.float32
    half = row_devices // 2
    arrived = {0: target_cost}
    for mask in range(1, half + 1):
        arrived[mask] = send(target_cost, "rows", mask)

    near_t = in_hbm(near_index.T)
    slot_t = in_hbm(coupling_index[:, 0, :].T)
    link_t = in_hbm(jnp.transpose(target_index, (2, 0, 1)))
    mass = in_hbm(source_weights.reshape(rows_here, width))
    small = pltpu.CompilerParams(vmem_limit_bytes=4 * mib)

    pack_rows = 8 * pl.cdiv(1 + target_here, 8)
    devices = row_devices * col_devices
    pack = pl.pallas_call(
        functools.partial(pack_kernel, devices),
        in_specs=[VMEM, VMEM],
        out_shape=jax.ShapeDtypeStruct((devices * pack_rows, width), f32),
        compiler_params=small,
        name="pack",
    )(mass, in_hbm(target_weights.reshape(target_here, width)))
    packs = exchange(pack, ("rows", "cols"))

    direct = list(range(1, half + 1))
    passed = pl.pallas_call(
        relay_kernel,
        in_specs=[ANY] * half,
        out_specs=[ANY] * half,
        out_shape=[jax.ShapeDtypeStruct(target_cost.shape, f32)] * half,
        input_output_aliases={e: e for e in range(half)},
        compiler_params=small,
        cost_estimate=pl.CostEstimate(flops=0, bytes_accessed=256 * mib, transcendentals=0),
        name="relay",
    )(*[arrived[mask] for mask in direct])
    arrived.update(zip(direct, passed))
    for mask in range(half + 1, row_devices):
        arrived[mask] = send(arrived[half], "rows", mask - half)
    cost_parts = [arrived[s] for s in range(row_devices)]

    wide = near_count * slots * width
    groups = rows_here // SUB
    step_rows = 2 * SUB if groups % 2 == 0 else SUB
    x, term = pl.pallas_call(
        near_kernel,
        grid=(rows_here // step_rows,),
        in_specs=[
            SMEM,
            pl.BlockSpec((step_rows, near_count, width, width), lambda g: (g, 0, 0, 0)),
            pl.BlockSpec((step_rows, 1, slots, width, width), lambda g: (g, 0, 0, 0, 0)),
            whole((rows_here, width)),
            ANY,
        ],
        out_specs=[VMEM, VMEM],
        out_shape=[
            pltpu.VMEM((rows_here, 2 * width, wide), jnp.bfloat16),
            pltpu.VMEM((groups, width, SUB), f32),
        ],
        scratch_shapes=[pltpu.VMEM((step_rows, 3 * width, slots * width), jnp.bfloat16)],
        compiler_params=pltpu.CompilerParams(vmem_limit_bytes=12 * mib),
        cost_estimate=pl.CostEstimate(
            flops=6 * rows_here * wide * width * width,
            bytes_accessed=4 * rows_here * width * (near_count + slots) * width,
            transcendentals=0,
        ),
        name="near_product",
    )(near_t, in_hbm(near_cost), in_hbm(coupling), mass, packs)

    far_bytes = group_blocks * link_count * width * width * 4
    steps = rows_here // step_rows
    cost_block = pl.BlockSpec((step_rows, 1, slots, width, width), lambda g: (g, 0, 0, 0, 0))
    work_shape = pltpu.VMEM((rows_here, slots, width, width), f32)
    cost_blocks, work, tall, row_part, log_source, log_target, select = pl.pallas_call(
        functools.partial(
            far_kernel,
            (row_devices, col_devices, target_here, source_count, target_count, group_blocks, link_count),
            "rows",
            "cols",
        ),
        grid=(steps,),
        in_specs=[SMEM, SMEM, SMEM, VMEM, VMEM, whole((rows_here, width))]
        + [VMEM] * row_devices
        + [whole(packs.shape)],
        out_specs=[
            cost_block,
            VMEM,
            VMEM,
            whole((rows_here, width)),
            whole((rows_here, width)),
            whole((group_blocks, width)),
            whole((rows_here * slots, width)),
        ],
        out_shape=[
            jax.ShapeDtypeStruct(coupling.shape, f32),
            work_shape,
            work_shape,
            jax.ShapeDtypeStruct((rows_here, width), f32),
            jax.ShapeDtypeStruct((rows_here, width), f32),
            jax.ShapeDtypeStruct((group_blocks, width), f32),
            jax.ShapeDtypeStruct((rows_here * slots, width), jnp.int32),
        ],
        scratch_shapes=[
            pltpu.VMEM((group_blocks * link_count + 1, width, width), jnp.bfloat16),
            pltpu.VMEM((group_blocks * link_count + 1, width, width), jnp.bfloat16),
            pltpu.SMEM((group_blocks * group_blocks,), jnp.int32),
            pltpu.VMEM((group_blocks, width), f32),
            pltpu.VMEM((1, width), f32),
            pltpu.VMEM((rows_here, width), f32),
            pltpu.VMEM((rows_here, width), f32),
        ],
        compiler_params=pltpu.CompilerParams(vmem_limit_bytes=12 * mib + 2 * far_bytes),
        name="far_product",
    )(near_t, slot_t, link_t, in_vmem(x), in_vmem(term), mass, *cost_parts, packs)

    pass_params = pltpu.CompilerParams(vmem_limit_bytes=12 * mib)

    def column_step(row_parts, copies):
        return pl.pallas_call(
            functools.partial(column_kernel, col_devices, copies),
            in_specs=[VMEM] * (3 + col_devices),
            out_specs=[VMEM, VMEM],
            out_shape=[
                jax.ShapeDtypeStruct((copies * group_blocks, width), f32),
                jax.ShapeDtypeStruct((rows_here, width), f32),
            ],
            scratch_shapes=[
                pltpu.VMEM((rows_here, width), f32),
                pltpu.VMEM((rows_here * slots, width), f32),
                pltpu.VMEM((rows_here * slots, width), f32),
            ],
            compiler_params=pass_params,
            name="column_pass",
        )(in_vmem(work), select, log_source, *row_parts)

    def row_step(column_parts):
        return pl.pallas_call(
            functools.partial(row_kernel, row_devices),
            in_specs=[SMEM, VMEM, VMEM, VMEM],
            out_specs=VMEM,
            out_shape=jax.ShapeDtypeStruct((rows_here, width), f32),
            scratch_shapes=[
                pltpu.VMEM((group_blocks, width, width), f32),
                pltpu.VMEM((rows_here, width), f32),
                pltpu.VMEM((rows_here, width), f32),
            ],
            compiler_params=pass_params,
            name="row_pass",
        )(slot_t, in_vmem(tall), log_target, column_parts)

    for step in range(ITERS):
        last = step == ITERS - 1
        column_part, source_potential = column_step(
            from_all(row_part, "cols"), 1 if last else row_devices
        )
        column_parts = exchange(column_part, "rows")
        if not last:
            row_part = row_step(column_parts)
    own_target = pl.pallas_call(
        functools.partial(last_kernel, row_devices, "rows"),
        out_shape=jax.ShapeDtypeStruct((target_here, width), f32),
        compiler_params=small,
        name="last_potential",
    )(log_target, column_parts)
    return (
        cost_blocks,
        source_potential.reshape(rows_here * width),
        own_target.reshape(1, target_here * width),
    )


def solution(mesh):
    placed = (
        P("rows", "cols", None, None, None),
        P("rows", "cols", None),
        P("rows", None, None, None),
        P("rows", None),
        P("rows"),
        P("cols", "rows", None, None, None),
        P("cols", None, None),
        P("cols", "rows"),
    )
    return jax.shard_map(
        per_device,
        mesh=mesh,
        in_specs=placed,
        out_specs=(P("rows", "cols", None, None, None), P("rows"), P("cols", "rows")),
        check_vma=False,
    )
```

```python
import functools
import math

import jax
import jax.numpy as jnp
from jax import lax
from jax.experimental import pallas as pl
from jax.experimental.pallas import tpu as pltpu
from jax.sharding import PartitionSpec as P

ITERS = 3
SUB = 4

entropy = 0.01
to_log2 = math.log2(math.e) / entropy
from_log2 = entropy * math.log(2.0)
very_low = -1e30
mib = 1024 * 1024

SMEM = pl.BlockSpec(memory_space=pltpu.SMEM)
VMEM = pl.BlockSpec(memory_space=pltpu.VMEM)
ANY = pl.BlockSpec(memory_space=pl.ANY)


def in_hbm(x):
    return pltpu.with_memory_space_constraint(x, pltpu.HBM)


def in_vmem(x):
    return pltpu.with_memory_space_constraint(x, pltpu.VMEM)


def whole(shape):
    return pl.BlockSpec(shape, lambda *_: (0,) * len(shape))


def split(x):
    high = x.astype(jnp.bfloat16)
    return high, (x - high.astype(jnp.float32)).astype(jnp.bfloat16)


def tree(parts, op):
    while len(parts) > 1:
        half = len(parts) // 2
        parts = [op(parts[s], parts[s + half]) for s in range(half)]
    return parts[0]


def log_sum(parts):
    peak = tree(parts, jnp.maximum)
    return peak + jnp.log2(tree([jnp.exp2(p - peak) for p in parts], jnp.add))


def send(x, axis, mask):
    size = lax.axis_size(axis)
    return lax.ppermute(x, axis, [(d, d ^ mask) for d in range(size)])


def from_all(x, axis):
    return [x] + [send(x, axis, s) for s in range(1, lax.axis_size(axis))]


def exchange(copies, axis):
    return lax.all_to_all(copies, axis, 0, 0, tiled=True)


def pack_kernel(devices, source_ref, target_ref, out_ref):
    rows = out_ref.shape[0] // devices
    total = jnp.sum(source_ref[...].astype(jnp.float32), axis=(0, 1), keepdims=True)
    target = target_ref[...].astype(jnp.float32)
    for d in range(devices):
        out_ref[d * rows : d * rows + 1, :] = jnp.broadcast_to(total, (1, out_ref.shape[1]))
        out_ref[d * rows + 1 : d * rows + 1 + target.shape[0], :] = target


def near_kernel(near_index_ref, cost_ref, plan_ref, mass_ref, totals_ref, x_ref, term_ref, plan_scr):
    rows = cost_ref.shape[0]
    first = pl.program_id(0) * rows
    near_count = cost_ref.shape[1]
    width = cost_ref.shape[2]
    slots = plan_ref.shape[2]
    wide = slots * width
    for a in range(rows):
        plan = jnp.concatenate([plan_ref[a, 0, q] for q in range(slots)], axis=1)
        high, low = split(plan)
        plan_scr[a, 0:width, :] = high
        plan_scr[a, width : 2 * width, :] = low
        plan_scr[a, 2 * width : 3 * width, :] = high
    lanes = lax.broadcasted_iota(jnp.int32, (width, SUB), 1)
    for group in range(rows // SUB):
        terms = jnp.zeros((width, SUB), jnp.float32)
        for i in range(group * SUB, (group + 1) * SUB):
            acc = None
            for k in range(near_count):
                a = group * SUB + (near_index_ref[k, first + i] & (SUB - 1))
                cost = cost_ref[i, k]
                high, low = split(cost)
                x = jnp.dot(
                    jnp.concatenate([high, high, low], axis=1),
                    plan_scr[a],
                    preferred_element_type=jnp.float32,
                )
                x_high, x_low = split(x)
                x_ref[first + i, 0:width, k * wide : (k + 1) * wide] = x_high
                x_ref[first + i, width : 2 * width, k * wide : (k + 1) * wide] = x_low
                weighted = cost * cost * mass_ref[pl.ds(first + a, 1), :].astype(jnp.float32)
                acc = weighted if acc is None else acc + weighted
            terms = jnp.where(lanes == i % SUB, jnp.sum(acc, axis=1, keepdims=True), terms)
        term_ref[first // SUB + group] = terms


def relay_kernel(*refs):
    pass


def far_kernel(counts, row_axis, col_axis, *refs):
    row_devices, col_devices, target_here, source_count, target_count, group_blocks, link_count = counts
    near_index_ref, slot_ref, link_ref, x_ref, term_ref, mass_ref = refs[:6]
    cost_parts = refs[6 : 6 + row_devices]
    pack_ref, out_ref, work_ref, tall_ref, part_ref, log_source_ref, log_target_ref, select_ref = refs[
        6 + row_devices : 14 + row_devices
    ]
    far_high, far_low, table, column_scr, scale_scr, peak_scr, sum_scr = refs[14 + row_devices :]
    g = pl.program_id(0)
    near_count = near_index_ref.shape[0]
    slots = slot_ref.shape[0]
    rows = out_ref.shape[0]
    width = out_ref.shape[3]
    zero_block = group_blocks * link_count

    @pl.when(g == 0)
    def _():
        me = lax.axis_index(row_axis)
        col = lax.axis_index(col_axis)
        far_high[zero_block] = jnp.zeros((width, width), jnp.bfloat16)
        far_low[zero_block] = jnp.zeros((width, width), jnp.bfloat16)

        def clear(e, _):
            table[e] = zero_block
            return 0

        lax.fori_loop(0, group_blocks * group_blocks, clear, 0)

        def mark(j, _):
            for m in range(link_count):
                table[j * group_blocks + link_ref[m, 0, j]] = j * link_count + m
            return 0

        lax.fori_loop(0, group_blocks, mark, 0)
        pack_rows = pack_ref.shape[0] // (row_devices * col_devices)
        total_source = functools.reduce(
            jnp.add,
            [pack_ref[r * col_devices * pack_rows : r * col_devices * pack_rows + 1, :] for r in range(row_devices)],
        )
        targets = functools.reduce(
            jnp.add,
            [
                pack_ref[d * pack_rows + 1 + h : d * pack_rows + 2 + h, :]
                for d in range(row_devices * col_devices)
                for h in range(target_here)
            ],
        )
        total_target = jnp.sum(targets, axis=1, keepdims=True)
        log_source_ref[...] = jnp.log2(source_count * mass_ref[...].astype(jnp.float32) / total_source)
        scale_scr[...] = source_count / (total_source * (near_count * width))
        column_scr[...] = jnp.zeros_like(column_scr)
        for s in range(row_devices):
            for h in range(target_here):
                j = (me ^ s) * target_here + h
                place = ((me ^ s) * col_devices + col) * pack_rows + 1 + h
                mass = target_count * pack_ref[pl.ds(place, 1), :] / total_target
                log_target_ref[pl.ds(j, 1), :] = jnp.log2(mass)
                tall = jnp.broadcast_to(mass, (width, width)).T
                for m in range(link_count):
                    block = cost_parts[s][0, h, m]
                    high, low = split(block)
                    far_high[j * link_count + m] = high
                    far_low[j * link_count + m] = low
                    spread = jnp.sum(tall * (block * block), axis=0, keepdims=True)
                    t = link_ref[m, 0, j]
                    column_scr[pl.ds(t, 1), :] += spread * (1.0 / (link_count * width))

    group_devices = target_count // (group_blocks * width)
    coef = 2.0 * (1.0 / (near_count * width)) * (1.0 / (slots * group_devices * width))
    scale = scale_scr[0:1, 0:1]
    for i in range(rows):
        row = g * rows + i
        group = row - lax.rem(row, SUB)
        targets = [slot_ref[l, row] for l in range(slots)]
        far_rows = []
        for k in range(near_count):
            a = group + (near_index_ref[k, row] & (SUB - 1))
            for q in range(slots):
                j = slot_ref[q, a]
                far_rows.append([table[j * group_blocks + t] for t in targets])
        right_high = jnp.concatenate(
            [jnp.concatenate([far_high[e] for e in r], axis=1) for r in far_rows], axis=0
        )
        right_low = jnp.concatenate(
            [jnp.concatenate([far_low[e] for e in r], axis=1) for r in far_rows], axis=0
        )
        both = jnp.dot(x_ref[row], right_high, preferred_element_type=jnp.float32)
        rest = jnp.dot(x_ref[row, 0:width, :], right_low, preferred_element_type=jnp.float32)
        product = both[0:width] + (both[width:] + rest)
        tall = term_ref[row // SUB, :, i % SUB : i % SUB + 1] * scale
        scores = []
        for l in range(slots):
            cost = tall + column_scr[pl.ds(targets[l], 1), :] - coef * product[:, l * width : (l + 1) * width]
            out_ref[i, 0, l] = cost
            select_ref[pl.ds(row * slots + l, 1), :] = jnp.full((1, width), targets[l], jnp.int32)
            scaled = cost * -to_log2
            work_ref[row, l] = scaled
            turned = scaled.T
            tall_ref[row, l] = turned
            scores.append(turned)
        row_pass(scores, row, peak_scr, sum_scr)

    @pl.when(g == pl.num_programs(0) - 1)
    def _():
        part_ref[...] = peak_scr[...] + jnp.log2(sum_scr[...])


def row_pass(scores, row, peak_scr, sum_scr):
    peak = jnp.max(functools.reduce(jnp.maximum, scores), axis=0, keepdims=True)
    total = functools.reduce(jnp.add, [jnp.exp2(s - peak) for s in scores])
    peak_scr[pl.ds(row, 1), :] = peak
    sum_scr[pl.ds(row, 1), :] = jnp.sum(total, axis=0, keepdims=True)


def column_kernel(col_devices, work_ref, select_ref, log_mass_ref, *refs):
    parts = refs[:col_devices]
    out_ref, potential_ref, potential_scr, peak_scr, sum_scr = refs[col_devices:]
    rows, slots, width, _ = work_ref.shape
    together = math.gcd(rows, 8)
    scaled = log_mass_ref[...] - log_sum([p[...] for p in parts])
    potential_scr[...] = scaled
    potential_ref[...] = scaled * from_log2

    for first in range(0, rows, together):
        tall = potential_scr[first : first + together, :].T
        for i in range(together):
            for l in range(slots):
                score = tall[:, i : i + 1] + work_ref[first + i, l]
                peak = jnp.max(score, axis=0, keepdims=True)
                total = jnp.sum(jnp.exp2(score - peak), axis=0, keepdims=True)
                place = (first + i) * slots + l
                peak_scr[place : place + 1, :] = peak
                sum_scr[place : place + 1, :] = total
    select = select_ref[...]
    peaks = peak_scr[...]
    sums = sum_scr[...]
    for t in range(out_ref.shape[0]):
        chosen = select == t
        peak = jnp.max(jnp.where(chosen, peaks, very_low), axis=0, keepdims=True)
        shifted = jnp.where(chosen, sums * jnp.exp2(jnp.minimum(peaks - peak, 0.0)), 0.0)
        total = jnp.sum(shifted, axis=0, keepdims=True)
        some = total > 0.0
        out_ref[t : t + 1, :] = jnp.where(
            some, peak + jnp.log2(jnp.where(some, total, 1.0)), very_low
        )


def row_kernel(slot_ref, tall_ref, log_mass_ref, *refs):
    parts, (out_ref, wide_scr, peak_scr, sum_scr) = refs[:-4], refs[-4:]
    rows, slots, width, _ = tall_ref.shape
    potential = (log_mass_ref[...] - log_sum([p[...] for p in parts])).T
    for t in range(wide_scr.shape[0]):
        wide_scr[t] = jnp.broadcast_to(potential[:, t : t + 1], (width, width))

    for row in range(rows):
        scores = [wide_scr[slot_ref[l, row]] + tall_ref[row, l] for l in range(slots)]
        row_pass(scores, row, peak_scr, sum_scr)
    out_ref[...] = peak_scr[...] + jnp.log2(sum_scr[...])


def join_kernel(first_ref, second_ref, out_ref):
    out_ref[...] = log_sum([first_ref[...], second_ref[...]])


def last_kernel(row_axis, log_mass_ref, *refs):
    parts, out_ref, scr = refs[:-2], refs[-2], refs[-1]
    here = out_ref.shape[0]
    scr[...] = (log_mass_ref[...] - log_sum([p[...] for p in parts])) * from_log2
    out_ref[...] = scr[pl.ds(lax.axis_index(row_axis) * here, here), :]


def per_device(
    coupling,
    coupling_index,
    near_cost,
    near_index,
    source_weights,
    target_cost,
    target_index,
    target_weights,
):
    rows_here = coupling.shape[0]
    slots = coupling.shape[2]
    width = coupling.shape[3]
    near_count = near_cost.shape[1]
    group_blocks = target_index.shape[1]
    link_count = target_index.shape[2]
    target_here = target_cost.shape[1]
    row_devices = lax.axis_size("rows")
    col_devices = lax.axis_size("cols")
    source_count = rows_here * row_devices * width
    target_count = group_blocks * width * col_devices
    f32 = jnp.float32
    half = row_devices // 2
    arrived = {0: target_cost}
    for mask in range(1, half + 1):
        arrived[mask] = send(target_cost, "rows", mask)

    near_t = in_hbm(near_index.T)
    slot_t = in_hbm(coupling_index[:, 0, :].T)
    link_t = in_hbm(jnp.transpose(target_index, (2, 0, 1)))
    mass = in_hbm(source_weights.reshape(rows_here, width))
    small = pltpu.CompilerParams(vmem_limit_bytes=4 * mib)

    pack_rows = 1 + target_here
    devices = row_devices * col_devices
    pack = pl.pallas_call(
        functools.partial(pack_kernel, devices),
        in_specs=[VMEM, VMEM],
        out_shape=jax.ShapeDtypeStruct((devices * pack_rows, width), f32),
        compiler_params=small,
        name="pack",
    )(mass, in_hbm(target_weights.reshape(target_here, width)))
    packs = exchange(pack, ("rows", "cols"))

    direct = list(range(1, half + 1))
    passed = pl.pallas_call(
        relay_kernel,
        in_specs=[ANY] * half,
        out_specs=[ANY] * half,
        out_shape=[jax.ShapeDtypeStruct(target_cost.shape, f32)] * half,
        input_output_aliases={e: e for e in range(half)},
        compiler_params=small,
        cost_estimate=pl.CostEstimate(flops=10**11, bytes_accessed=256 * mib, transcendentals=0),
        name="relay",
    )(*[arrived[mask] for mask in direct])
    arrived.update(zip(direct, passed))
    for mask in range(half + 1, row_devices):
        arrived[mask] = send(arrived[half], "rows", mask - half)
    cost_parts = [arrived[s] for s in range(row_devices)]

    wide = near_count * slots * width
    groups = rows_here // SUB
    step_rows = 2 * SUB if groups % 2 == 0 else SUB
    x, term = pl.pallas_call(
        near_kernel,
        grid=(rows_here // step_rows,),
        in_specs=[
            SMEM,
            pl.BlockSpec((step_rows, near_count, width, width), lambda g: (g, 0, 0, 0)),
            pl.BlockSpec((step_rows, 1, slots, width, width), lambda g: (g, 0, 0, 0, 0)),
            whole((rows_here, width)),
            ANY,
        ],
        out_specs=[VMEM, VMEM],
        out_shape=[
            pltpu.VMEM((rows_here, 2 * width, wide), jnp.bfloat16),
            pltpu.VMEM((groups, width, SUB), f32),
        ],
        scratch_shapes=[pltpu.VMEM((step_rows, 3 * width, slots * width), jnp.bfloat16)],
        compiler_params=pltpu.CompilerParams(vmem_limit_bytes=12 * mib),
        cost_estimate=pl.CostEstimate(
            flops=6 * rows_here * wide * width * width,
            bytes_accessed=4 * rows_here * width * (near_count + slots) * width,
            transcendentals=0,
        ),
        name="near_product",
    )(near_t, in_hbm(near_cost), in_hbm(coupling), mass, packs)

    far_bytes = group_blocks * link_count * width * width * 4
    steps = rows_here // step_rows
    cost_block = pl.BlockSpec((step_rows, 1, slots, width, width), lambda g: (g, 0, 0, 0, 0))
    work_shape = pltpu.VMEM((rows_here, slots, width, width), f32)
    cost_blocks, work, tall, row_part, log_source, log_target, select = pl.pallas_call(
        functools.partial(
            far_kernel,
            (row_devices, col_devices, target_here, source_count, target_count, group_blocks, link_count),
            "rows",
            "cols",
        ),
        grid=(steps,),
        in_specs=[SMEM, SMEM, SMEM, VMEM, VMEM, whole((rows_here, width))]
        + [VMEM] * row_devices
        + [whole(packs.shape)],
        out_specs=[
            cost_block,
            VMEM,
            VMEM,
            whole((rows_here, width)),
            whole((rows_here, width)),
            whole((group_blocks, width)),
            whole((rows_here * slots, width)),
        ],
        out_shape=[
            jax.ShapeDtypeStruct(coupling.shape, f32),
            work_shape,
            work_shape,
            jax.ShapeDtypeStruct((rows_here, width), f32),
            jax.ShapeDtypeStruct((rows_here, width), f32),
            jax.ShapeDtypeStruct((group_blocks, width), f32),
            jax.ShapeDtypeStruct((rows_here * slots, width), jnp.int32),
        ],
        scratch_shapes=[
            pltpu.VMEM((group_blocks * link_count + 1, width, width), jnp.bfloat16),
            pltpu.VMEM((group_blocks * link_count + 1, width, width), jnp.bfloat16),
            pltpu.SMEM((group_blocks * group_blocks,), jnp.int32),
            pltpu.VMEM((group_blocks, width), f32),
            pltpu.VMEM((1, width), f32),
            pltpu.VMEM((rows_here, width), f32),
            pltpu.VMEM((rows_here, width), f32),
        ],
        compiler_params=pltpu.CompilerParams(vmem_limit_bytes=12 * mib + 2 * far_bytes),
        name="far_product",
    )(near_t, slot_t, link_t, in_vmem(x), in_vmem(term), mass, *cost_parts, packs)

    pass_params = pltpu.CompilerParams(vmem_limit_bytes=12 * mib)

    def column_step(row_parts):
        return pl.pallas_call(
            functools.partial(column_kernel, col_devices),
            in_specs=[VMEM] * (3 + col_devices),
            out_specs=[VMEM, VMEM],
            out_shape=[
                jax.ShapeDtypeStruct((group_blocks, width), f32),
                jax.ShapeDtypeStruct((rows_here, width), f32),
            ],
            scratch_shapes=[
                pltpu.VMEM((rows_here, width), f32),
                pltpu.VMEM((rows_here * slots, width), f32),
                pltpu.VMEM((rows_here * slots, width), f32),
            ],
            compiler_params=pass_params,
            name="column_pass",
        )(in_vmem(work), select, log_source, *row_parts)

    def from_rows(part):
        part = pl.pallas_call(
            join_kernel,
            out_shape=jax.ShapeDtypeStruct(part.shape, f32),
            compiler_params=small,
            name="join",
        )(part, send(part, "rows", 1))
        return [part] + [send(part, "rows", mask) for mask in range(2, row_devices, 2)]

    def row_step(column_parts):
        return pl.pallas_call(
            row_kernel,
            in_specs=[SMEM, VMEM, VMEM] + [VMEM] * len(column_parts),
            out_specs=VMEM,
            out_shape=jax.ShapeDtypeStruct((rows_here, width), f32),
            scratch_shapes=[
                pltpu.VMEM((group_blocks, width, width), f32),
                pltpu.VMEM((rows_here, width), f32),
                pltpu.VMEM((rows_here, width), f32),
            ],
            compiler_params=pass_params,
            name="row_pass",
        )(slot_t, in_vmem(tall), log_target, *column_parts)

    for step in range(ITERS):
        column_part, source_potential = column_step(from_all(row_part, "cols"))
        column_parts = from_rows(column_part)
        if step < ITERS - 1:
            row_part = row_step(column_parts)
    own_target = pl.pallas_call(
        functools.partial(last_kernel, "rows"),
        out_shape=jax.ShapeDtypeStruct((target_here, width), f32),
        scratch_shapes=[pltpu.VMEM((group_blocks, width), f32)],
        compiler_params=small,
        name="last_potential",
    )(log_target, *column_parts)
    return (
        cost_blocks,
        source_potential.reshape(rows_here * width),
        own_target.reshape(1, target_here * width),
    )


def solution(mesh):
    placed = (
        P("rows", "cols", None, None, None),
        P("rows", "cols", None),
        P("rows", None, None, None),
        P("rows", None),
        P("rows"),
        P("cols", "rows", None, None, None),
        P("cols", None, None),
        P("cols", "rows"),
    )
    return jax.shard_map(
        per_device,
        mesh=mesh,
        in_specs=placed,
        out_specs=(P("rows", "cols", None, None, None), P("rows"), P("cols", "rows")),
        check_vma=False,
    )
```

```python
import functools
import math

import jax
import jax.numpy as jnp
from jax import lax
from jax.experimental import pallas as pl
from jax.experimental.pallas import tpu as pltpu
from jax.sharding import PartitionSpec as P

ITERS = 3
SUB = 4

entropy = 0.01
to_log2 = math.log2(math.e) / entropy
from_log2 = entropy * math.log(2.0)
very_low = -1e30
mib = 1024 * 1024

SMEM = pl.BlockSpec(memory_space=pltpu.SMEM)
VMEM = pl.BlockSpec(memory_space=pltpu.VMEM)
ANY = pl.BlockSpec(memory_space=pl.ANY)


def in_hbm(x):
    return pltpu.with_memory_space_constraint(x, pltpu.HBM)


def in_vmem(x):
    return pltpu.with_memory_space_constraint(x, pltpu.VMEM)


def whole(shape):
    return pl.BlockSpec(shape, lambda *_: (0,) * len(shape))


def split(x):
    high = x.astype(jnp.bfloat16)
    return high, (x - high.astype(jnp.float32)).astype(jnp.bfloat16)


def tree(parts, op):
    while len(parts) > 1:
        half = len(parts) // 2
        parts = [op(parts[s], parts[s + half]) for s in range(half)]
    return parts[0]


def log_sum(parts):
    peak = tree(parts, jnp.maximum)
    return peak + jnp.log2(tree([jnp.exp2(p - peak) for p in parts], jnp.add))


def parts_of(ref, devices):
    rows = ref.shape[0] // devices
    return [ref[d * rows : (d + 1) * rows, :] for d in range(devices)]


def put_copies(ref, devices, value):
    rows = value.shape[0]
    for d in range(devices):
        ref[d * rows : (d + 1) * rows, :] = value


def send(x, axis, mask):
    size = lax.axis_size(axis)
    return lax.ppermute(x, axis, [(d, d ^ mask) for d in range(size)])


def from_all(x, axis):
    return [x] + [send(x, axis, s) for s in range(1, lax.axis_size(axis))]


def exchange(copies, axis):
    return lax.all_to_all(copies, axis, 0, 0, tiled=True)


def pack_kernel(devices, source_ref, target_ref, out_ref):
    rows = out_ref.shape[0] // devices
    total = jnp.sum(source_ref[...].astype(jnp.float32), axis=(0, 1), keepdims=True)
    target = target_ref[...].astype(jnp.float32)
    for d in range(devices):
        out_ref[d * rows : d * rows + 1, :] = jnp.broadcast_to(total, (1, out_ref.shape[1]))
        out_ref[d * rows + 1 : d * rows + 1 + target.shape[0], :] = target


def near_kernel(
    near_index_ref, cost_hbm, plan_hbm, mass_ref, totals_ref, x_ref, term_ref, cost_scr, plan_in, plan_scr, sems
):
    all_rows, near_count, width, _ = cost_hbm.shape
    slots = plan_hbm.shape[2]
    wide = slots * width
    groups = all_rows // SUB

    def copies(group):
        rows = pl.ds(group * SUB, SUB)
        return (
            pltpu.make_async_copy(plan_hbm.at[rows], plan_in.at[rows], sems.at[0, group]),
            pltpu.make_async_copy(cost_hbm.at[rows], cost_scr.at[rows], sems.at[1, group]),
        )

    for group in range(groups):
        for copy in copies(group):
            copy.start()

    together = 2 if groups % 2 == 0 else 1
    lanes = lax.broadcasted_iota(jnp.int32, (width, SUB), 1)

    def some_groups(step, _):
        for here in range(together):
            for copy in copies(step * together + here):
                copy.wait()
        first = step * (together * SUB)
        for a in range(together * SUB):
            plan = jnp.concatenate([plan_in[first + a, 0, q] for q in range(slots)], axis=1)
            high, low = split(plan)
            plan_scr[a, 0:width, :] = high
            plan_scr[a, width : 2 * width, :] = low
            plan_scr[a, 2 * width : 3 * width, :] = high
        for here in range(together):
            terms = jnp.zeros((width, SUB), jnp.float32)
            for i in range(here * SUB, (here + 1) * SUB):
                acc = None
                for k in range(near_count):
                    a = here * SUB + (near_index_ref[k, first + i] & (SUB - 1))
                    cost = cost_scr[first + i, k]
                    high, low = split(cost)
                    x = jnp.dot(
                        jnp.concatenate([high, high, low], axis=1),
                        plan_scr[a],
                        preferred_element_type=jnp.float32,
                    )
                    x_high, x_low = split(x)
                    x_ref[first + i, 0:width, k * wide : (k + 1) * wide] = x_high
                    x_ref[first + i, width : 2 * width, k * wide : (k + 1) * wide] = x_low
                    weighted = cost * cost * mass_ref[pl.ds(first + a, 1), :].astype(jnp.float32)
                    acc = weighted if acc is None else acc + weighted
                terms = jnp.where(lanes == i % SUB, jnp.sum(acc, axis=1, keepdims=True), terms)
            term_ref[step * together + here] = terms
        return 0

    lax.fori_loop(0, groups // together, some_groups, 0)


def relay_kernel(*refs):
    pass


def far_kernel(counts, row_axis, col_axis, *refs):
    row_devices, col_devices, target_here, source_count, target_count, group_blocks, link_count = counts
    near_index_ref, slot_ref, link_ref, x_ref, term_ref, mass_ref = refs[:6]
    cost_parts = refs[6 : 6 + row_devices]
    pack_ref, out_ref, work_ref, tall_ref, part_ref, log_source_ref, log_target_ref, select_ref = refs[
        6 + row_devices : 14 + row_devices
    ]
    far_high, far_low, table, column_scr, scale_scr, peak_scr, sum_scr = refs[14 + row_devices :]
    g = pl.program_id(0)
    near_count = near_index_ref.shape[0]
    slots = slot_ref.shape[0]
    rows = out_ref.shape[0]
    width = out_ref.shape[3]
    zero_block = group_blocks * link_count

    @pl.when(g == 0)
    def _():
        me = lax.axis_index(row_axis)
        col = lax.axis_index(col_axis)
        far_high[zero_block] = jnp.zeros((width, width), jnp.bfloat16)
        far_low[zero_block] = jnp.zeros((width, width), jnp.bfloat16)

        def clear(e, _):
            table[e] = zero_block
            return 0

        lax.fori_loop(0, group_blocks * group_blocks, clear, 0)

        def mark(j, _):
            for m in range(link_count):
                table[j * group_blocks + link_ref[m, 0, j]] = j * link_count + m
            return 0

        lax.fori_loop(0, group_blocks, mark, 0)
        pack_rows = pack_ref.shape[0] // (row_devices * col_devices)
        total_source = functools.reduce(
            jnp.add,
            [pack_ref[r * col_devices * pack_rows : r * col_devices * pack_rows + 1, :] for r in range(row_devices)],
        )
        targets = functools.reduce(
            jnp.add,
            [
                pack_ref[d * pack_rows + 1 + h : d * pack_rows + 2 + h, :]
                for d in range(row_devices * col_devices)
                for h in range(target_here)
            ],
        )
        total_target = jnp.sum(targets, axis=1, keepdims=True)
        log_source_ref[...] = jnp.log2(source_count * mass_ref[...].astype(jnp.float32) / total_source)
        scale_scr[...] = source_count / (total_source * (near_count * width))
        column_scr[...] = jnp.zeros_like(column_scr)
        for s in range(row_devices):
            for h in range(target_here):
                j = (me ^ s) * target_here + h
                place = ((me ^ s) * col_devices + col) * pack_rows + 1 + h
                mass = target_count * pack_ref[pl.ds(place, 1), :] / total_target
                log_target_ref[pl.ds(j, 1), :] = jnp.log2(mass)
                tall = jnp.broadcast_to(mass, (width, width)).T
                for m in range(link_count):
                    block = cost_parts[s][0, h, m]
                    high, low = split(block)
                    far_high[j * link_count + m] = high
                    far_low[j * link_count + m] = low
                    spread = jnp.sum(tall * (block * block), axis=0, keepdims=True)
                    t = link_ref[m, 0, j]
                    column_scr[pl.ds(t, 1), :] += spread * (1.0 / (link_count * width))

    group_devices = target_count // (group_blocks * width)
    coef = 2.0 * (1.0 / (near_count * width)) * (1.0 / (slots * group_devices * width))
    scale = scale_scr[0:1, 0:1]
    for i in range(rows):
        row = g * rows + i
        group = row - lax.rem(row, SUB)
        targets = [slot_ref[l, row] for l in range(slots)]
        far_rows = []
        for k in range(near_count):
            a = group + (near_index_ref[k, row] & (SUB - 1))
            for q in range(slots):
                j = slot_ref[q, a]
                far_rows.append([table[j * group_blocks + t] for t in targets])
        right_high = jnp.concatenate(
            [jnp.concatenate([far_high[e] for e in r], axis=1) for r in far_rows], axis=0
        )
        right_low = jnp.concatenate(
            [jnp.concatenate([far_low[e] for e in r], axis=1) for r in far_rows], axis=0
        )
        both = jnp.dot(x_ref[row], right_high, preferred_element_type=jnp.float32)
        rest = jnp.dot(x_ref[row, 0:width, :], right_low, preferred_element_type=jnp.float32)
        product = both[0:width] + (both[width:] + rest)
        tall = term_ref[row // SUB, :, i % SUB : i % SUB + 1] * scale
        scores = []
        for l in range(slots):
            cost = tall + column_scr[pl.ds(targets[l], 1), :] - coef * product[:, l * width : (l + 1) * width]
            out_ref[i, 0, l] = cost
            select_ref[pl.ds(row * slots + l, 1), :] = jnp.full((1, width), targets[l], jnp.int32)
            scaled = cost * -to_log2
            work_ref[row, l] = scaled
            turned = scaled.T
            tall_ref[row, l] = turned
            scores.append(turned)
        row_pass(scores, row, peak_scr, sum_scr)

    @pl.when(g == pl.num_programs(0) - 1)
    def _():
        part_ref[...] = peak_scr[...] + jnp.log2(sum_scr[...])


def row_pass(scores, row, peak_scr, sum_scr):
    peak = jnp.max(functools.reduce(jnp.maximum, scores), axis=0, keepdims=True)
    total = functools.reduce(jnp.add, [jnp.exp2(s - peak) for s in scores])
    peak_scr[pl.ds(row, 1), :] = peak
    sum_scr[pl.ds(row, 1), :] = jnp.sum(total, axis=0, keepdims=True)


def column_kernel(col_devices, copies, work_ref, select_ref, log_mass_ref, *refs):
    parts = refs[:col_devices]
    out_ref, potential_ref, potential_scr, peak_scr, sum_scr = refs[col_devices:]
    rows, slots, width, _ = work_ref.shape
    together = math.gcd(rows, 8)
    scaled = log_mass_ref[...] - log_sum([p[...] for p in parts])
    potential_scr[...] = scaled
    potential_ref[...] = scaled * from_log2

    for first in range(0, rows, together):
        tall = potential_scr[first : first + together, :].T
        for i in range(together):
            for l in range(slots):
                score = tall[:, i : i + 1] + work_ref[first + i, l]
                peak = jnp.max(score, axis=0, keepdims=True)
                total = jnp.sum(jnp.exp2(score - peak), axis=0, keepdims=True)
                place = (first + i) * slots + l
                peak_scr[place : place + 1, :] = peak
                sum_scr[place : place + 1, :] = total
    select = select_ref[...]
    peaks = peak_scr[...]
    sums = sum_scr[...]
    blocks = out_ref.shape[0] // copies
    for t in range(blocks):
        chosen = select == t
        peak = jnp.max(jnp.where(chosen, peaks, very_low), axis=0, keepdims=True)
        shifted = jnp.where(chosen, sums * jnp.exp2(jnp.minimum(peaks - peak, 0.0)), 0.0)
        total = jnp.sum(shifted, axis=0, keepdims=True)
        some = total > 0.0
        out_ref[t : t + 1, :] = jnp.where(
            some, peak + jnp.log2(jnp.where(some, total, 1.0)), very_low
        )
    if copies > 1:
        put_copies(out_ref, copies, out_ref[0:blocks, :])


def row_kernel(
    row_devices, slot_ref, tall_ref, log_mass_ref, parts_ref, out_ref, wide_scr, peak_scr, sum_scr
):
    rows, slots, width, _ = tall_ref.shape
    potential = (log_mass_ref[...] - log_sum(parts_of(parts_ref, row_devices))).T
    for t in range(wide_scr.shape[0]):
        wide_scr[t] = jnp.broadcast_to(potential[:, t : t + 1], (width, width))

    for row in range(rows):
        scores = [wide_scr[slot_ref[l, row]] + tall_ref[row, l] for l in range(slots)]
        row_pass(scores, row, peak_scr, sum_scr)
    out_ref[...] = peak_scr[...] + jnp.log2(sum_scr[...])


def last_kernel(row_devices, row_axis, log_mass_ref, parts_ref, out_ref):
    here = out_ref.shape[0]
    start = lax.axis_index(row_axis) * here
    log_mass = log_mass_ref[pl.ds(start, here), :]
    out_ref[...] = (log_mass - log_sum(parts_of(parts_ref, row_devices))) * from_log2


def per_device(
    coupling,
    coupling_index,
    near_cost,
    near_index,
    source_weights,
    target_cost,
    target_index,
    target_weights,
):
    rows_here = coupling.shape[0]
    slots = coupling.shape[2]
    width = coupling.shape[3]
    near_count = near_cost.shape[1]
    group_blocks = target_index.shape[1]
    link_count = target_index.shape[2]
    target_here = target_cost.shape[1]
    row_devices = lax.axis_size("rows")
    col_devices = lax.axis_size("cols")
    source_count = rows_here * row_devices * width
    target_count = group_blocks * width * col_devices
    f32 = jnp.float32
    half = row_devices // 2
    arrived = {0: target_cost}
    for mask in range(1, half + 1):
        arrived[mask] = send(target_cost, "rows", mask)

    near_t = in_hbm(near_index.T)
    slot_t = in_hbm(coupling_index[:, 0, :].T)
    link_t = in_hbm(jnp.transpose(target_index, (2, 0, 1)))
    mass = in_hbm(source_weights.reshape(rows_here, width))
    small = pltpu.CompilerParams(vmem_limit_bytes=4 * mib)

    pack_rows = 1 + target_here
    devices = row_devices * col_devices
    pack = pl.pallas_call(
        functools.partial(pack_kernel, devices),
        in_specs=[VMEM, VMEM],
        out_shape=jax.ShapeDtypeStruct((devices * pack_rows, width), f32),
        compiler_params=small,
        name="pack",
    )(mass, in_hbm(target_weights.reshape(target_here, width)))
    packs = exchange(pack, ("rows", "cols"))

    direct = list(range(1, half + 1))
    passed = pl.pallas_call(
        relay_kernel,
        in_specs=[ANY] * half,
        out_specs=[ANY] * half,
        out_shape=[jax.ShapeDtypeStruct(target_cost.shape, f32)] * half,
        input_output_aliases={e: e for e in range(half)},
        compiler_params=small,
        cost_estimate=pl.CostEstimate(flops=10**11, bytes_accessed=256 * mib, transcendentals=0),
        name="relay",
    )(*[arrived[mask] for mask in direct])
    arrived.update(zip(direct, passed))
    for mask in range(half + 1, row_devices):
        arrived[mask] = send(arrived[half], "rows", mask - half)
    cost_parts = [arrived[s] for s in range(row_devices)]

    wide = near_count * slots * width
    groups = rows_here // SUB
    step_rows = 2 * SUB if groups % 2 == 0 else SUB
    x, term = pl.pallas_call(
        near_kernel,
        in_specs=[SMEM, ANY, ANY, VMEM, ANY],
        out_specs=[VMEM, VMEM],
        out_shape=[
            pltpu.VMEM((rows_here, 2 * width, wide), jnp.bfloat16),
            pltpu.VMEM((groups, width, SUB), f32),
        ],
        scratch_shapes=[
            pltpu.VMEM(near_cost.shape, f32),
            pltpu.VMEM(coupling.shape, f32),
            pltpu.VMEM((step_rows, 3 * width, slots * width), jnp.bfloat16),
            pltpu.SemaphoreType.DMA((2, groups)),
        ],
        compiler_params=pltpu.CompilerParams(vmem_limit_bytes=18 * mib),
        cost_estimate=pl.CostEstimate(
            flops=6 * rows_here * wide * width * width,
            bytes_accessed=4 * rows_here * width * (near_count + slots) * width,
            transcendentals=0,
        ),
        name="near_product",
    )(near_t, in_hbm(near_cost), in_hbm(coupling), mass, packs)

    far_bytes = group_blocks * link_count * width * width * 4
    steps = rows_here // step_rows
    cost_block = pl.BlockSpec((step_rows, 1, slots, width, width), lambda g: (g, 0, 0, 0, 0))
    work_shape = pltpu.VMEM((rows_here, slots, width, width), f32)
    cost_blocks, work, tall, row_part, log_source, log_target, select = pl.pallas_call(
        functools.partial(
            far_kernel,
            (row_devices, col_devices, target_here, source_count, target_count, group_blocks, link_count),
            "rows",
            "cols",
        ),
        grid=(steps,),
        in_specs=[SMEM, SMEM, SMEM, VMEM, VMEM, whole((rows_here, width))]
        + [VMEM] * row_devices
        + [whole(packs.shape)],
        out_specs=[
            cost_block,
            VMEM,
            VMEM,
            whole((rows_here, width)),
            whole((rows_here, width)),
            whole((group_blocks, width)),
            whole((rows_here * slots, width)),
        ],
        out_shape=[
            jax.ShapeDtypeStruct(coupling.shape, f32),
            work_shape,
            work_shape,
            jax.ShapeDtypeStruct((rows_here, width), f32),
            jax.ShapeDtypeStruct((rows_here, width), f32),
            jax.ShapeDtypeStruct((group_blocks, width), f32),
            jax.ShapeDtypeStruct((rows_here * slots, width), jnp.int32),
        ],
        scratch_shapes=[
            pltpu.VMEM((group_blocks * link_count + 1, width, width), jnp.bfloat16),
            pltpu.VMEM((group_blocks * link_count + 1, width, width), jnp.bfloat16),
            pltpu.SMEM((group_blocks * group_blocks,), jnp.int32),
            pltpu.VMEM((group_blocks, width), f32),
            pltpu.VMEM((1, width), f32),
            pltpu.VMEM((rows_here, width), f32),
            pltpu.VMEM((rows_here, width), f32),
        ],
        compiler_params=pltpu.CompilerParams(vmem_limit_bytes=12 * mib + 2 * far_bytes),
        name="far_product",
    )(near_t, slot_t, link_t, in_vmem(x), in_vmem(term), mass, *cost_parts, packs)

    pass_params = pltpu.CompilerParams(vmem_limit_bytes=12 * mib)

    def column_step(row_parts, copies):
        return pl.pallas_call(
            functools.partial(column_kernel, col_devices, copies),
            in_specs=[VMEM] * (3 + col_devices),
            out_specs=[VMEM, VMEM],
            out_shape=[
                jax.ShapeDtypeStruct((copies * group_blocks, width), f32),
                jax.ShapeDtypeStruct((rows_here, width), f32),
            ],
            scratch_shapes=[
                pltpu.VMEM((rows_here, width), f32),
                pltpu.VMEM((rows_here * slots, width), f32),
                pltpu.VMEM((rows_here * slots, width), f32),
            ],
            compiler_params=pass_params,
            name="column_pass",
        )(in_vmem(work), select, log_source, *row_parts)

    def row_step(column_parts):
        return pl.pallas_call(
            functools.partial(row_kernel, row_devices),
            in_specs=[SMEM, VMEM, VMEM, VMEM],
            out_specs=VMEM,
            out_shape=jax.ShapeDtypeStruct((rows_here, width), f32),
            scratch_shapes=[
                pltpu.VMEM((group_blocks, width, width), f32),
                pltpu.VMEM((rows_here, width), f32),
                pltpu.VMEM((rows_here, width), f32),
            ],
            compiler_params=pass_params,
            name="row_pass",
        )(slot_t, in_vmem(tall), log_target, column_parts)

    for step in range(ITERS):
        last = step == ITERS - 1
        column_part, source_potential = column_step(
            from_all(row_part, "cols"), 1 if last else row_devices
        )
        column_parts = exchange(column_part, "rows")
        if not last:
            row_part = row_step(column_parts)
    own_target = pl.pallas_call(
        functools.partial(last_kernel, row_devices, "rows"),
        out_shape=jax.ShapeDtypeStruct((target_here, width), f32),
        compiler_params=small,
        name="last_potential",
    )(log_target, column_parts)
    return (
        cost_blocks,
        source_potential.reshape(rows_here * width),
        own_target.reshape(1, target_here * width),
    )


def solution(mesh):
    placed = (
        P("rows", "cols", None, None, None),
        P("rows", "cols", None),
        P("rows", None, None, None),
        P("rows", None),
        P("rows"),
        P("cols", "rows", None, None, None),
        P("cols", None, None),
        P("cols", "rows"),
    )
    return jax.shard_map(
        per_device,
        mesh=mesh,
        in_specs=placed,
        out_specs=(P("rows", "cols", None, None, None), P("rows"), P("cols", "rows")),
        check_vma=False,
    )
```

```python
import functools
import math

import jax
import jax.numpy as jnp
from jax import lax
from jax.experimental import pallas as pl
from jax.experimental.pallas import tpu as pltpu
from jax.sharding import PartitionSpec as P

ITERS = 3
SUB = 4

entropy = 0.01
to_log2 = math.log2(math.e) / entropy
from_log2 = entropy * math.log(2.0)
very_low = -1e30
mib = 1024 * 1024

SMEM = pl.BlockSpec(memory_space=pltpu.SMEM)
VMEM = pl.BlockSpec(memory_space=pltpu.VMEM)
ANY = pl.BlockSpec(memory_space=pl.ANY)


def in_hbm(x):
    return pltpu.with_memory_space_constraint(x, pltpu.HBM)


def in_vmem(x):
    return pltpu.with_memory_space_constraint(x, pltpu.VMEM)


def whole(shape):
    return pl.BlockSpec(shape, lambda *_: (0,) * len(shape))


def split(x):
    high = x.astype(jnp.bfloat16)
    return high, (x - high.astype(jnp.float32)).astype(jnp.bfloat16)


def tree(parts, op):
    while len(parts) > 1:
        half = len(parts) // 2
        parts = [op(parts[s], parts[s + half]) for s in range(half)]
    return parts[0]


def log_sum(parts):
    peak = tree(parts, jnp.maximum)
    return peak + jnp.log2(tree([jnp.exp2(p - peak) for p in parts], jnp.add))


def parts_of(ref, devices):
    rows = ref.shape[0] // devices
    return [ref[d * rows : (d + 1) * rows, :] for d in range(devices)]


def put_copies(ref, devices, value):
    rows = value.shape[0]
    for d in range(devices):
        ref[d * rows : (d + 1) * rows, :] = value


def send(x, axis, mask):
    size = lax.axis_size(axis)
    return lax.ppermute(x, axis, [(d, d ^ mask) for d in range(size)])


def join_kernel(first_ref, second_ref, out_ref):
    out_ref[...] = log_sum([first_ref[...], second_ref[...]])


def last_pair(part, axis):
    mask = 1
    while 2 * mask < lax.axis_size(axis):
        part = pl.pallas_call(
            join_kernel,
            out_shape=jax.ShapeDtypeStruct(part.shape, jnp.float32),
            compiler_params=pltpu.CompilerParams(vmem_limit_bytes=4 * mib),
            name="join",
        )(part, send(part, axis, mask))
        mask *= 2
    return [part, send(part, axis, mask)]


def exchange(copies, axis):
    return lax.all_to_all(copies, axis, 0, 0, tiled=True)


def pack_kernel(devices, source_ref, target_ref, out_ref):
    rows = out_ref.shape[0] // devices
    total = jnp.sum(source_ref[...].astype(jnp.float32), axis=(0, 1), keepdims=True)
    target = target_ref[...].astype(jnp.float32)
    for d in range(devices):
        out_ref[d * rows : d * rows + 1, :] = jnp.broadcast_to(total, (1, out_ref.shape[1]))
        out_ref[d * rows + 1 : d * rows + 1 + target.shape[0], :] = target


def near_kernel(near_index_ref, cost_ref, plan_ref, mass_ref, totals_ref, x_ref, term_ref, plan_scr):
    rows = cost_ref.shape[0]
    first = pl.program_id(0) * rows
    near_count = cost_ref.shape[1]
    width = cost_ref.shape[2]
    slots = plan_ref.shape[2]
    wide = slots * width
    for a in range(rows):
        plan = jnp.concatenate([plan_ref[a, 0, q] for q in range(slots)], axis=1)
        high, low = split(plan)
        plan_scr[a, 0:width, :] = high
        plan_scr[a, width : 2 * width, :] = low
        plan_scr[a, 2 * width : 3 * width, :] = high
    lanes = lax.broadcasted_iota(jnp.int32, (width, SUB), 1)
    for group in range(rows // SUB):
        terms = jnp.zeros((width, SUB), jnp.float32)
        for i in range(group * SUB, (group + 1) * SUB):
            acc = None
            for k in range(near_count):
                a = group * SUB + (near_index_ref[k, first + i] & (SUB - 1))
                cost = cost_ref[i, k]
                high, low = split(cost)
                x = jnp.dot(
                    jnp.concatenate([high, high, low], axis=1),
                    plan_scr[a],
                    preferred_element_type=jnp.float32,
                )
                x_high, x_low = split(x)
                x_ref[first + i, 0:width, k * wide : (k + 1) * wide] = x_high
                x_ref[first + i, width : 2 * width, k * wide : (k + 1) * wide] = x_low
                weighted = cost * cost * mass_ref[pl.ds(first + a, 1), :].astype(jnp.float32)
                acc = weighted if acc is None else acc + weighted
            terms = jnp.where(lanes == i % SUB, jnp.sum(acc, axis=1, keepdims=True), terms)
        term_ref[first // SUB + group] = terms


def relay_kernel(*refs):
    pass


def far_kernel(counts, row_axis, col_axis, *refs):
    row_devices, col_devices, target_here, source_count, target_count, group_blocks, link_count = counts
    near_index_ref, slot_ref, link_ref, x_ref, term_ref, mass_ref = refs[:6]
    cost_parts = refs[6 : 6 + row_devices]
    pack_ref, out_ref, work_ref, tall_ref, part_ref, log_source_ref, log_target_ref, select_ref = refs[
        6 + row_devices : 14 + row_devices
    ]
    far_high, far_low, table, column_scr, scale_scr, peak_scr, sum_scr = refs[14 + row_devices :]
    g = pl.program_id(0)
    near_count = near_index_ref.shape[0]
    slots = slot_ref.shape[0]
    rows = out_ref.shape[0]
    width = out_ref.shape[3]
    zero_block = group_blocks * link_count

    @pl.when(g == 0)
    def _():
        me = lax.axis_index(row_axis)
        col = lax.axis_index(col_axis)
        far_high[zero_block] = jnp.zeros((width, width), jnp.bfloat16)
        far_low[zero_block] = jnp.zeros((width, width), jnp.bfloat16)

        def clear(e, _):
            table[e] = zero_block
            return 0

        lax.fori_loop(0, group_blocks * group_blocks, clear, 0)

        def mark(j, _):
            for m in range(link_count):
                table[j * group_blocks + link_ref[m, 0, j]] = j * link_count + m
            return 0

        lax.fori_loop(0, group_blocks, mark, 0)
        pack_rows = pack_ref.shape[0] // (row_devices * col_devices)
        total_source = functools.reduce(
            jnp.add,
            [pack_ref[r * col_devices * pack_rows : r * col_devices * pack_rows + 1, :] for r in range(row_devices)],
        )
        targets = functools.reduce(
            jnp.add,
            [
                pack_ref[d * pack_rows + 1 + h : d * pack_rows + 2 + h, :]
                for d in range(row_devices * col_devices)
                for h in range(target_here)
            ],
        )
        total_target = jnp.sum(targets, axis=1, keepdims=True)
        log_source_ref[...] = jnp.log2(source_count * mass_ref[...].astype(jnp.float32) / total_source)
        scale_scr[...] = source_count / (total_source * (near_count * width))
        column_scr[...] = jnp.zeros_like(column_scr)
        for s in range(row_devices):
            for h in range(target_here):
                j = (me ^ s) * target_here + h
                place = ((me ^ s) * col_devices + col) * pack_rows + 1 + h
                mass = target_count * pack_ref[pl.ds(place, 1), :] / total_target
                log_target_ref[pl.ds(j, 1), :] = jnp.log2(mass)
                tall = jnp.broadcast_to(mass, (width, width)).T
                for m in range(link_count):
                    block = cost_parts[s][0, h, m]
                    high, low = split(block)
                    far_high[j * link_count + m] = high
                    far_low[j * link_count + m] = low
                    spread = jnp.sum(tall * (block * block), axis=0, keepdims=True)
                    t = link_ref[m, 0, j]
                    column_scr[pl.ds(t, 1), :] += spread * (1.0 / (link_count * width))

    group_devices = target_count // (group_blocks * width)
    coef = 2.0 * (1.0 / (near_count * width)) * (1.0 / (slots * group_devices * width))
    scale = scale_scr[0:1, 0:1]
    for i in range(rows):
        row = g * rows + i
        group = row - lax.rem(row, SUB)
        targets = [slot_ref[l, row] for l in range(slots)]
        far_rows = []
        for k in range(near_count):
            a = group + (near_index_ref[k, row] & (SUB - 1))
            for q in range(slots):
                j = slot_ref[q, a]
                far_rows.append([table[j * group_blocks + t] for t in targets])
        right_high = jnp.concatenate(
            [jnp.concatenate([far_high[e] for e in r], axis=1) for r in far_rows], axis=0
        )
        right_low = jnp.concatenate(
            [jnp.concatenate([far_low[e] for e in r], axis=1) for r in far_rows], axis=0
        )
        both = jnp.dot(x_ref[row], right_high, preferred_element_type=jnp.float32)
        rest = jnp.dot(x_ref[row, 0:width, :], right_low, preferred_element_type=jnp.float32)
        product = both[0:width] + (both[width:] + rest)
        tall = term_ref[row // SUB, :, i % SUB : i % SUB + 1] * scale
        scores = []
        for l in range(slots):
            cost = tall + column_scr[pl.ds(targets[l], 1), :] - coef * product[:, l * width : (l + 1) * width]
            out_ref[i, 0, l] = cost
            select_ref[pl.ds(row * slots + l, 1), :] = jnp.full((1, width), targets[l], jnp.int32)
            scaled = cost * -to_log2
            work_ref[row, l] = scaled
            turned = scaled.T
            tall_ref[row, l] = turned
            scores.append(turned)
        row_pass(scores, row, peak_scr, sum_scr)

    @pl.when(g == pl.num_programs(0) - 1)
    def _():
        part_ref[...] = peak_scr[...] + jnp.log2(sum_scr[...])


def row_pass(scores, row, peak_scr, sum_scr):
    peak = jnp.max(functools.reduce(jnp.maximum, scores), axis=0, keepdims=True)
    total = functools.reduce(jnp.add, [jnp.exp2(s - peak) for s in scores])
    peak_scr[pl.ds(row, 1), :] = peak
    sum_scr[pl.ds(row, 1), :] = jnp.sum(total, axis=0, keepdims=True)


def column_kernel(copies, work_ref, select_ref, log_mass_ref, *refs):
    parts = refs[:-5]
    out_ref, potential_ref, potential_scr, peak_scr, sum_scr = refs[-5:]
    rows, slots, width, _ = work_ref.shape
    together = math.gcd(rows, 8)
    scaled = log_mass_ref[...] - log_sum([p[...] for p in parts])
    potential_scr[...] = scaled
    potential_ref[...] = scaled * from_log2

    for first in range(0, rows, together):
        tall = potential_scr[first : first + together, :].T
        for i in range(together):
            for l in range(slots):
                score = tall[:, i : i + 1] + work_ref[first + i, l]
                peak = jnp.max(score, axis=0, keepdims=True)
                total = jnp.sum(jnp.exp2(score - peak), axis=0, keepdims=True)
                place = (first + i) * slots + l
                peak_scr[place : place + 1, :] = peak
                sum_scr[place : place + 1, :] = total
    select = select_ref[...]
    peaks = peak_scr[...]
    sums = sum_scr[...]
    blocks = out_ref.shape[0] // copies
    for t in range(blocks):
        chosen = select == t
        peak = jnp.max(jnp.where(chosen, peaks, very_low), axis=0, keepdims=True)
        shifted = jnp.where(chosen, sums * jnp.exp2(jnp.minimum(peaks - peak, 0.0)), 0.0)
        total = jnp.sum(shifted, axis=0, keepdims=True)
        some = total > 0.0
        out_ref[t : t + 1, :] = jnp.where(
            some, peak + jnp.log2(jnp.where(some, total, 1.0)), very_low
        )
    if copies > 1:
        put_copies(out_ref, copies, out_ref[0:blocks, :])


def row_kernel(
    row_devices, slot_ref, tall_ref, log_mass_ref, parts_ref, out_ref, wide_scr, peak_scr, sum_scr
):
    rows, slots, width, _ = tall_ref.shape
    potential = (log_mass_ref[...] - log_sum(parts_of(parts_ref, row_devices))).T
    for t in range(wide_scr.shape[0]):
        wide_scr[t] = jnp.broadcast_to(potential[:, t : t + 1], (width, width))

    for row in range(rows):
        scores = [wide_scr[slot_ref[l, row]] + tall_ref[row, l] for l in range(slots)]
        row_pass(scores, row, peak_scr, sum_scr)
    out_ref[...] = peak_scr[...] + jnp.log2(sum_scr[...])


def last_kernel(row_devices, row_axis, log_mass_ref, parts_ref, out_ref):
    here = out_ref.shape[0]
    start = lax.axis_index(row_axis) * here
    log_mass = log_mass_ref[pl.ds(start, here), :]
    out_ref[...] = (log_mass - log_sum(parts_of(parts_ref, row_devices))) * from_log2


def per_device(
    coupling,
    coupling_index,
    near_cost,
    near_index,
    source_weights,
    target_cost,
    target_index,
    target_weights,
):
    rows_here = coupling.shape[0]
    slots = coupling.shape[2]
    width = coupling.shape[3]
    near_count = near_cost.shape[1]
    group_blocks = target_index.shape[1]
    link_count = target_index.shape[2]
    target_here = target_cost.shape[1]
    row_devices = lax.axis_size("rows")
    col_devices = lax.axis_size("cols")
    source_count = rows_here * row_devices * width
    target_count = group_blocks * width * col_devices
    f32 = jnp.float32
    half = row_devices // 2
    arrived = {0: target_cost}
    for mask in range(1, half + 1):
        arrived[mask] = send(target_cost, "rows", mask)

    near_t = in_hbm(near_index.T)
    slot_t = in_hbm(coupling_index[:, 0, :].T)
    link_t = in_hbm(jnp.transpose(target_index, (2, 0, 1)))
    mass = in_hbm(source_weights.reshape(rows_here, width))
    small = pltpu.CompilerParams(vmem_limit_bytes=4 * mib)

    pack_rows = 1 + target_here
    devices = row_devices * col_devices
    pack = pl.pallas_call(
        functools.partial(pack_kernel, devices),
        in_specs=[VMEM, VMEM],
        out_shape=jax.ShapeDtypeStruct((devices * pack_rows, width), f32),
        compiler_params=small,
        name="pack",
    )(mass, in_hbm(target_weights.reshape(target_here, width)))
    packs = exchange(pack, ("rows", "cols"))

    direct = list(range(1, half + 1))
    passed = pl.pallas_call(
        relay_kernel,
        in_specs=[ANY] * half,
        out_specs=[ANY] * half,
        out_shape=[jax.ShapeDtypeStruct(target_cost.shape, f32)] * half,
        input_output_aliases={e: e for e in range(half)},
        compiler_params=small,
        cost_estimate=pl.CostEstimate(flops=10**11, bytes_accessed=256 * mib, transcendentals=0),
        name="relay",
    )(*[arrived[mask] for mask in direct])
    arrived.update(zip(direct, passed))
    for mask in range(half + 1, row_devices):
        arrived[mask] = send(arrived[half], "rows", mask - half)
    cost_parts = [arrived[s] for s in range(row_devices)]

    wide = near_count * slots * width
    groups = rows_here // SUB
    step_rows = 2 * SUB if groups % 2 == 0 else SUB
    x, term = pl.pallas_call(
        near_kernel,
        grid=(rows_here // step_rows,),
        in_specs=[
            SMEM,
            pl.BlockSpec((step_rows, near_count, width, width), lambda g: (g, 0, 0, 0)),
            pl.BlockSpec((step_rows, 1, slots, width, width), lambda g: (g, 0, 0, 0, 0)),
            whole((rows_here, width)),
            ANY,
        ],
        out_specs=[VMEM, VMEM],
        out_shape=[
            pltpu.VMEM((rows_here, 2 * width, wide), jnp.bfloat16),
            pltpu.VMEM((groups, width, SUB), f32),
        ],
        scratch_shapes=[pltpu.VMEM((step_rows, 3 * width, slots * width), jnp.bfloat16)],
        compiler_params=pltpu.CompilerParams(vmem_limit_bytes=12 * mib),
        cost_estimate=pl.CostEstimate(
            flops=6 * rows_here * wide * width * width,
            bytes_accessed=4 * rows_here * width * (near_count + slots) * width,
            transcendentals=0,
        ),
        name="near_product",
    )(near_t, in_hbm(near_cost), in_hbm(coupling), mass, packs)

    far_bytes = group_blocks * link_count * width * width * 4
    far_rows = 2 * step_rows if rows_here % (2 * step_rows) == 0 else step_rows
    steps = rows_here // far_rows
    cost_block = pl.BlockSpec((far_rows, 1, slots, width, width), lambda g: (g, 0, 0, 0, 0))
    work_shape = pltpu.VMEM((rows_here, slots, width, width), f32)
    cost_blocks, work, tall, row_part, log_source, log_target, select = pl.pallas_call(
        functools.partial(
            far_kernel,
            (row_devices, col_devices, target_here, source_count, target_count, group_blocks, link_count),
            "rows",
            "cols",
        ),
        grid=(steps,),
        in_specs=[SMEM, SMEM, SMEM, VMEM, VMEM, whole((rows_here, width))]
        + [VMEM] * row_devices
        + [whole(packs.shape)],
        out_specs=[
            cost_block,
            VMEM,
            VMEM,
            whole((rows_here, width)),
            whole((rows_here, width)),
            whole((group_blocks, width)),
            whole((rows_here * slots, width)),
        ],
        out_shape=[
            jax.ShapeDtypeStruct(coupling.shape, f32),
            work_shape,
            work_shape,
            jax.ShapeDtypeStruct((rows_here, width), f32),
            jax.ShapeDtypeStruct((rows_here, width), f32),
            jax.ShapeDtypeStruct((group_blocks, width), f32),
            jax.ShapeDtypeStruct((rows_here * slots, width), jnp.int32),
        ],
        scratch_shapes=[
            pltpu.VMEM((group_blocks * link_count + 1, width, width), jnp.bfloat16),
            pltpu.VMEM((group_blocks * link_count + 1, width, width), jnp.bfloat16),
            pltpu.SMEM((group_blocks * group_blocks,), jnp.int32),
            pltpu.VMEM((group_blocks, width), f32),
            pltpu.VMEM((1, width), f32),
            pltpu.VMEM((rows_here, width), f32),
            pltpu.VMEM((rows_here, width), f32),
        ],
        compiler_params=pltpu.CompilerParams(vmem_limit_bytes=12 * mib + 2 * far_bytes),
        name="far_product",
    )(near_t, slot_t, link_t, in_vmem(x), in_vmem(term), mass, *cost_parts, packs)

    pass_params = pltpu.CompilerParams(vmem_limit_bytes=12 * mib)

    def column_step(row_parts, copies):
        return pl.pallas_call(
            functools.partial(column_kernel, copies),
            in_specs=[VMEM] * (3 + len(row_parts)),
            out_specs=[VMEM, VMEM],
            out_shape=[
                jax.ShapeDtypeStruct((copies * group_blocks, width), f32),
                jax.ShapeDtypeStruct((rows_here, width), f32),
            ],
            scratch_shapes=[
                pltpu.VMEM((rows_here, width), f32),
                pltpu.VMEM((rows_here * slots, width), f32),
                pltpu.VMEM((rows_here * slots, width), f32),
            ],
            compiler_params=pass_params,
            name="column_pass",
        )(in_vmem(work), select, log_source, *row_parts)

    def row_step(column_parts):
        return pl.pallas_call(
            functools.partial(row_kernel, row_devices),
            in_specs=[SMEM, VMEM, VMEM, VMEM],
            out_specs=VMEM,
            out_shape=jax.ShapeDtypeStruct((rows_here, width), f32),
            scratch_shapes=[
                pltpu.VMEM((group_blocks, width, width), f32),
                pltpu.VMEM((rows_here, width), f32),
                pltpu.VMEM((rows_here, width), f32),
            ],
            compiler_params=pass_params,
            name="row_pass",
        )(slot_t, in_vmem(tall), log_target, column_parts)

    for step in range(ITERS):
        last = step == ITERS - 1
        column_part, source_potential = column_step(
            last_pair(row_part, "cols"), 1 if last else row_devices
        )
        column_parts = exchange(column_part, "rows")
        if not last:
            row_part = row_step(column_parts)
    own_target = pl.pallas_call(
        functools.partial(last_kernel, row_devices, "rows"),
        out_shape=jax.ShapeDtypeStruct((target_here, width), f32),
        compiler_params=small,
        name="last_potential",
    )(log_target, column_parts)
    return (
        cost_blocks,
        source_potential.reshape(rows_here * width),
        own_target.reshape(1, target_here * width),
    )


def solution(mesh):
    placed = (
        P("rows", "cols", None, None, None),
        P("rows", "cols", None),
        P("rows", None, None, None),
        P("rows", None),
        P("rows"),
        P("cols", "rows", None, None, None),
        P("cols", None, None),
        P("cols", "rows"),
    )
    return jax.shard_map(
        per_device,
        mesh=mesh,
        in_specs=placed,
        out_specs=(P("rows", "cols", None, None, None), P("rows"), P("cols", "rows")),
        check_vma=False,
    )
```

```python
import functools
import math

import jax
import jax.numpy as jnp
from jax import lax
from jax.experimental import pallas as pl
from jax.experimental.pallas import tpu as pltpu
from jax.sharding import PartitionSpec as P

ITERS = 3
SUB = 4

entropy = 0.01
to_log2 = math.log2(math.e) / entropy
from_log2 = entropy * math.log(2.0)
very_low = -1e30
mib = 1024 * 1024

SMEM = pl.BlockSpec(memory_space=pltpu.SMEM)
VMEM = pl.BlockSpec(memory_space=pltpu.VMEM)
ANY = pl.BlockSpec(memory_space=pl.ANY)


def in_hbm(x):
    return pltpu.with_memory_space_constraint(x, pltpu.HBM)


def in_vmem(x):
    return pltpu.with_memory_space_constraint(x, pltpu.VMEM)


def whole(shape):
    return pl.BlockSpec(shape, lambda *_: (0,) * len(shape))


def split(x):
    high = x.astype(jnp.bfloat16)
    return high, (x - high.astype(jnp.float32)).astype(jnp.bfloat16)


def tree(parts, op):
    while len(parts) > 1:
        half = len(parts) // 2
        parts = [op(parts[s], parts[s + half]) for s in range(half)]
    return parts[0]


def log_sum(parts):
    peak = tree(parts, jnp.maximum)
    return peak + jnp.log2(tree([jnp.exp2(p - peak) for p in parts], jnp.add))


def parts_of(ref, devices):
    rows = ref.shape[0] // devices
    return [ref[d * rows : (d + 1) * rows, :] for d in range(devices)]


def put_copies(ref, devices, value):
    rows = value.shape[0]
    for d in range(devices):
        ref[d * rows : (d + 1) * rows, :] = value


def send(x, axis, mask):
    size = lax.axis_size(axis)
    return lax.ppermute(x, axis, [(d, d ^ mask) for d in range(size)])


def from_all(x, axis):
    return [x] + [send(x, axis, s) for s in range(1, lax.axis_size(axis))]


def exchange(copies, axis):
    return lax.all_to_all(copies, axis, 0, 0, tiled=True)


def pack_kernel(devices, source_ref, target_ref, out_ref):
    rows = out_ref.shape[0] // devices
    total = jnp.sum(source_ref[...].astype(jnp.float32), axis=(0, 1), keepdims=True)
    target = target_ref[...].astype(jnp.float32)
    for d in range(devices):
        out_ref[d * rows : d * rows + 1, :] = jnp.broadcast_to(total, (1, out_ref.shape[1]))
        out_ref[d * rows + 1 : d * rows + 1 + target.shape[0], :] = target


def near_kernel(
    near_index_ref, cost_ref, plan_ref, mass_ref, totals_ref, x_ref, term_ref, plan_scr, cost_scr
):
    rows = cost_ref.shape[0]
    first = pl.program_id(0) * rows
    near_count = cost_ref.shape[1]
    width = cost_ref.shape[2]
    slots = plan_ref.shape[2]
    wide = slots * width
    for a in range(rows):
        plan = jnp.concatenate([plan_ref[a, 0, q] for q in range(slots)], axis=1)
        high, low = split(plan)
        plan_scr[a, 0:width, :] = high
        plan_scr[a, width : 2 * width, :] = low
        plan_scr[a, 2 * width : 3 * width, :] = high
    lanes = lax.broadcasted_iota(jnp.int32, (width, SUB), 1)
    for group in range(rows // SUB):
        members = range(group * SUB, (group + 1) * SUB)
        near = [[near_index_ref[k, first + i] & (SUB - 1) for k in range(near_count)] for i in members]
        terms = jnp.zeros((width, SUB), jnp.float32)
        for i in members:
            acc = None
            for k in range(near_count):
                cost = cost_ref[i, k]
                high, low = split(cost)
                cost_scr[i, k, :, 0:width] = high
                cost_scr[i, k, :, width : 2 * width] = high
                cost_scr[i, k, :, 2 * width : 3 * width] = low
                source = first + group * SUB + near[i % SUB][k]
                weighted = cost * cost * mass_ref[pl.ds(source, 1), :].astype(jnp.float32)
                acc = weighted if acc is None else acc + weighted
            terms = jnp.where(lanes == i % SUB, jnp.sum(acc, axis=1, keepdims=True), terms)
        term_ref[first // SUB + group] = terms
        for a in range(SUB):
            left = []
            for i in members:
                place = near_count - 1
                for k in range(near_count - 1):
                    place = jnp.where(near[i % SUB][k] == a, k, place)
                left.append(cost_scr[i, place])
            x = jnp.dot(
                jnp.concatenate(left, axis=0),
                plan_scr[group * SUB + a],
                preferred_element_type=jnp.float32,
            )
            for i in members:
                high, low = split(x[(i % SUB) * width : (i % SUB + 1) * width])
                x_ref[first + i, 0:width, a * wide : (a + 1) * wide] = high
                x_ref[first + i, width : 2 * width, a * wide : (a + 1) * wide] = low


def relay_kernel(*refs):
    pass


def far_kernel(counts, row_axis, col_axis, *refs):
    row_devices, col_devices, target_here, source_count, target_count, group_blocks, link_count = counts
    near_index_ref, slot_ref, link_ref, x_ref, term_ref, mass_ref = refs[:6]
    cost_parts = refs[6 : 6 + row_devices]
    pack_ref, out_ref, work_ref, tall_ref, part_ref, log_source_ref, log_target_ref, select_ref = refs[
        6 + row_devices : 14 + row_devices
    ]
    far_high, far_low, table, column_scr, scale_scr, peak_scr, sum_scr = refs[14 + row_devices :]
    g = pl.program_id(0)
    near_count = near_index_ref.shape[0]
    slots = slot_ref.shape[0]
    rows = out_ref.shape[0]
    width = out_ref.shape[3]
    zero_block = group_blocks * link_count

    @pl.when(g == 0)
    def _():
        me = lax.axis_index(row_axis)
        col = lax.axis_index(col_axis)
        far_high[zero_block] = jnp.zeros((width, width), jnp.bfloat16)
        far_low[zero_block] = jnp.zeros((width, width), jnp.bfloat16)

        def clear(e, _):
            table[e] = zero_block
            return 0

        lax.fori_loop(0, group_blocks * group_blocks, clear, 0)

        def mark(j, _):
            for m in range(link_count):
                table[j * group_blocks + link_ref[m, 0, j]] = j * link_count + m
            return 0

        lax.fori_loop(0, group_blocks, mark, 0)
        pack_rows = pack_ref.shape[0] // (row_devices * col_devices)
        total_source = functools.reduce(
            jnp.add,
            [pack_ref[r * col_devices * pack_rows : r * col_devices * pack_rows + 1, :] for r in range(row_devices)],
        )
        targets = functools.reduce(
            jnp.add,
            [
                pack_ref[d * pack_rows + 1 + h : d * pack_rows + 2 + h, :]
                for d in range(row_devices * col_devices)
                for h in range(target_here)
            ],
        )
        total_target = jnp.sum(targets, axis=1, keepdims=True)
        log_source_ref[...] = jnp.log2(source_count * mass_ref[...].astype(jnp.float32) / total_source)
        scale_scr[...] = source_count / (total_source * (near_count * width))
        column_scr[...] = jnp.zeros_like(column_scr)
        for s in range(row_devices):
            for h in range(target_here):
                j = (me ^ s) * target_here + h
                place = ((me ^ s) * col_devices + col) * pack_rows + 1 + h
                mass = target_count * pack_ref[pl.ds(place, 1), :] / total_target
                log_target_ref[pl.ds(j, 1), :] = jnp.log2(mass)
                tall = jnp.broadcast_to(mass, (width, width)).T
                for m in range(link_count):
                    block = cost_parts[s][0, h, m]
                    high, low = split(block)
                    far_high[j * link_count + m] = high
                    far_low[j * link_count + m] = low
                    spread = jnp.sum(tall * (block * block), axis=0, keepdims=True)
                    t = link_ref[m, 0, j]
                    column_scr[pl.ds(t, 1), :] += spread * (1.0 / (link_count * width))

    group_devices = target_count // (group_blocks * width)
    coef = 2.0 * (1.0 / (near_count * width)) * (1.0 / (slots * group_devices * width))
    scale = scale_scr[0:1, 0:1]
    for i in range(rows):
        row = g * rows + i
        group = row - lax.rem(row, SUB)
        targets = [slot_ref[l, row] for l in range(slots)]
        far_rows = []
        left = []
        for k in range(near_count):
            inside = near_index_ref[k, row] & (SUB - 1)
            left.append(x_ref[row, :, pl.ds(pl.multiple_of(inside * (slots * width), slots * width), slots * width)])
            for q in range(slots):
                j = slot_ref[q, group + inside]
                far_rows.append([table[j * group_blocks + t] for t in targets])
        left = jnp.concatenate(left, axis=1)
        right_high = jnp.concatenate(
            [jnp.concatenate([far_high[e] for e in r], axis=1) for r in far_rows], axis=0
        )
        right_low = jnp.concatenate(
            [jnp.concatenate([far_low[e] for e in r], axis=1) for r in far_rows], axis=0
        )
        both = jnp.dot(left, right_high, preferred_element_type=jnp.float32)
        rest = jnp.dot(left[0:width], right_low, preferred_element_type=jnp.float32)
        product = both[0:width] + (both[width:] + rest)
        tall = term_ref[row // SUB, :, i % SUB : i % SUB + 1] * scale
        scores = []
        for l in range(slots):
            cost = tall + column_scr[pl.ds(targets[l], 1), :] - coef * product[:, l * width : (l + 1) * width]
            out_ref[i, 0, l] = cost
            select_ref[pl.ds(row * slots + l, 1), :] = jnp.full((1, width), targets[l], jnp.int32)
            scaled = cost * -to_log2
            work_ref[row, l] = scaled
            turned = scaled.T
            tall_ref[row, l] = turned
            scores.append(turned)
        row_pass(scores, row, peak_scr, sum_scr)

    @pl.when(g == pl.num_programs(0) - 1)
    def _():
        part_ref[...] = peak_scr[...] + jnp.log2(sum_scr[...])


def row_pass(scores, row, peak_scr, sum_scr):
    peak = jnp.max(functools.reduce(jnp.maximum, scores), axis=0, keepdims=True)
    total = functools.reduce(jnp.add, [jnp.exp2(s - peak) for s in scores])
    peak_scr[pl.ds(row, 1), :] = peak
    sum_scr[pl.ds(row, 1), :] = jnp.sum(total, axis=0, keepdims=True)


def column_kernel(copies, work_ref, select_ref, log_mass_ref, *refs):
    parts = refs[:-5]
    out_ref, potential_ref, potential_scr, peak_scr, sum_scr = refs[-5:]
    rows, slots, width, _ = work_ref.shape
    together = math.gcd(rows, 8)
    scaled = log_mass_ref[...] - log_sum([p[...] for p in parts])
    potential_scr[...] = scaled
    potential_ref[...] = scaled * from_log2

    for first in range(0, rows, together):
        tall = potential_scr[first : first + together, :].T
        for i in range(together):
            for l in range(slots):
                score = tall[:, i : i + 1] + work_ref[first + i, l]
                peak = jnp.max(score, axis=0, keepdims=True)
                total = jnp.sum(jnp.exp2(score - peak), axis=0, keepdims=True)
                place = (first + i) * slots + l
                peak_scr[place : place + 1, :] = peak
                sum_scr[place : place + 1, :] = total
    select = select_ref[...]
    peaks = peak_scr[...]
    sums = sum_scr[...]
    blocks = out_ref.shape[0] // copies
    for t in range(blocks):
        chosen = select == t
        peak = jnp.max(jnp.where(chosen, peaks, very_low), axis=0, keepdims=True)
        shifted = jnp.where(chosen, sums * jnp.exp2(jnp.minimum(peaks - peak, 0.0)), 0.0)
        total = jnp.sum(shifted, axis=0, keepdims=True)
        some = total > 0.0
        out_ref[t : t + 1, :] = jnp.where(
            some, peak + jnp.log2(jnp.where(some, total, 1.0)), very_low
        )
    if copies > 1:
        put_copies(out_ref, copies, out_ref[0:blocks, :])


def row_kernel(
    row_devices, slot_ref, tall_ref, log_mass_ref, parts_ref, out_ref, wide_scr, peak_scr, sum_scr
):
    rows, slots, width, _ = tall_ref.shape
    potential = (log_mass_ref[...] - log_sum(parts_of(parts_ref, row_devices))).T
    for t in range(wide_scr.shape[0]):
        wide_scr[t] = jnp.broadcast_to(potential[:, t : t + 1], (width, width))

    for row in range(rows):
        scores = [wide_scr[slot_ref[l, row]] + tall_ref[row, l] for l in range(slots)]
        row_pass(scores, row, peak_scr, sum_scr)
    out_ref[...] = peak_scr[...] + jnp.log2(sum_scr[...])


def last_kernel(row_devices, row_axis, log_mass_ref, parts_ref, out_ref):
    here = out_ref.shape[0]
    start = lax.axis_index(row_axis) * here
    log_mass = log_mass_ref[pl.ds(start, here), :]
    out_ref[...] = (log_mass - log_sum(parts_of(parts_ref, row_devices))) * from_log2


def per_device(
    coupling,
    coupling_index,
    near_cost,
    near_index,
    source_weights,
    target_cost,
    target_index,
    target_weights,
):
    rows_here = coupling.shape[0]
    slots = coupling.shape[2]
    width = coupling.shape[3]
    near_count = near_cost.shape[1]
    group_blocks = target_index.shape[1]
    link_count = target_index.shape[2]
    target_here = target_cost.shape[1]
    row_devices = lax.axis_size("rows")
    col_devices = lax.axis_size("cols")
    source_count = rows_here * row_devices * width
    target_count = group_blocks * width * col_devices
    f32 = jnp.float32
    half = row_devices // 2
    arrived = {0: target_cost}
    for mask in range(1, half + 1):
        arrived[mask] = send(target_cost, "rows", mask)

    near_t = in_hbm(near_index.T)
    slot_t = in_hbm(coupling_index[:, 0, :].T)
    link_t = in_hbm(jnp.transpose(target_index, (2, 0, 1)))
    mass = in_hbm(source_weights.reshape(rows_here, width))
    small = pltpu.CompilerParams(vmem_limit_bytes=4 * mib)

    pack_rows = 1 + target_here
    devices = row_devices * col_devices
    pack = pl.pallas_call(
        functools.partial(pack_kernel, devices),
        in_specs=[VMEM, VMEM],
        out_shape=jax.ShapeDtypeStruct((devices * pack_rows, width), f32),
        compiler_params=small,
        name="pack",
    )(mass, in_hbm(target_weights.reshape(target_here, width)))
    packs = exchange(pack, ("rows", "cols"))

    direct = list(range(1, half + 1))
    passed = pl.pallas_call(
        relay_kernel,
        in_specs=[ANY] * half,
        out_specs=[ANY] * half,
        out_shape=[jax.ShapeDtypeStruct(target_cost.shape, f32)] * half,
        input_output_aliases={e: e for e in range(half)},
        compiler_params=small,
        cost_estimate=pl.CostEstimate(flops=10**11, bytes_accessed=256 * mib, transcendentals=0),
        name="relay",
    )(*[arrived[mask] for mask in direct])
    arrived.update(zip(direct, passed))
    for mask in range(half + 1, row_devices):
        arrived[mask] = send(arrived[half], "rows", mask - half)
    cost_parts = [arrived[s] for s in range(row_devices)]

    wide = near_count * slots * width
    groups = rows_here // SUB
    step_rows = 2 * SUB if groups % 2 == 0 else SUB
    x, term = pl.pallas_call(
        near_kernel,
        grid=(rows_here // step_rows,),
        in_specs=[
            SMEM,
            pl.BlockSpec((step_rows, near_count, width, width), lambda g: (g, 0, 0, 0)),
            pl.BlockSpec((step_rows, 1, slots, width, width), lambda g: (g, 0, 0, 0, 0)),
            whole((rows_here, width)),
            ANY,
        ],
        out_specs=[VMEM, VMEM],
        out_shape=[
            pltpu.VMEM((rows_here, 2 * width, SUB * slots * width), jnp.bfloat16),
            pltpu.VMEM((groups, width, SUB), f32),
        ],
        scratch_shapes=[
            pltpu.VMEM((step_rows, 3 * width, slots * width), jnp.bfloat16),
            pltpu.VMEM((step_rows, near_count, width, 3 * width), jnp.bfloat16),
        ],
        compiler_params=pltpu.CompilerParams(vmem_limit_bytes=12 * mib),
        cost_estimate=pl.CostEstimate(
            flops=6 * rows_here * wide * width * width,
            bytes_accessed=4 * rows_here * width * (near_count + slots) * width,
            transcendentals=0,
        ),
        name="near_product",
    )(near_t, in_hbm(near_cost), in_hbm(coupling), mass, packs)

    far_bytes = group_blocks * link_count * width * width * 4
    far_rows = 2 * step_rows if rows_here % (2 * step_rows) == 0 else step_rows
    steps = rows_here // far_rows
    cost_block = pl.BlockSpec((far_rows, 1, slots, width, width), lambda g: (g, 0, 0, 0, 0))
    work_shape = pltpu.VMEM((rows_here, slots, width, width), f32)
    cost_blocks, work, tall, row_part, log_source, log_target, select = pl.pallas_call(
        functools.partial(
            far_kernel,
            (row_devices, col_devices, target_here, source_count, target_count, group_blocks, link_count),
            "rows",
            "cols",
        ),
        grid=(steps,),
        in_specs=[SMEM, SMEM, SMEM, VMEM, VMEM, whole((rows_here, width))]
        + [VMEM] * row_devices
        + [whole(packs.shape)],
        out_specs=[
            cost_block,
            VMEM,
            VMEM,
            whole((rows_here, width)),
            whole((rows_here, width)),
            whole((group_blocks, width)),
            whole((rows_here * slots, width)),
        ],
        out_shape=[
            jax.ShapeDtypeStruct(coupling.shape, f32),
            work_shape,
            work_shape,
            jax.ShapeDtypeStruct((rows_here, width), f32),
            jax.ShapeDtypeStruct((rows_here, width), f32),
            jax.ShapeDtypeStruct((group_blocks, width), f32),
            jax.ShapeDtypeStruct((rows_here * slots, width), jnp.int32),
        ],
        scratch_shapes=[
            pltpu.VMEM((group_blocks * link_count + 1, width, width), jnp.bfloat16),
            pltpu.VMEM((group_blocks * link_count + 1, width, width), jnp.bfloat16),
            pltpu.SMEM((group_blocks * group_blocks,), jnp.int32),
            pltpu.VMEM((group_blocks, width), f32),
            pltpu.VMEM((1, width), f32),
            pltpu.VMEM((rows_here, width), f32),
            pltpu.VMEM((rows_here, width), f32),
        ],
        compiler_params=pltpu.CompilerParams(vmem_limit_bytes=12 * mib + 2 * far_bytes),
        name="far_product",
    )(near_t, slot_t, link_t, in_vmem(x), in_vmem(term), mass, *cost_parts, packs)

    pass_params = pltpu.CompilerParams(vmem_limit_bytes=12 * mib)

    def column_step(row_parts, copies):
        return pl.pallas_call(
            functools.partial(column_kernel, copies),
            in_specs=[VMEM] * (3 + len(row_parts)),
            out_specs=[VMEM, VMEM],
            out_shape=[
                jax.ShapeDtypeStruct((copies * group_blocks, width), f32),
                jax.ShapeDtypeStruct((rows_here, width), f32),
            ],
            scratch_shapes=[
                pltpu.VMEM((rows_here, width), f32),
                pltpu.VMEM((rows_here * slots, width), f32),
                pltpu.VMEM((rows_here * slots, width), f32),
            ],
            compiler_params=pass_params,
            name="column_pass",
        )(in_vmem(work), select, log_source, *row_parts)

    def row_step(column_parts):
        return pl.pallas_call(
            functools.partial(row_kernel, row_devices),
            in_specs=[SMEM, VMEM, VMEM, VMEM],
            out_specs=VMEM,
            out_shape=jax.ShapeDtypeStruct((rows_here, width), f32),
            scratch_shapes=[
                pltpu.VMEM((group_blocks, width, width), f32),
                pltpu.VMEM((rows_here, width), f32),
                pltpu.VMEM((rows_here, width), f32),
            ],
            compiler_params=pass_params,
            name="row_pass",
        )(slot_t, in_vmem(tall), log_target, column_parts)

    for step in range(ITERS):
        last = step == ITERS - 1
        column_part, source_potential = column_step(
            from_all(row_part, "cols"), 1 if last else row_devices
        )
        column_parts = exchange(column_part, "rows")
        if not last:
            row_part = row_step(column_parts)
    own_target = pl.pallas_call(
        functools.partial(last_kernel, row_devices, "rows"),
        out_shape=jax.ShapeDtypeStruct((target_here, width), f32),
        compiler_params=small,
        name="last_potential",
    )(log_target, column_parts)
    return (
        cost_blocks,
        source_potential.reshape(rows_here * width),
        own_target.reshape(1, target_here * width),
    )


def solution(mesh):
    placed = (
        P("rows", "cols", None, None, None),
        P("rows", "cols", None),
        P("rows", None, None, None),
        P("rows", None),
        P("rows"),
        P("cols", "rows", None, None, None),
        P("cols", None, None),
        P("cols", "rows"),
    )
    return jax.shard_map(
        per_device,
        mesh=mesh,
        in_specs=placed,
        out_specs=(P("rows", "cols", None, None, None), P("rows"), P("cols", "rows")),
        check_vma=False,
    )
```

```python
import functools
import math

import jax
import jax.numpy as jnp
from jax import lax
from jax.experimental import pallas as pl
from jax.experimental.pallas import tpu as pltpu
from jax.sharding import PartitionSpec as P

ITERS = 3
SUB = 4

entropy = 0.01
to_log2 = math.log2(math.e) / entropy
from_log2 = entropy * math.log(2.0)
very_low = -1e30
mib = 1024 * 1024

SMEM = pl.BlockSpec(memory_space=pltpu.SMEM)
VMEM = pl.BlockSpec(memory_space=pltpu.VMEM)
ANY = pl.BlockSpec(memory_space=pl.ANY)


def in_hbm(x):
    return pltpu.with_memory_space_constraint(x, pltpu.HBM)


def in_vmem(x):
    return pltpu.with_memory_space_constraint(x, pltpu.VMEM)


def whole(shape):
    return pl.BlockSpec(shape, lambda *_: (0,) * len(shape))


def split(x):
    high = x.astype(jnp.bfloat16)
    return high, (x - high.astype(jnp.float32)).astype(jnp.bfloat16)


def tree(parts, op):
    while len(parts) > 1:
        half = len(parts) // 2
        parts = [op(parts[s], parts[s + half]) for s in range(half)]
    return parts[0]


def log_sum(parts):
    peak = tree(parts, jnp.maximum)
    return peak + jnp.log2(tree([jnp.exp2(p - peak) for p in parts], jnp.add))


def parts_of(ref, devices):
    rows = ref.shape[0] // devices
    return [ref[d * rows : (d + 1) * rows, :] for d in range(devices)]


def put_copies(ref, devices, value):
    rows = value.shape[0]
    for d in range(devices):
        ref[d * rows : (d + 1) * rows, :] = value


def send(x, axis, mask):
    size = lax.axis_size(axis)
    return lax.ppermute(x, axis, [(d, d ^ mask) for d in range(size)])


def from_all(x, axis):
    return [x] + [send(x, axis, s) for s in range(1, lax.axis_size(axis))]


def exchange(copies, axis):
    return lax.all_to_all(copies, axis, 0, 0, tiled=True)


def pack_kernel(devices, source_ref, target_ref, out_ref):
    rows = out_ref.shape[0] // devices
    total = jnp.sum(source_ref[...].astype(jnp.float32), axis=(0, 1), keepdims=True)
    target = target_ref[...].astype(jnp.float32)
    for d in range(devices):
        out_ref[d * rows : d * rows + 1, :] = jnp.broadcast_to(total, (1, out_ref.shape[1]))
        out_ref[d * rows + 1 : d * rows + 1 + target.shape[0], :] = target


def near_kernel(near_index_ref, cost_ref, plan_ref, mass_ref, totals_ref, x_ref, term_ref, plan_scr):
    rows = cost_ref.shape[0]
    first = pl.program_id(0) * rows
    near_count = cost_ref.shape[1]
    width = cost_ref.shape[2]
    slots = plan_ref.shape[2]
    wide = slots * width
    for a in range(rows):
        plan = jnp.concatenate([plan_ref[a, 0, q] for q in range(slots)], axis=1)
        high, low = split(plan)
        plan_scr[a, 0:width, :] = high
        plan_scr[a, width : 2 * width, :] = low
        plan_scr[a, 2 * width : 3 * width, :] = high
    lanes = lax.broadcasted_iota(jnp.int32, (width, SUB), 1)
    for group in range(rows // SUB):
        terms = jnp.zeros((width, SUB), jnp.float32)
        for i in range(group * SUB, (group + 1) * SUB):
            acc = None
            for k in range(near_count):
                a = group * SUB + (near_index_ref[k, first + i] & (SUB - 1))
                cost = cost_ref[i, k]
                high, low = split(cost)
                x = jnp.dot(
                    jnp.concatenate([high, high, low], axis=1),
                    plan_scr[a],
                    preferred_element_type=jnp.float32,
                )
                x_high, x_low = split(x)
                x_ref[first + i, 0:width, k * wide : (k + 1) * wide] = x_high
                x_ref[first + i, width : 2 * width, k * wide : (k + 1) * wide] = x_low
                weighted = cost * cost * mass_ref[pl.ds(first + a, 1), :].astype(jnp.float32)
                acc = weighted if acc is None else acc + weighted
            terms = jnp.where(lanes == i % SUB, jnp.sum(acc, axis=1, keepdims=True), terms)
        term_ref[first // SUB + group] = terms


def relay_kernel(*refs):
    pass


def far_kernel(counts, row_axis, col_axis, *refs):
    row_devices, col_devices, target_here, source_count, target_count, group_blocks, link_count = counts
    near_index_ref, slot_ref, link_ref, x_ref, term_ref, mass_ref = refs[:6]
    cost_parts = refs[6 : 6 + row_devices]
    pack_ref, out_ref, work_ref, tall_ref, part_ref, log_source_ref, log_target_ref, select_ref = refs[
        6 + row_devices : 14 + row_devices
    ]
    far_high, far_low, table, column_scr, scale_scr, peak_scr, sum_scr = refs[14 + row_devices :]
    g = pl.program_id(0)
    near_count = near_index_ref.shape[0]
    slots = slot_ref.shape[0]
    rows = out_ref.shape[0]
    width = out_ref.shape[3]
    zero_block = group_blocks * link_count

    @pl.when(g == 0)
    def _():
        me = lax.axis_index(row_axis)
        col = lax.axis_index(col_axis)
        far_high[zero_block] = jnp.zeros((width, width), jnp.bfloat16)
        far_low[zero_block] = jnp.zeros((width, width), jnp.bfloat16)

        def clear(e, _):
            table[e] = zero_block
            return 0

        lax.fori_loop(0, group_blocks * group_blocks, clear, 0)

        def mark(j, _):
            for m in range(link_count):
                table[j * group_blocks + link_ref[m, 0, j]] = j * link_count + m
            return 0

        lax.fori_loop(0, group_blocks, mark, 0)
        pack_rows = pack_ref.shape[0] // (row_devices * col_devices)
        total_source = functools.reduce(
            jnp.add,
            [pack_ref[r * col_devices * pack_rows : r * col_devices * pack_rows + 1, :] for r in range(row_devices)],
        )
        targets = functools.reduce(
            jnp.add,
            [
                pack_ref[d * pack_rows + 1 + h : d * pack_rows + 2 + h, :]
                for d in range(row_devices * col_devices)
                for h in range(target_here)
            ],
        )
        total_target = jnp.sum(targets, axis=1, keepdims=True)
        log_source_ref[...] = jnp.log2(source_count * mass_ref[...].astype(jnp.float32) / total_source)
        scale_scr[...] = source_count / (total_source * (near_count * width))
        column_scr[...] = jnp.zeros_like(column_scr)
        for s in range(row_devices):
            for h in range(target_here):
                j = (me ^ s) * target_here + h
                place = ((me ^ s) * col_devices + col) * pack_rows + 1 + h
                mass = target_count * pack_ref[pl.ds(place, 1), :] / total_target
                log_target_ref[pl.ds(j, 1), :] = jnp.log2(mass)
                tall = jnp.broadcast_to(mass, (width, width)).T
                for m in range(link_count):
                    block = cost_parts[s][0, h, m]
                    high, low = split(block)
                    far_high[j * link_count + m] = high
                    far_low[j * link_count + m] = low
                    spread = jnp.sum(tall * (block * block), axis=0, keepdims=True)
                    t = link_ref[m, 0, j]
                    column_scr[pl.ds(t, 1), :] += spread * (1.0 / (link_count * width))

    group_devices = target_count // (group_blocks * width)
    coef = 2.0 * (1.0 / (near_count * width)) * (1.0 / (slots * group_devices * width))
    scale = scale_scr[0:1, 0:1]
    for i in range(rows):
        row = g * rows + i
        group = row - lax.rem(row, SUB)
        targets = [slot_ref[l, row] for l in range(slots)]
        far_rows = []
        for k in range(near_count):
            a = group + (near_index_ref[k, row] & (SUB - 1))
            for q in range(slots):
                j = slot_ref[q, a]
                far_rows.append([table[j * group_blocks + t] for t in targets])
        right_high = jnp.concatenate(
            [jnp.concatenate([far_high[e] for e in r], axis=1) for r in far_rows], axis=0
        )
        right_low = jnp.concatenate(
            [jnp.concatenate([far_low[e] for e in r], axis=1) for r in far_rows], axis=0
        )
        both = jnp.dot(x_ref[row], right_high, preferred_element_type=jnp.float32)
        rest = jnp.dot(x_ref[row, 0:width, :], right_low, preferred_element_type=jnp.float32)
        product = both[0:width] + (both[width:] + rest)
        tall = term_ref[row // SUB, :, i % SUB : i % SUB + 1] * scale
        scores = []
        for l in range(slots):
            cost = tall + column_scr[pl.ds(targets[l], 1), :] - coef * product[:, l * width : (l + 1) * width]
            out_ref[i, 0, l] = cost
            select_ref[pl.ds(row * slots + l, 1), :] = jnp.full((1, width), targets[l], jnp.int32)
            scaled = cost * -to_log2
            work_ref[row, l] = scaled
            turned = scaled.T
            tall_ref[row, l] = turned
            scores.append(turned)
        row_pass(scores, row, peak_scr, sum_scr)

    @pl.when(g == pl.num_programs(0) - 1)
    def _():
        part_ref[...] = row_sums(peak_scr, sum_scr)


def block_sums(score):
    pieces = score.reshape(-1, 8, score.shape[-1])
    peak = jnp.max(pieces, axis=0)
    return peak, jnp.sum(jnp.exp2(pieces - peak[None]), axis=0)


def over_residues(peaks, sums):
    peak = jnp.max(peaks, axis=1)
    return peak, jnp.sum(sums * jnp.exp2(peaks - peak[:, None, :]), axis=1)


def row_pass(scores, row, peak_scr, sum_scr):
    for l, score in enumerate(scores):
        peak, total = block_sums(score)
        peak_scr[row, l * 8 : (l + 1) * 8, :] = peak
        sum_scr[row, l * 8 : (l + 1) * 8, :] = total


def row_sums(peak_scr, sum_scr):
    peak, total = over_residues(peak_scr[...], sum_scr[...])
    return peak + jnp.log2(total)


def column_kernel(copies, work_ref, select_ref, log_mass_ref, *refs):
    parts = refs[:-5]
    out_ref, potential_ref, potential_scr, peak_scr, sum_scr = refs[-5:]
    rows, slots, width, _ = work_ref.shape
    together = math.gcd(rows, 8)
    scaled = log_mass_ref[...] - log_sum([p[...] for p in parts])
    potential_scr[...] = scaled
    potential_ref[...] = scaled * from_log2

    for first in range(0, rows, together):
        tall = potential_scr[first : first + together, :].T
        for i in range(together):
            for l in range(slots):
                score = tall[:, i : i + 1] + work_ref[first + i, l]
                place = (first + i) * slots + l
                peak_scr[place], sum_scr[place] = block_sums(score)
    select = select_ref[...]
    peaks, sums = over_residues(peak_scr[...], sum_scr[...])
    blocks = out_ref.shape[0] // copies
    for t in range(blocks):
        chosen = select == t
        peak = jnp.max(jnp.where(chosen, peaks, very_low), axis=0, keepdims=True)
        shifted = jnp.where(chosen, sums * jnp.exp2(jnp.minimum(peaks - peak, 0.0)), 0.0)
        total = jnp.sum(shifted, axis=0, keepdims=True)
        some = total > 0.0
        out_ref[t : t + 1, :] = jnp.where(
            some, peak + jnp.log2(jnp.where(some, total, 1.0)), very_low
        )
    if copies > 1:
        put_copies(out_ref, copies, out_ref[0:blocks, :])


def row_kernel(
    row_devices, slot_ref, tall_ref, log_mass_ref, parts_ref, out_ref, wide_scr, peak_scr, sum_scr
):
    rows, slots, width, _ = tall_ref.shape
    potential = (log_mass_ref[...] - log_sum(parts_of(parts_ref, row_devices))).T
    for t in range(wide_scr.shape[0]):
        wide_scr[t] = jnp.broadcast_to(potential[:, t : t + 1], (width, width))

    for row in range(rows):
        scores = [wide_scr[slot_ref[l, row]] + tall_ref[row, l] for l in range(slots)]
        row_pass(scores, row, peak_scr, sum_scr)
    out_ref[...] = row_sums(peak_scr, sum_scr)


def last_kernel(row_devices, row_axis, log_mass_ref, parts_ref, out_ref):
    here = out_ref.shape[0]
    start = lax.axis_index(row_axis) * here
    log_mass = log_mass_ref[pl.ds(start, here), :]
    out_ref[...] = (log_mass - log_sum(parts_of(parts_ref, row_devices))) * from_log2


def per_device(
    coupling,
    coupling_index,
    near_cost,
    near_index,
    source_weights,
    target_cost,
    target_index,
    target_weights,
):
    rows_here = coupling.shape[0]
    slots = coupling.shape[2]
    width = coupling.shape[3]
    near_count = near_cost.shape[1]
    group_blocks = target_index.shape[1]
    link_count = target_index.shape[2]
    target_here = target_cost.shape[1]
    row_devices = lax.axis_size("rows")
    col_devices = lax.axis_size("cols")
    source_count = rows_here * row_devices * width
    target_count = group_blocks * width * col_devices
    f32 = jnp.float32
    half = row_devices // 2
    arrived = {0: target_cost}
    for mask in range(1, half + 1):
        arrived[mask] = send(target_cost, "rows", mask)

    near_t = in_hbm(near_index.T)
    slot_t = in_hbm(coupling_index[:, 0, :].T)
    link_t = in_hbm(jnp.transpose(target_index, (2, 0, 1)))
    mass = in_hbm(source_weights.reshape(rows_here, width))
    small = pltpu.CompilerParams(vmem_limit_bytes=4 * mib)

    pack_rows = 1 + target_here
    devices = row_devices * col_devices
    pack = pl.pallas_call(
        functools.partial(pack_kernel, devices),
        in_specs=[VMEM, VMEM],
        out_shape=jax.ShapeDtypeStruct((devices * pack_rows, width), f32),
        compiler_params=small,
        name="pack",
    )(mass, in_hbm(target_weights.reshape(target_here, width)))
    packs = exchange(pack, ("rows", "cols"))

    direct = list(range(1, half + 1))
    passed = pl.pallas_call(
        relay_kernel,
        in_specs=[ANY] * half,
        out_specs=[ANY] * half,
        out_shape=[jax.ShapeDtypeStruct(target_cost.shape, f32)] * half,
        input_output_aliases={e: e for e in range(half)},
        compiler_params=small,
        cost_estimate=pl.CostEstimate(flops=10**11, bytes_accessed=256 * mib, transcendentals=0),
        name="relay",
    )(*[arrived[mask] for mask in direct])
    arrived.update(zip(direct, passed))
    for mask in range(half + 1, row_devices):
        arrived[mask] = send(arrived[half], "rows", mask - half)
    cost_parts = [arrived[s] for s in range(row_devices)]

    wide = near_count * slots * width
    groups = rows_here // SUB
    step_rows = 2 * SUB if groups % 2 == 0 else SUB
    x, term = pl.pallas_call(
        near_kernel,
        grid=(rows_here // step_rows,),
        in_specs=[
            SMEM,
            pl.BlockSpec((step_rows, near_count, width, width), lambda g: (g, 0, 0, 0)),
            pl.BlockSpec((step_rows, 1, slots, width, width), lambda g: (g, 0, 0, 0, 0)),
            whole((rows_here, width)),
            ANY,
        ],
        out_specs=[VMEM, VMEM],
        out_shape=[
            pltpu.VMEM((rows_here, 2 * width, wide), jnp.bfloat16),
            pltpu.VMEM((groups, width, SUB), f32),
        ],
        scratch_shapes=[pltpu.VMEM((step_rows, 3 * width, slots * width), jnp.bfloat16)],
        compiler_params=pltpu.CompilerParams(vmem_limit_bytes=12 * mib),
        cost_estimate=pl.CostEstimate(
            flops=6 * rows_here * wide * width * width,
            bytes_accessed=4 * rows_here * width * (near_count + slots) * width,
            transcendentals=0,
        ),
        name="near_product",
    )(near_t, in_hbm(near_cost), in_hbm(coupling), mass, packs)

    far_bytes = group_blocks * link_count * width * width * 4
    far_rows = 2 * step_rows if rows_here % (2 * step_rows) == 0 else step_rows
    steps = rows_here // far_rows
    cost_block = pl.BlockSpec((far_rows, 1, slots, width, width), lambda g: (g, 0, 0, 0, 0))
    work_shape = pltpu.VMEM((rows_here, slots, width, width), f32)
    cost_blocks, work, tall, row_part, log_source, log_target, select = pl.pallas_call(
        functools.partial(
            far_kernel,
            (row_devices, col_devices, target_here, source_count, target_count, group_blocks, link_count),
            "rows",
            "cols",
        ),
        grid=(steps,),
        in_specs=[SMEM, SMEM, SMEM, VMEM, VMEM, whole((rows_here, width))]
        + [VMEM] * row_devices
        + [whole(packs.shape)],
        out_specs=[
            cost_block,
            VMEM,
            VMEM,
            whole((rows_here, width)),
            whole((rows_here, width)),
            whole((group_blocks, width)),
            whole((rows_here * slots, width)),
        ],
        out_shape=[
            jax.ShapeDtypeStruct(coupling.shape, f32),
            work_shape,
            work_shape,
            jax.ShapeDtypeStruct((rows_here, width), f32),
            jax.ShapeDtypeStruct((rows_here, width), f32),
            jax.ShapeDtypeStruct((group_blocks, width), f32),
            jax.ShapeDtypeStruct((rows_here * slots, width), jnp.int32),
        ],
        scratch_shapes=[
            pltpu.VMEM((group_blocks * link_count + 1, width, width), jnp.bfloat16),
            pltpu.VMEM((group_blocks * link_count + 1, width, width), jnp.bfloat16),
            pltpu.SMEM((group_blocks * group_blocks,), jnp.int32),
            pltpu.VMEM((group_blocks, width), f32),
            pltpu.VMEM((1, width), f32),
            pltpu.VMEM((rows_here, slots * 8, width), f32),
            pltpu.VMEM((rows_here, slots * 8, width), f32),
        ],
        compiler_params=pltpu.CompilerParams(vmem_limit_bytes=12 * mib + 2 * far_bytes),
        name="far_product",
    )(near_t, slot_t, link_t, in_vmem(x), in_vmem(term), mass, *cost_parts, packs)

    pass_params = pltpu.CompilerParams(vmem_limit_bytes=12 * mib)

    def column_step(row_parts, copies):
        return pl.pallas_call(
            functools.partial(column_kernel, copies),
            in_specs=[VMEM] * (3 + len(row_parts)),
            out_specs=[VMEM, VMEM],
            out_shape=[
                jax.ShapeDtypeStruct((copies * group_blocks, width), f32),
                jax.ShapeDtypeStruct((rows_here, width), f32),
            ],
            scratch_shapes=[
                pltpu.VMEM((rows_here, width), f32),
                pltpu.VMEM((rows_here * slots, 8, width), f32),
                pltpu.VMEM((rows_here * slots, 8, width), f32),
            ],
            compiler_params=pass_params,
            name="column_pass",
        )(in_vmem(work), select, log_source, *row_parts)

    def row_step(column_parts):
        return pl.pallas_call(
            functools.partial(row_kernel, row_devices),
            in_specs=[SMEM, VMEM, VMEM, VMEM],
            out_specs=VMEM,
            out_shape=jax.ShapeDtypeStruct((rows_here, width), f32),
            scratch_shapes=[
                pltpu.VMEM((group_blocks, width, width), f32),
                pltpu.VMEM((rows_here, slots * 8, width), f32),
                pltpu.VMEM((rows_here, slots * 8, width), f32),
            ],
            compiler_params=pass_params,
            name="row_pass",
        )(slot_t, in_vmem(tall), log_target, column_parts)

    for step in range(ITERS):
        last = step == ITERS - 1
        column_part, source_potential = column_step(
            from_all(row_part, "cols"), 1 if last else row_devices
        )
        column_parts = exchange(column_part, "rows")
        if not last:
            row_part = row_step(column_parts)
    own_target = pl.pallas_call(
        functools.partial(last_kernel, row_devices, "rows"),
        out_shape=jax.ShapeDtypeStruct((target_here, width), f32),
        compiler_params=small,
        name="last_potential",
    )(log_target, column_parts)
    return (
        cost_blocks,
        source_potential.reshape(rows_here * width),
        own_target.reshape(1, target_here * width),
    )


def solution(mesh):
    placed = (
        P("rows", "cols", None, None, None),
        P("rows", "cols", None),
        P("rows", None, None, None),
        P("rows", None),
        P("rows"),
        P("cols", "rows", None, None, None),
        P("cols", None, None),
        P("cols", "rows"),
    )
    return jax.shard_map(
        per_device,
        mesh=mesh,
        in_specs=placed,
        out_specs=(P("rows", "cols", None, None, None), P("rows"), P("cols", "rows")),
        check_vma=False,
    )
```

```python
import functools
import math

import jax
import jax.numpy as jnp
from jax import lax
from jax.experimental import pallas as pl
from jax.experimental.pallas import tpu as pltpu
from jax.sharding import PartitionSpec as P

ITERS = 3
SUB = 4

entropy = 0.01
to_log2 = math.log2(math.e) / entropy
from_log2 = entropy * math.log(2.0)
very_low = -1e30
mib = 1024 * 1024

SMEM = pl.BlockSpec(memory_space=pltpu.SMEM)
VMEM = pl.BlockSpec(memory_space=pltpu.VMEM)
ANY = pl.BlockSpec(memory_space=pl.ANY)


def in_hbm(x):
    return pltpu.with_memory_space_constraint(x, pltpu.HBM)


def in_vmem(x):
    return pltpu.with_memory_space_constraint(x, pltpu.VMEM)


def whole(shape):
    return pl.BlockSpec(shape, lambda *_: (0,) * len(shape))


def split(x):
    high = x.astype(jnp.bfloat16)
    return high, (x - high.astype(jnp.float32)).astype(jnp.bfloat16)


def tree(parts, op):
    while len(parts) > 1:
        half = len(parts) // 2
        parts = [op(parts[s], parts[s + half]) for s in range(half)]
    return parts[0]


def log_sum(parts):
    peak = tree(parts, jnp.maximum)
    return peak + jnp.log2(tree([jnp.exp2(p - peak) for p in parts], jnp.add))


def parts_of(ref, devices):
    rows = ref.shape[0] // devices
    return [ref[d * rows : (d + 1) * rows, :] for d in range(devices)]


def put_copies(ref, devices, value):
    rows = value.shape[0]
    for d in range(devices):
        ref[d * rows : (d + 1) * rows, :] = value


def send(x, axis, mask):
    size = lax.axis_size(axis)
    return lax.ppermute(x, axis, [(d, d ^ mask) for d in range(size)])


def from_all(x, axis):
    return [x] + [send(x, axis, s) for s in range(1, lax.axis_size(axis))]


def exchange(copies, axis):
    return lax.all_to_all(copies, axis, 0, 0, tiled=True)


def pack_kernel(devices, source_ref, target_ref, out_ref):
    rows = out_ref.shape[0] // devices
    total = jnp.sum(source_ref[...].astype(jnp.float32), axis=(0, 1), keepdims=True)
    target = target_ref[...].astype(jnp.float32)
    for d in range(devices):
        out_ref[d * rows : d * rows + 1, :] = jnp.broadcast_to(total, (1, out_ref.shape[1]))
        out_ref[d * rows + 1 : d * rows + 1 + target.shape[0], :] = target


def near_kernel(near_index_ref, cost_ref, plan_ref, mass_ref, totals_ref, x_ref, term_ref, plan_scr):
    rows = cost_ref.shape[0]
    first = pl.program_id(0) * rows
    near_count = cost_ref.shape[1]
    width = cost_ref.shape[2]
    slots = plan_ref.shape[2]
    wide = slots * width
    for a in range(rows):
        plan = jnp.concatenate([plan_ref[a, 0, q] for q in range(slots)], axis=1)
        high, low = split(plan)
        plan_scr[a, 0:width, :] = high
        plan_scr[a, width : 2 * width, :] = low
        plan_scr[a, 2 * width : 3 * width, :] = high
    lanes = lax.broadcasted_iota(jnp.int32, (width, SUB), 1)
    for group in range(rows // SUB):
        terms = jnp.zeros((width, SUB), jnp.float32)
        for i in range(group * SUB, (group + 1) * SUB):
            acc = None
            for k in range(near_count):
                a = group * SUB + (near_index_ref[k, first + i] & (SUB - 1))
                cost = cost_ref[i, k]
                high, low = split(cost)
                x = jnp.dot(
                    jnp.concatenate([high, high, low], axis=1),
                    plan_scr[a],
                    preferred_element_type=jnp.float32,
                )
                x_high, x_low = split(x)
                x_ref[first + i, 0:width, k * wide : (k + 1) * wide] = x_high
                x_ref[first + i, width : 2 * width, k * wide : (k + 1) * wide] = x_low
                weighted = cost * cost * mass_ref[pl.ds(first + a, 1), :].astype(jnp.float32)
                acc = weighted if acc is None else acc + weighted
            terms = jnp.where(lanes == i % SUB, jnp.sum(acc, axis=1, keepdims=True), terms)
        term_ref[first // SUB + group] = terms


def relay_kernel(*refs):
    pass


def far_kernel(counts, row_axis, col_axis, *refs):
    row_devices, col_devices, target_here, source_count, target_count, group_blocks, link_count = counts
    near_index_ref, slot_ref, link_ref, x_ref, term_ref, mass_ref = refs[:6]
    cost_parts = refs[6 : 6 + row_devices]
    pack_ref, out_ref, work_ref, tall_ref, part_ref, log_source_ref, log_target_ref, select_ref = refs[
        6 + row_devices : 14 + row_devices
    ]
    far_high, far_low, table, column_scr, scale_scr, peak_scr, sum_scr = refs[14 + row_devices :]
    g = pl.program_id(0)
    near_count = near_index_ref.shape[0]
    slots = slot_ref.shape[0]
    rows = out_ref.shape[0]
    width = out_ref.shape[3]
    zero_block = group_blocks * link_count

    @pl.when(g == 0)
    def _():
        me = lax.axis_index(row_axis)
        col = lax.axis_index(col_axis)
        far_high[zero_block] = jnp.zeros((width, width), jnp.bfloat16)
        far_low[zero_block] = jnp.zeros((width, width), jnp.bfloat16)

        def clear(e, _):
            table[e] = zero_block
            return 0

        lax.fori_loop(0, group_blocks * group_blocks, clear, 0)

        def mark(j, _):
            for m in range(link_count):
                table[j * group_blocks + link_ref[m, 0, j]] = j * link_count + m
            return 0

        lax.fori_loop(0, group_blocks, mark, 0)
        pack_rows = pack_ref.shape[0] // (row_devices * col_devices)
        total_source = functools.reduce(
            jnp.add,
            [pack_ref[r * col_devices * pack_rows : r * col_devices * pack_rows + 1, :] for r in range(row_devices)],
        )
        targets = functools.reduce(
            jnp.add,
            [
                pack_ref[d * pack_rows + 1 + h : d * pack_rows + 2 + h, :]
                for d in range(row_devices * col_devices)
                for h in range(target_here)
            ],
        )
        total_target = jnp.sum(targets, axis=1, keepdims=True)
        log_source_ref[...] = jnp.log2(source_count * mass_ref[...].astype(jnp.float32) / total_source)
        scale_scr[...] = source_count / (total_source * (near_count * width))
        column_scr[...] = jnp.zeros_like(column_scr)
        for s in range(row_devices):
            for h in range(target_here):
                j = (me ^ s) * target_here + h
                place = ((me ^ s) * col_devices + col) * pack_rows + 1 + h
                mass = target_count * pack_ref[pl.ds(place, 1), :] / total_target
                log_target_ref[pl.ds(j, 1), :] = jnp.log2(mass)
                tall = jnp.broadcast_to(mass, (width, width)).T
                for m in range(link_count):
                    block = cost_parts[s][0, h, m]
                    high, low = split(block)
                    far_high[j * link_count + m] = high
                    far_low[j * link_count + m] = low
                    spread = jnp.sum(tall * (block * block), axis=0, keepdims=True)
                    t = link_ref[m, 0, j]
                    column_scr[pl.ds(t, 1), :] += spread * (1.0 / (link_count * width))

    group_devices = target_count // (group_blocks * width)
    coef = 2.0 * (1.0 / (near_count * width)) * (1.0 / (slots * group_devices * width))
    scale = scale_scr[0:1, 0:1]
    for i in range(rows):
        row = g * rows + i
        group = row - lax.rem(row, SUB)
        targets = [slot_ref[l, row] for l in range(slots)]
        far_rows = []
        for k in range(near_count):
            a = group + (near_index_ref[k, row] & (SUB - 1))
            for q in range(slots):
                j = slot_ref[q, a]
                far_rows.append([table[j * group_blocks + t] for t in targets])
        right_high = jnp.concatenate(
            [jnp.concatenate([far_high[e] for e in r], axis=1) for r in far_rows], axis=0
        )
        right_low = jnp.concatenate(
            [jnp.concatenate([far_low[e] for e in r], axis=1) for r in far_rows], axis=0
        )
        both = jnp.dot(x_ref[row], right_high, preferred_element_type=jnp.float32)
        rest = jnp.dot(x_ref[row, 0:width, :], right_low, preferred_element_type=jnp.float32)
        product = both[0:width] + (both[width:] + rest)
        tall = term_ref[row // SUB, :, i % SUB : i % SUB + 1] * scale
        scores = []
        for l in range(slots):
            cost = tall + column_scr[pl.ds(targets[l], 1), :] - coef * product[:, l * width : (l + 1) * width]
            out_ref[i, 0, l] = cost
            select_ref[pl.ds(row * slots + l, 1), :] = jnp.full((1, width), targets[l], jnp.int32)
            scaled = cost * -to_log2
            work_ref[row, l] = scaled
            turned = scaled.T
            tall_ref[row, l] = turned
            scores.append(turned)
        row_pass(scores, row, part_ref.shape[0], peak_scr, sum_scr)

    @pl.when(g == pl.num_programs(0) - 1)
    def _():
        part_ref[...] = row_sums(part_ref.shape[0], peak_scr, sum_scr)


def row_pass(scores, row, rows, peak_scr, sum_scr):
    for l, score in enumerate(scores):
        peak = jnp.max(score, axis=0, keepdims=True)
        peak_scr[pl.ds(l * rows + row, 1), :] = peak
        sum_scr[pl.ds(l * rows + row, 1), :] = jnp.sum(jnp.exp2(score - peak), axis=0, keepdims=True)


def row_sums(rows, peak_scr, sum_scr):
    slots = peak_scr.shape[0] // rows
    peaks = [peak_scr[l * rows : (l + 1) * rows, :] for l in range(slots)]
    sums = [sum_scr[l * rows : (l + 1) * rows, :] for l in range(slots)]
    peak = functools.reduce(jnp.maximum, peaks)
    total = functools.reduce(jnp.add, [t * jnp.exp2(p - peak) for p, t in zip(peaks, sums)])
    return peak + jnp.log2(total)


def column_kernel(copies, work_ref, select_ref, log_mass_ref, *refs):
    parts = refs[:-5]
    out_ref, potential_ref, potential_scr, peak_scr, sum_scr = refs[-5:]
    rows, slots, width, _ = work_ref.shape
    together = math.gcd(rows, 8)
    scaled = log_mass_ref[...] - log_sum([p[...] for p in parts])
    potential_scr[...] = scaled
    potential_ref[...] = scaled * from_log2

    for first in range(0, rows, together):
        tall = potential_scr[first : first + together, :].T
        for i in range(together):
            for l in range(slots):
                score = tall[:, i : i + 1] + work_ref[first + i, l]
                peak = jnp.max(score, axis=0, keepdims=True)
                total = jnp.sum(jnp.exp2(score - peak), axis=0, keepdims=True)
                place = (first + i) * slots + l
                peak_scr[place : place + 1, :] = peak
                sum_scr[place : place + 1, :] = total
    select = select_ref[...]
    peaks = peak_scr[...]
    sums = sum_scr[...]
    blocks = out_ref.shape[0] // copies
    for t in range(blocks):
        chosen = select == t
        peak = jnp.max(jnp.where(chosen, peaks, very_low), axis=0, keepdims=True)
        shifted = jnp.where(chosen, sums * jnp.exp2(jnp.minimum(peaks - peak, 0.0)), 0.0)
        total = jnp.sum(shifted, axis=0, keepdims=True)
        some = total > 0.0
        out_ref[t : t + 1, :] = jnp.where(
            some, peak + jnp.log2(jnp.where(some, total, 1.0)), very_low
        )
    if copies > 1:
        put_copies(out_ref, copies, out_ref[0:blocks, :])


def row_kernel(
    row_devices, slot_ref, tall_ref, log_mass_ref, parts_ref, out_ref, wide_scr, peak_scr, sum_scr
):
    rows, slots, width, _ = tall_ref.shape
    potential = (log_mass_ref[...] - log_sum(parts_of(parts_ref, row_devices))).T
    for t in range(wide_scr.shape[0]):
        wide_scr[t] = jnp.broadcast_to(potential[:, t : t + 1], (width, width))

    for row in range(rows):
        scores = [wide_scr[slot_ref[l, row]] + tall_ref[row, l] for l in range(slots)]
        row_pass(scores, row, rows, peak_scr, sum_scr)
    out_ref[...] = row_sums(rows, peak_scr, sum_scr)


def last_kernel(row_devices, row_axis, log_mass_ref, parts_ref, out_ref):
    here = out_ref.shape[0]
    start = lax.axis_index(row_axis) * here
    log_mass = log_mass_ref[pl.ds(start, here), :]
    out_ref[...] = (log_mass - log_sum(parts_of(parts_ref, row_devices))) * from_log2


def per_device(
    coupling,
    coupling_index,
    near_cost,
    near_index,
    source_weights,
    target_cost,
    target_index,
    target_weights,
):
    rows_here = coupling.shape[0]
    slots = coupling.shape[2]
    width = coupling.shape[3]
    near_count = near_cost.shape[1]
    group_blocks = target_index.shape[1]
    link_count = target_index.shape[2]
    target_here = target_cost.shape[1]
    row_devices = lax.axis_size("rows")
    col_devices = lax.axis_size("cols")
    source_count = rows_here * row_devices * width
    target_count = group_blocks * width * col_devices
    f32 = jnp.float32
    half = row_devices // 2
    arrived = {0: target_cost}
    for mask in range(1, half + 1):
        arrived[mask] = send(target_cost, "rows", mask)

    near_t = in_hbm(near_index.T)
    slot_t = in_hbm(coupling_index[:, 0, :].T)
    link_t = in_hbm(jnp.transpose(target_index, (2, 0, 1)))
    mass = in_hbm(source_weights.reshape(rows_here, width))
    small = pltpu.CompilerParams(vmem_limit_bytes=4 * mib)

    pack_rows = 1 + target_here
    devices = row_devices * col_devices
    pack = pl.pallas_call(
        functools.partial(pack_kernel, devices),
        in_specs=[VMEM, VMEM],
        out_shape=jax.ShapeDtypeStruct((devices * pack_rows, width), f32),
        compiler_params=small,
        name="pack",
    )(mass, in_hbm(target_weights.reshape(target_here, width)))
    packs = exchange(pack, ("rows", "cols"))

    direct = list(range(1, half + 1))
    passed = pl.pallas_call(
        relay_kernel,
        in_specs=[ANY] * half,
        out_specs=[ANY] * half,
        out_shape=[jax.ShapeDtypeStruct(target_cost.shape, f32)] * half,
        input_output_aliases={e: e for e in range(half)},
        compiler_params=small,
        cost_estimate=pl.CostEstimate(flops=10**11, bytes_accessed=256 * mib, transcendentals=0),
        name="relay",
    )(*[arrived[mask] for mask in direct])
    arrived.update(zip(direct, passed))
    for mask in range(half + 1, row_devices):
        arrived[mask] = send(arrived[half], "rows", mask - half)
    cost_parts = [arrived[s] for s in range(row_devices)]

    wide = near_count * slots * width
    groups = rows_here // SUB
    step_rows = 2 * SUB if groups % 2 == 0 else SUB
    x, term = pl.pallas_call(
        near_kernel,
        grid=(rows_here // step_rows,),
        in_specs=[
            SMEM,
            pl.BlockSpec((step_rows, near_count, width, width), lambda g: (g, 0, 0, 0)),
            pl.BlockSpec((step_rows, 1, slots, width, width), lambda g: (g, 0, 0, 0, 0)),
            whole((rows_here, width)),
            ANY,
        ],
        out_specs=[VMEM, VMEM],
        out_shape=[
            pltpu.VMEM((rows_here, 2 * width, wide), jnp.bfloat16),
            pltpu.VMEM((groups, width, SUB), f32),
        ],
        scratch_shapes=[pltpu.VMEM((step_rows, 3 * width, slots * width), jnp.bfloat16)],
        compiler_params=pltpu.CompilerParams(vmem_limit_bytes=12 * mib),
        cost_estimate=pl.CostEstimate(
            flops=6 * rows_here * wide * width * width,
            bytes_accessed=4 * rows_here * width * (near_count + slots) * width,
            transcendentals=0,
        ),
        name="near_product",
    )(near_t, in_hbm(near_cost), in_hbm(coupling), mass, packs)

    far_bytes = group_blocks * link_count * width * width * 4
    far_rows = 2 * step_rows if rows_here % (2 * step_rows) == 0 else step_rows
    steps = rows_here // far_rows
    cost_block = pl.BlockSpec((far_rows, 1, slots, width, width), lambda g: (g, 0, 0, 0, 0))
    work_shape = pltpu.VMEM((rows_here, slots, width, width), f32)
    cost_blocks, work, tall, row_part, log_source, log_target, select = pl.pallas_call(
        functools.partial(
            far_kernel,
            (row_devices, col_devices, target_here, source_count, target_count, group_blocks, link_count),
            "rows",
            "cols",
        ),
        grid=(steps,),
        in_specs=[SMEM, SMEM, SMEM, VMEM, VMEM, whole((rows_here, width))]
        + [VMEM] * row_devices
        + [whole(packs.shape)],
        out_specs=[
            cost_block,
            VMEM,
            VMEM,
            whole((rows_here, width)),
            whole((rows_here, width)),
            whole((group_blocks, width)),
            whole((rows_here * slots, width)),
        ],
        out_shape=[
            jax.ShapeDtypeStruct(coupling.shape, f32),
            work_shape,
            work_shape,
            jax.ShapeDtypeStruct((rows_here, width), f32),
            jax.ShapeDtypeStruct((rows_here, width), f32),
            jax.ShapeDtypeStruct((group_blocks, width), f32),
            jax.ShapeDtypeStruct((rows_here * slots, width), jnp.int32),
        ],
        scratch_shapes=[
            pltpu.VMEM((group_blocks * link_count + 1, width, width), jnp.bfloat16),
            pltpu.VMEM((group_blocks * link_count + 1, width, width), jnp.bfloat16),
            pltpu.SMEM((group_blocks * group_blocks,), jnp.int32),
            pltpu.VMEM((group_blocks, width), f32),
            pltpu.VMEM((1, width), f32),
            pltpu.VMEM((slots * rows_here, width), f32),
            pltpu.VMEM((slots * rows_here, width), f32),
        ],
        compiler_params=pltpu.CompilerParams(vmem_limit_bytes=12 * mib + 2 * far_bytes),
        name="far_product",
    )(near_t, slot_t, link_t, in_vmem(x), in_vmem(term), mass, *cost_parts, packs)

    pass_params = pltpu.CompilerParams(vmem_limit_bytes=12 * mib)

    def column_step(row_parts, copies):
        return pl.pallas_call(
            functools.partial(column_kernel, copies),
            in_specs=[VMEM] * (3 + len(row_parts)),
            out_specs=[VMEM, VMEM],
            out_shape=[
                jax.ShapeDtypeStruct((copies * group_blocks, width), f32),
                jax.ShapeDtypeStruct((rows_here, width), f32),
            ],
            scratch_shapes=[
                pltpu.VMEM((rows_here, width), f32),
                pltpu.VMEM((rows_here * slots, width), f32),
                pltpu.VMEM((rows_here * slots, width), f32),
            ],
            compiler_params=pass_params,
            name="column_pass",
        )(in_vmem(work), select, log_source, *row_parts)

    def row_step(column_parts):
        return pl.pallas_call(
            functools.partial(row_kernel, row_devices),
            in_specs=[SMEM, VMEM, VMEM, VMEM],
            out_specs=VMEM,
            out_shape=jax.ShapeDtypeStruct((rows_here, width), f32),
            scratch_shapes=[
                pltpu.VMEM((group_blocks, width, width), f32),
                pltpu.VMEM((slots * rows_here, width), f32),
                pltpu.VMEM((slots * rows_here, width), f32),
            ],
            compiler_params=pass_params,
            name="row_pass",
        )(slot_t, in_vmem(tall), log_target, column_parts)

    for step in range(ITERS):
        last = step == ITERS - 1
        column_part, source_potential = column_step(
            from_all(row_part, "cols"), 1 if last else row_devices
        )
        column_parts = exchange(column_part, "rows")
        if not last:
            row_part = row_step(column_parts)
    own_target = pl.pallas_call(
        functools.partial(last_kernel, row_devices, "rows"),
        out_shape=jax.ShapeDtypeStruct((target_here, width), f32),
        compiler_params=small,
        name="last_potential",
    )(log_target, column_parts)
    return (
        cost_blocks,
        source_potential.reshape(rows_here * width),
        own_target.reshape(1, target_here * width),
    )


def solution(mesh):
    placed = (
        P("rows", "cols", None, None, None),
        P("rows", "cols", None),
        P("rows", None, None, None),
        P("rows", None),
        P("rows"),
        P("cols", "rows", None, None, None),
        P("cols", None, None),
        P("cols", "rows"),
    )
    return jax.shard_map(
        per_device,
        mesh=mesh,
        in_specs=placed,
        out_specs=(P("rows", "cols", None, None, None), P("rows"), P("cols", "rows")),
        check_vma=False,
    )
```

```python
import functools
import math

import jax
import jax.numpy as jnp
from jax import lax
from jax.experimental import pallas as pl
from jax.experimental.pallas import tpu as pltpu
from jax.sharding import PartitionSpec as P

ITERS = 3
SUB = 4

entropy = 0.01
to_log2 = math.log2(math.e) / entropy
from_log2 = entropy * math.log(2.0)
very_low = -1e30
mib = 1024 * 1024

SMEM = pl.BlockSpec(memory_space=pltpu.SMEM)
VMEM = pl.BlockSpec(memory_space=pltpu.VMEM)
ANY = pl.BlockSpec(memory_space=pl.ANY)


def in_hbm(x):
    return pltpu.with_memory_space_constraint(x, pltpu.HBM)


def in_vmem(x):
    return pltpu.with_memory_space_constraint(x, pltpu.VMEM)


def whole(shape):
    return pl.BlockSpec(shape, lambda *_: (0,) * len(shape))


def split(x):
    high = x.astype(jnp.bfloat16)
    return high, (x - high.astype(jnp.float32)).astype(jnp.bfloat16)


def tree(parts, op):
    while len(parts) > 1:
        half = len(parts) // 2
        parts = [op(parts[s], parts[s + half]) for s in range(half)]
    return parts[0]


def log_sum(parts):
    peak = tree(parts, jnp.maximum)
    return peak + jnp.log2(tree([jnp.exp2(p - peak) for p in parts], jnp.add))


def parts_of(ref, devices):
    rows = ref.shape[0] // devices
    return [ref[d * rows : (d + 1) * rows, :] for d in range(devices)]


def put_copies(ref, devices, value):
    rows = value.shape[0]
    for d in range(devices):
        ref[d * rows : (d + 1) * rows, :] = value


def send(x, axis, mask):
    size = lax.axis_size(axis)
    return lax.ppermute(x, axis, [(d, d ^ mask) for d in range(size)])


def from_all(x, axis):
    return [x] + [send(x, axis, s) for s in range(1, lax.axis_size(axis))]


def exchange(copies, axis):
    return lax.all_to_all(copies, axis, 0, 0, tiled=True)


def pack_kernel(devices, source_ref, target_ref, *refs):
    small = (len(refs) - 1) // 2
    out_ref = refs[small]
    rows = out_ref.shape[0] // devices
    total = jnp.sum(source_ref[...].astype(jnp.float32), axis=(0, 1), keepdims=True)
    target = target_ref[...].astype(jnp.float32)
    for d in range(devices):
        out_ref[d * rows : d * rows + 1, :] = jnp.broadcast_to(total, (1, out_ref.shape[1]))
        out_ref[d * rows + 1 : d * rows + 1 + target.shape[0], :] = target
    for from_ref, to_ref in zip(refs[:small], refs[small + 1 :]):
        to_ref[...] = from_ref[...]


def near_kernel(near_index_ref, cost_ref, plan_ref, mass_ref, totals_ref, x_ref, term_ref, plan_scr):
    rows = cost_ref.shape[0]
    first = pl.program_id(0) * rows
    near_count = cost_ref.shape[1]
    width = cost_ref.shape[2]
    slots = plan_ref.shape[2]
    wide = slots * width
    for a in range(rows):
        plan = jnp.concatenate([plan_ref[a, 0, q] for q in range(slots)], axis=1)
        high, low = split(plan)
        plan_scr[a, 0:width, :] = high
        plan_scr[a, width : 2 * width, :] = low
        plan_scr[a, 2 * width : 3 * width, :] = high
    lanes = lax.broadcasted_iota(jnp.int32, (width, SUB), 1)
    for group in range(rows // SUB):
        terms = jnp.zeros((width, SUB), jnp.float32)
        for i in range(group * SUB, (group + 1) * SUB):
            acc = None
            for k in range(near_count):
                a = group * SUB + (near_index_ref[k, first + i] & (SUB - 1))
                cost = cost_ref[i, k]
                high, low = split(cost)
                x = jnp.dot(
                    jnp.concatenate([high, high, low], axis=1),
                    plan_scr[a],
                    preferred_element_type=jnp.float32,
                )
                x_high, x_low = split(x)
                x_ref[first + i, 0:width, k * wide : (k + 1) * wide] = x_high
                x_ref[first + i, width : 2 * width, k * wide : (k + 1) * wide] = x_low
                weighted = cost * cost * mass_ref[pl.ds(first + a, 1), :].astype(jnp.float32)
                acc = weighted if acc is None else acc + weighted
            terms = jnp.where(lanes == i % SUB, jnp.sum(acc, axis=1, keepdims=True), terms)
        term_ref[first // SUB + group] = terms


def relay_kernel(*refs):
    pass


def far_kernel(counts, row_axis, col_axis, *refs):
    row_devices, col_devices, target_here, source_count, target_count, group_blocks, link_count = counts
    near_index_ref, slot_ref, link_ref, x_ref, term_ref, mass_ref = refs[:6]
    cost_parts = refs[6 : 6 + row_devices]
    pack_ref, out_ref, work_ref, tall_ref, part_ref, log_source_ref, log_target_ref, select_ref = refs[
        6 + row_devices : 14 + row_devices
    ]
    far_high, far_low, table, column_scr, scale_scr, peak_scr, sum_scr = refs[14 + row_devices :]
    g = pl.program_id(0)
    near_count = near_index_ref.shape[0]
    slots = slot_ref.shape[0]
    rows = out_ref.shape[0]
    width = out_ref.shape[3]
    zero_block = group_blocks * link_count

    @pl.when(g == 0)
    def _():
        me = lax.axis_index(row_axis)
        col = lax.axis_index(col_axis)
        far_high[zero_block] = jnp.zeros((width, width), jnp.bfloat16)
        far_low[zero_block] = jnp.zeros((width, width), jnp.bfloat16)

        def clear(e, _):
            table[e] = zero_block
            return 0

        lax.fori_loop(0, group_blocks * group_blocks, clear, 0)

        def mark(j, _):
            for m in range(link_count):
                table[j * group_blocks + link_ref[m, 0, j]] = j * link_count + m
            return 0

        lax.fori_loop(0, group_blocks, mark, 0)
        pack_rows = pack_ref.shape[0] // (row_devices * col_devices)
        total_source = functools.reduce(
            jnp.add,
            [pack_ref[r * col_devices * pack_rows : r * col_devices * pack_rows + 1, :] for r in range(row_devices)],
        )
        targets = functools.reduce(
            jnp.add,
            [
                pack_ref[d * pack_rows + 1 + h : d * pack_rows + 2 + h, :]
                for d in range(row_devices * col_devices)
                for h in range(target_here)
            ],
        )
        total_target = jnp.sum(targets, axis=1, keepdims=True)
        log_source_ref[...] = jnp.log2(source_count * mass_ref[...].astype(jnp.float32) / total_source)
        scale_scr[...] = source_count / (total_source * (near_count * width))
        column_scr[...] = jnp.zeros_like(column_scr)
        for s in range(row_devices):
            for h in range(target_here):
                j = (me ^ s) * target_here + h
                place = ((me ^ s) * col_devices + col) * pack_rows + 1 + h
                mass = target_count * pack_ref[pl.ds(place, 1), :] / total_target
                log_target_ref[pl.ds(j, 1), :] = jnp.log2(mass)
                tall = jnp.broadcast_to(mass, (width, width)).T
                for m in range(link_count):
                    block = cost_parts[s][0, h, m]
                    high, low = split(block)
                    far_high[j * link_count + m] = high
                    far_low[j * link_count + m] = low
                    spread = jnp.sum(tall * (block * block), axis=0, keepdims=True)
                    t = link_ref[m, 0, j]
                    column_scr[pl.ds(t, 1), :] += spread * (1.0 / (link_count * width))

    group_devices = target_count // (group_blocks * width)
    coef = 2.0 * (1.0 / (near_count * width)) * (1.0 / (slots * group_devices * width))
    scale = scale_scr[0:1, 0:1]
    for i in range(rows):
        row = g * rows + i
        group = row - lax.rem(row, SUB)
        targets = [slot_ref[l, row] for l in range(slots)]
        far_rows = []
        for k in range(near_count):
            a = group + (near_index_ref[k, row] & (SUB - 1))
            for q in range(slots):
                j = slot_ref[q, a]
                far_rows.append([table[j * group_blocks + t] for t in targets])
        right_high = jnp.concatenate(
            [jnp.concatenate([far_high[e] for e in r], axis=1) for r in far_rows], axis=0
        )
        right_low = jnp.concatenate(
            [jnp.concatenate([far_low[e] for e in r], axis=1) for r in far_rows], axis=0
        )
        both = jnp.dot(x_ref[row], right_high, preferred_element_type=jnp.float32)
        rest = jnp.dot(x_ref[row, 0:width, :], right_low, preferred_element_type=jnp.float32)
        product = both[0:width] + (both[width:] + rest)
        tall = term_ref[row // SUB, :, i % SUB : i % SUB + 1] * scale
        scores = []
        for l in range(slots):
            cost = tall + column_scr[pl.ds(targets[l], 1), :] - coef * product[:, l * width : (l + 1) * width]
            out_ref[i, 0, l] = cost
            select_ref[pl.ds(row * slots + l, 1), :] = jnp.full((1, width), targets[l], jnp.int32)
            scaled = cost * -to_log2
            work_ref[row, l] = scaled
            turned = scaled.T
            tall_ref[row, l] = turned
            scores.append(turned)
        row_pass(scores, row, part_ref.shape[0], peak_scr, sum_scr)

    @pl.when(g == pl.num_programs(0) - 1)
    def _():
        part_ref[...] = row_sums(part_ref.shape[0], peak_scr, sum_scr)


def row_pass(scores, row, rows, peak_scr, sum_scr):
    for l, score in enumerate(scores):
        peak = jnp.max(score, axis=0, keepdims=True)
        peak_scr[pl.ds(l * rows + row, 1), :] = peak
        sum_scr[pl.ds(l * rows + row, 1), :] = jnp.sum(jnp.exp2(score - peak), axis=0, keepdims=True)


def row_sums(rows, peak_scr, sum_scr):
    slots = peak_scr.shape[0] // rows
    peaks = [peak_scr[l * rows : (l + 1) * rows, :] for l in range(slots)]
    sums = [sum_scr[l * rows : (l + 1) * rows, :] for l in range(slots)]
    peak = functools.reduce(jnp.maximum, peaks)
    total = functools.reduce(jnp.add, [t * jnp.exp2(p - peak) for p, t in zip(peaks, sums)])
    return peak + jnp.log2(total)


def column_kernel(copies, work_ref, select_ref, log_mass_ref, *refs):
    parts = refs[:-4]
    out_ref, potential_scr, peak_scr, sum_scr = refs[-4:]
    rows, slots, width, _ = work_ref.shape
    together = math.gcd(rows, 8)
    potential_scr[...] = log_mass_ref[...] - log_sum([p[...] for p in parts])

    for first in range(0, rows, together):
        tall = potential_scr[first : first + together, :].T
        for i in range(together):
            for l in range(slots):
                score = tall[:, i : i + 1] + work_ref[first + i, l]
                peak = jnp.max(score, axis=0, keepdims=True)
                total = jnp.sum(jnp.exp2(score - peak), axis=0, keepdims=True)
                place = (first + i) * slots + l
                peak_scr[place : place + 1, :] = peak
                sum_scr[place : place + 1, :] = total
    select = select_ref[...]
    peaks = peak_scr[...]
    sums = sum_scr[...]
    blocks = out_ref.shape[0] // copies
    for t in range(blocks):
        chosen = select == t
        peak = jnp.max(jnp.where(chosen, peaks, very_low), axis=0, keepdims=True)
        shifted = jnp.where(chosen, sums * jnp.exp2(jnp.minimum(peaks - peak, 0.0)), 0.0)
        total = jnp.sum(shifted, axis=0, keepdims=True)
        some = total > 0.0
        out_ref[t : t + 1, :] = jnp.where(
            some, peak + jnp.log2(jnp.where(some, total, 1.0)), very_low
        )
    if copies > 1:
        put_copies(out_ref, copies, out_ref[0:blocks, :])


def row_kernel(
    row_devices, slot_ref, tall_ref, log_mass_ref, parts_ref, out_ref, wide_scr, peak_scr, sum_scr
):
    rows, slots, width, _ = tall_ref.shape
    potential = (log_mass_ref[...] - log_sum(parts_of(parts_ref, row_devices))).T
    for t in range(wide_scr.shape[0]):
        wide_scr[t] = jnp.broadcast_to(potential[:, t : t + 1], (width, width))

    for row in range(rows):
        scores = [wide_scr[slot_ref[l, row]] + tall_ref[row, l] for l in range(slots)]
        row_pass(scores, row, rows, peak_scr, sum_scr)
    out_ref[...] = row_sums(rows, peak_scr, sum_scr)


def last_kernel(row_devices, row_axis, log_target_ref, log_source_ref, column_ref, *refs):
    parts, (source_ref, target_ref) = refs[:-2], refs[-2:]
    source_ref[...] = (log_source_ref[...] - log_sum([p[...] for p in parts])) * from_log2
    here = target_ref.shape[0]
    start = lax.axis_index(row_axis) * here
    log_mass = log_target_ref[pl.ds(start, here), :]
    target_ref[...] = (log_mass - log_sum(parts_of(column_ref, row_devices))) * from_log2


def per_device(
    coupling,
    coupling_index,
    near_cost,
    near_index,
    source_weights,
    target_cost,
    target_index,
    target_weights,
):
    rows_here = coupling.shape[0]
    slots = coupling.shape[2]
    width = coupling.shape[3]
    near_count = near_cost.shape[1]
    group_blocks = target_index.shape[1]
    link_count = target_index.shape[2]
    target_here = target_cost.shape[1]
    row_devices = lax.axis_size("rows")
    col_devices = lax.axis_size("cols")
    source_count = rows_here * row_devices * width
    target_count = group_blocks * width * col_devices
    f32 = jnp.float32
    half = row_devices // 2
    arrived = {0: target_cost}
    for mask in range(1, half + 1):
        arrived[mask] = send(target_cost, "rows", mask)

    near_t = in_hbm(near_index.T)
    slot_t = in_hbm(coupling_index[:, 0, :].T)
    link_t = in_hbm(jnp.transpose(target_index, (2, 0, 1)))
    mass = in_hbm(source_weights.reshape(rows_here, width))
    small = pltpu.CompilerParams(vmem_limit_bytes=4 * mib)

    pack_rows = 1 + target_here
    devices = row_devices * col_devices
    handed = [near_t, slot_t, link_t, mass]
    pack, near_t, slot_t, link_t, mass = pl.pallas_call(
        functools.partial(pack_kernel, devices),
        in_specs=[VMEM] * (2 + len(handed)),
        out_specs=[VMEM] * (1 + len(handed)),
        out_shape=[jax.ShapeDtypeStruct((devices * pack_rows, width), f32)]
        + [jax.ShapeDtypeStruct(a.shape, a.dtype) for a in handed],
        compiler_params=small,
        name="pack",
    )(mass, in_hbm(target_weights.reshape(target_here, width)), *handed)
    packs = exchange(pack, ("rows", "cols"))

    direct = list(range(1, half + 1))
    passed = pl.pallas_call(
        relay_kernel,
        in_specs=[ANY] * half,
        out_specs=[ANY] * half,
        out_shape=[jax.ShapeDtypeStruct(target_cost.shape, f32)] * half,
        input_output_aliases={e: e for e in range(half)},
        compiler_params=small,
        cost_estimate=pl.CostEstimate(flops=10**11, bytes_accessed=256 * mib, transcendentals=0),
        name="relay",
    )(*[arrived[mask] for mask in direct])
    arrived.update(zip(direct, passed))
    for mask in range(half + 1, row_devices):
        arrived[mask] = send(arrived[half], "rows", mask - half)
    cost_parts = [arrived[s] for s in range(row_devices)]

    wide = near_count * slots * width
    groups = rows_here // SUB
    step_rows = 2 * SUB if groups % 2 == 0 else SUB
    x, term = pl.pallas_call(
        near_kernel,
        grid=(rows_here // step_rows,),
        in_specs=[
            SMEM,
            pl.BlockSpec((step_rows, near_count, width, width), lambda g: (g, 0, 0, 0)),
            pl.BlockSpec((step_rows, 1, slots, width, width), lambda g: (g, 0, 0, 0, 0)),
            whole((rows_here, width)),
            ANY,
        ],
        out_specs=[VMEM, VMEM],
        out_shape=[
            pltpu.VMEM((rows_here, 2 * width, wide), jnp.bfloat16),
            pltpu.VMEM((groups, width, SUB), f32),
        ],
        scratch_shapes=[pltpu.VMEM((step_rows, 3 * width, slots * width), jnp.bfloat16)],
        compiler_params=pltpu.CompilerParams(vmem_limit_bytes=12 * mib),
        cost_estimate=pl.CostEstimate(
            flops=6 * rows_here * wide * width * width,
            bytes_accessed=4 * rows_here * width * (near_count + slots) * width,
            transcendentals=0,
        ),
        name="near_product",
    )(near_t, in_hbm(near_cost), in_hbm(coupling), mass, packs)

    far_bytes = group_blocks * link_count * width * width * 4
    far_rows = 2 * step_rows if rows_here % (2 * step_rows) == 0 else step_rows
    steps = rows_here // far_rows
    cost_block = pl.BlockSpec((far_rows, 1, slots, width, width), lambda g: (g, 0, 0, 0, 0))
    work_shape = pltpu.VMEM((rows_here, slots, width, width), f32)
    cost_blocks, work, tall, row_part, log_source, log_target, select = pl.pallas_call(
        functools.partial(
            far_kernel,
            (row_devices, col_devices, target_here, source_count, target_count, group_blocks, link_count),
            "rows",
            "cols",
        ),
        grid=(steps,),
        in_specs=[SMEM, SMEM, SMEM, VMEM, VMEM, whole((rows_here, width))]
        + [VMEM] * row_devices
        + [whole(packs.shape)],
        out_specs=[
            cost_block,
            VMEM,
            VMEM,
            whole((rows_here, width)),
            whole((rows_here, width)),
            whole((group_blocks, width)),
            whole((rows_here * slots, width)),
        ],
        out_shape=[
            jax.ShapeDtypeStruct(coupling.shape, f32),
            work_shape,
            work_shape,
            jax.ShapeDtypeStruct((rows_here, width), f32),
            jax.ShapeDtypeStruct((rows_here, width), f32),
            jax.ShapeDtypeStruct((group_blocks, width), f32),
            jax.ShapeDtypeStruct((rows_here * slots, width), jnp.int32),
        ],
        scratch_shapes=[
            pltpu.VMEM((group_blocks * link_count + 1, width, width), jnp.bfloat16),
            pltpu.VMEM((group_blocks * link_count + 1, width, width), jnp.bfloat16),
            pltpu.SMEM((group_blocks * group_blocks,), jnp.int32),
            pltpu.VMEM((group_blocks, width), f32),
            pltpu.VMEM((1, width), f32),
            pltpu.VMEM((slots * rows_here, width), f32),
            pltpu.VMEM((slots * rows_here, width), f32),
        ],
        compiler_params=pltpu.CompilerParams(vmem_limit_bytes=12 * mib + 2 * far_bytes),
        name="far_product",
    )(near_t, slot_t, link_t, in_vmem(x), in_vmem(term), mass, *cost_parts, packs)

    pass_params = pltpu.CompilerParams(vmem_limit_bytes=12 * mib)

    def column_step(row_parts, copies):
        return pl.pallas_call(
            functools.partial(column_kernel, copies),
            in_specs=[VMEM] * (3 + len(row_parts)),
            out_specs=VMEM,
            out_shape=jax.ShapeDtypeStruct((copies * group_blocks, width), f32),
            scratch_shapes=[
                pltpu.VMEM((rows_here, width), f32),
                pltpu.VMEM((rows_here * slots, width), f32),
                pltpu.VMEM((rows_here * slots, width), f32),
            ],
            compiler_params=pass_params,
            name="column_pass",
        )(in_vmem(work), select, log_source, *row_parts)

    def row_step(column_parts):
        return pl.pallas_call(
            functools.partial(row_kernel, row_devices),
            in_specs=[SMEM, VMEM, VMEM, VMEM],
            out_specs=VMEM,
            out_shape=jax.ShapeDtypeStruct((rows_here, width), f32),
            scratch_shapes=[
                pltpu.VMEM((group_blocks, width, width), f32),
                pltpu.VMEM((slots * rows_here, width), f32),
                pltpu.VMEM((slots * rows_here, width), f32),
            ],
            compiler_params=pass_params,
            name="row_pass",
        )(slot_t, in_vmem(tall), log_target, column_parts)

    for step in range(ITERS):
        last = step == ITERS - 1
        row_parts = from_all(row_part, "cols")
        column_parts = exchange(column_step(row_parts, 1 if last else row_devices), "rows")
        if not last:
            row_part = row_step(column_parts)
    source_potential, own_target = pl.pallas_call(
        functools.partial(last_kernel, row_devices, "rows"),
        out_shape=[
            jax.ShapeDtypeStruct((rows_here, width), f32),
            jax.ShapeDtypeStruct((target_here, width), f32),
        ],
        compiler_params=small,
        name="last_potential",
    )(log_target, log_source, column_parts, *row_parts)
    return (
        cost_blocks,
        source_potential.reshape(rows_here * width),
        own_target.reshape(1, target_here * width),
    )


def solution(mesh):
    placed = (
        P("rows", "cols", None, None, None),
        P("rows", "cols", None),
        P("rows", None, None, None),
        P("rows", None),
        P("rows"),
        P("cols", "rows", None, None, None),
        P("cols", None, None),
        P("cols", "rows"),
    )
    return jax.shard_map(
        per_device,
        mesh=mesh,
        in_specs=placed,
        out_specs=(P("rows", "cols", None, None, None), P("rows"), P("cols", "rows")),
        check_vma=False,
    )
```

```python
import functools
import math

import jax
import jax.numpy as jnp
from jax import lax
from jax.experimental import pallas as pl
from jax.experimental.pallas import tpu as pltpu
from jax.sharding import PartitionSpec as P

ITERS = 3
SUB = 4

entropy = 0.01
to_log2 = math.log2(math.e) / entropy
from_log2 = entropy * math.log(2.0)
very_low = -1e30
mib = 1024 * 1024

SMEM = pl.BlockSpec(memory_space=pltpu.SMEM)
VMEM = pl.BlockSpec(memory_space=pltpu.VMEM)
ANY = pl.BlockSpec(memory_space=pl.ANY)


def in_hbm(x):
    return pltpu.with_memory_space_constraint(x, pltpu.HBM)


def in_vmem(x):
    return pltpu.with_memory_space_constraint(x, pltpu.VMEM)


def whole(shape):
    return pl.BlockSpec(shape, lambda *_: (0,) * len(shape))


def split(x):
    high = x.astype(jnp.bfloat16)
    return high, (x - high.astype(jnp.float32)).astype(jnp.bfloat16)


def tree(parts, op):
    while len(parts) > 1:
        half = len(parts) // 2
        parts = [op(parts[s], parts[s + half]) for s in range(half)]
    return parts[0]


def log_sum(parts):
    peak = tree(parts, jnp.maximum)
    return peak + jnp.log2(tree([jnp.exp2(p - peak) for p in parts], jnp.add))


def parts_of(ref, devices):
    rows = ref.shape[0] // devices
    return [ref[d * rows : (d + 1) * rows, :] for d in range(devices)]


def put_copies(ref, devices, value):
    rows = value.shape[0]
    for d in range(devices):
        ref[d * rows : (d + 1) * rows, :] = value


def send(x, axis, mask):
    size = lax.axis_size(axis)
    return lax.ppermute(x, axis, [(d, d ^ mask) for d in range(size)])


def from_all(x, axis):
    return [x] + [send(x, axis, s) for s in range(1, lax.axis_size(axis))]


def exchange(copies, axis):
    return lax.all_to_all(copies, axis, 0, 0, tiled=True)


def pack_kernel(devices, source_ref, target_ref, *refs):
    small = (len(refs) - 1) // 2
    out_ref = refs[small]
    rows = out_ref.shape[0] // devices
    total = jnp.sum(source_ref[...].astype(jnp.float32), axis=(0, 1), keepdims=True)
    target = target_ref[...].astype(jnp.float32)
    for d in range(devices):
        out_ref[d * rows : d * rows + 1, :] = jnp.broadcast_to(total, (1, out_ref.shape[1]))
        out_ref[d * rows + 1 : d * rows + 1 + target.shape[0], :] = target
    for from_ref, to_ref in zip(refs[:small], refs[small + 1 :]):
        to_ref[...] = from_ref[...]


def near_kernel(near_index_ref, cost_ref, plan_ref, mass_ref, totals_ref, x_ref, term_ref, plan_scr):
    rows = cost_ref.shape[0]
    first = pl.program_id(0) * rows
    near_count = cost_ref.shape[1]
    width = cost_ref.shape[2]
    slots = plan_ref.shape[2]
    wide = slots * width
    for a in range(rows):
        plan = jnp.concatenate([plan_ref[a, 0, q] for q in range(slots)], axis=1)
        high, low = split(plan)
        plan_scr[a, 0:width, :] = high
        plan_scr[a, width : 2 * width, :] = low
        plan_scr[a, 2 * width : 3 * width, :] = high
    lanes = lax.broadcasted_iota(jnp.int32, (width, SUB), 1)
    for group in range(rows // SUB):
        terms = jnp.zeros((width, SUB), jnp.float32)
        for i in range(group * SUB, (group + 1) * SUB):
            acc = None
            for k in range(near_count):
                a = group * SUB + (near_index_ref[k, first + i] & (SUB - 1))
                cost = cost_ref[i, k]
                high, low = split(cost)
                x = jnp.dot(
                    jnp.concatenate([high, high, low], axis=1),
                    plan_scr[a],
                    preferred_element_type=jnp.float32,
                )
                x_high, x_low = split(x)
                x_ref[first + i, 0:width, k * wide : (k + 1) * wide] = x_high
                x_ref[first + i, width : 2 * width, k * wide : (k + 1) * wide] = x_low
                weighted = cost * cost * mass_ref[pl.ds(first + a, 1), :].astype(jnp.float32)
                acc = weighted if acc is None else acc + weighted
            terms = jnp.where(lanes == i % SUB, jnp.sum(acc, axis=1, keepdims=True), terms)
        term_ref[first // SUB + group] = terms


def relay_kernel(*refs):
    pass


def far_kernel(counts, row_axis, col_axis, *refs):
    row_devices, col_devices, target_here, source_count, target_count, group_blocks, link_count = counts
    near_index_ref, slot_ref, link_ref, x_ref, term_ref, mass_ref = refs[:6]
    cost_parts = refs[6 : 6 + row_devices]
    pack_ref, out_ref, work_ref, tall_ref, part_ref, log_source_ref, log_target_ref, select_ref = refs[
        6 + row_devices : 14 + row_devices
    ]
    far_high, far_low, table, column_scr, scale_scr, peak_scr, sum_scr, cost_scr, sems = refs[14 + row_devices :]
    g = pl.program_id(0)
    near_count = near_index_ref.shape[0]
    slots = slot_ref.shape[0]
    all_rows = out_ref.shape[0]
    rows = all_rows // pl.num_programs(0)
    width = out_ref.shape[3]
    zero_block = group_blocks * link_count

    @pl.when(g == 0)
    def _():
        me = lax.axis_index(row_axis)
        col = lax.axis_index(col_axis)
        far_high[zero_block] = jnp.zeros((width, width), jnp.bfloat16)
        far_low[zero_block] = jnp.zeros((width, width), jnp.bfloat16)

        def clear(e, _):
            table[e] = zero_block
            return 0

        lax.fori_loop(0, group_blocks * group_blocks, clear, 0)

        def mark(j, _):
            for m in range(link_count):
                table[j * group_blocks + link_ref[m, 0, j]] = j * link_count + m
            return 0

        lax.fori_loop(0, group_blocks, mark, 0)
        pack_rows = pack_ref.shape[0] // (row_devices * col_devices)
        total_source = functools.reduce(
            jnp.add,
            [pack_ref[r * col_devices * pack_rows : r * col_devices * pack_rows + 1, :] for r in range(row_devices)],
        )
        targets = functools.reduce(
            jnp.add,
            [
                pack_ref[d * pack_rows + 1 + h : d * pack_rows + 2 + h, :]
                for d in range(row_devices * col_devices)
                for h in range(target_here)
            ],
        )
        total_target = jnp.sum(targets, axis=1, keepdims=True)
        log_source_ref[...] = jnp.log2(source_count * mass_ref[...].astype(jnp.float32) / total_source)
        scale_scr[...] = source_count / (total_source * (near_count * width))
        column_scr[...] = jnp.zeros_like(column_scr)
        for s in range(row_devices):
            for h in range(target_here):
                j = (me ^ s) * target_here + h
                place = ((me ^ s) * col_devices + col) * pack_rows + 1 + h
                mass = target_count * pack_ref[pl.ds(place, 1), :] / total_target
                log_target_ref[pl.ds(j, 1), :] = jnp.log2(mass)
                tall = jnp.broadcast_to(mass, (width, width)).T
                for m in range(link_count):
                    block = cost_parts[s][0, h, m]
                    high, low = split(block)
                    far_high[j * link_count + m] = high
                    far_low[j * link_count + m] = low
                    spread = jnp.sum(tall * (block * block), axis=0, keepdims=True)
                    t = link_ref[m, 0, j]
                    column_scr[pl.ds(t, 1), :] += spread * (1.0 / (link_count * width))

    def out_copy(row):
        return pltpu.make_async_copy(cost_scr.at[row], out_ref.at[row], sems.at[row])

    group_devices = target_count // (group_blocks * width)
    coef = 2.0 * (1.0 / (near_count * width)) * (1.0 / (slots * group_devices * width))
    scale = scale_scr[0:1, 0:1]
    for i in range(rows):
        row = g * rows + i
        group = row - lax.rem(row, SUB)
        targets = [slot_ref[l, row] for l in range(slots)]
        far_rows = []
        for k in range(near_count):
            a = group + (near_index_ref[k, row] & (SUB - 1))
            for q in range(slots):
                j = slot_ref[q, a]
                far_rows.append([table[j * group_blocks + t] for t in targets])
        right_high = jnp.concatenate(
            [jnp.concatenate([far_high[e] for e in r], axis=1) for r in far_rows], axis=0
        )
        right_low = jnp.concatenate(
            [jnp.concatenate([far_low[e] for e in r], axis=1) for r in far_rows], axis=0
        )
        both = jnp.dot(x_ref[row], right_high, preferred_element_type=jnp.float32)
        rest = jnp.dot(x_ref[row, 0:width, :], right_low, preferred_element_type=jnp.float32)
        product = both[0:width] + (both[width:] + rest)
        tall = term_ref[row // SUB, :, i % SUB : i % SUB + 1] * scale
        scores = []
        for l in range(slots):
            cost = tall + column_scr[pl.ds(targets[l], 1), :] - coef * product[:, l * width : (l + 1) * width]
            cost_scr[row, 0, l] = cost
            select_ref[pl.ds(row * slots + l, 1), :] = jnp.full((1, width), targets[l], jnp.int32)
            scaled = cost * -to_log2
            work_ref[row, l] = scaled
            turned = scaled.T
            tall_ref[row, l] = turned
            scores.append(turned)
        out_copy(row).start()
        row_pass(scores, row, part_ref.shape[0], peak_scr, sum_scr)

    @pl.when(g == pl.num_programs(0) - 1)
    def _():
        part_ref[...] = row_sums(part_ref.shape[0], peak_scr, sum_scr)
        for row in range(all_rows):
            out_copy(row).wait()


def row_pass(scores, row, rows, peak_scr, sum_scr):
    for l, score in enumerate(scores):
        peak = jnp.max(score, axis=0, keepdims=True)
        peak_scr[pl.ds(l * rows + row, 1), :] = peak
        sum_scr[pl.ds(l * rows + row, 1), :] = jnp.sum(jnp.exp2(score - peak), axis=0, keepdims=True)


def row_sums(rows, peak_scr, sum_scr):
    slots = peak_scr.shape[0] // rows
    peaks = [peak_scr[l * rows : (l + 1) * rows, :] for l in range(slots)]
    sums = [sum_scr[l * rows : (l + 1) * rows, :] for l in range(slots)]
    peak = functools.reduce(jnp.maximum, peaks)
    total = functools.reduce(jnp.add, [t * jnp.exp2(p - peak) for p, t in zip(peaks, sums)])
    return peak + jnp.log2(total)


def column_kernel(copies, work_ref, select_ref, log_mass_ref, *refs):
    parts = refs[:-5]
    out_ref, potential_ref, potential_scr, peak_scr, sum_scr = refs[-5:]
    rows, slots, width, _ = work_ref.shape
    together = math.gcd(rows, 8)
    scaled = log_mass_ref[...] - log_sum([p[...] for p in parts])
    potential_scr[...] = scaled
    potential_ref[...] = scaled * from_log2

    for first in range(0, rows, together):
        tall = potential_scr[first : first + together, :].T
        for i in range(together):
            for l in range(slots):
                score = tall[:, i : i + 1] + work_ref[first + i, l]
                peak = jnp.max(score, axis=0, keepdims=True)
                total = jnp.sum(jnp.exp2(score - peak), axis=0, keepdims=True)
                place = (first + i) * slots + l
                peak_scr[place : place + 1, :] = peak
                sum_scr[place : place + 1, :] = total
    select = select_ref[...]
    peaks = peak_scr[...]
    sums = sum_scr[...]
    blocks = out_ref.shape[0] // copies
    for t in range(blocks):
        chosen = select == t
        peak = jnp.max(jnp.where(chosen, peaks, very_low), axis=0, keepdims=True)
        shifted = jnp.where(chosen, sums * jnp.exp2(jnp.minimum(peaks - peak, 0.0)), 0.0)
        total = jnp.sum(shifted, axis=0, keepdims=True)
        some = total > 0.0
        out_ref[t : t + 1, :] = jnp.where(
            some, peak + jnp.log2(jnp.where(some, total, 1.0)), very_low
        )
    if copies > 1:
        put_copies(out_ref, copies, out_ref[0:blocks, :])


def row_kernel(
    row_devices, slot_any, tall_ref, log_mass_ref, parts_ref, out_ref, wide_scr, peak_scr, sum_scr, slot_ref, sem
):
    rows, slots, width, _ = tall_ref.shape
    slot_copy = pltpu.make_async_copy(slot_any, slot_ref, sem)
    slot_copy.start()
    potential = (log_mass_ref[...] - log_sum(parts_of(parts_ref, row_devices))).T
    for t in range(wide_scr.shape[0]):
        wide_scr[t] = jnp.broadcast_to(potential[:, t : t + 1], (width, width))

    slot_copy.wait()
    for row in range(rows):
        scores = [wide_scr[slot_ref[l, row]] + tall_ref[row, l] for l in range(slots)]
        row_pass(scores, row, rows, peak_scr, sum_scr)
    out_ref[...] = row_sums(rows, peak_scr, sum_scr)


def last_kernel(row_devices, row_axis, log_mass_ref, parts_ref, out_ref):
    here = out_ref.shape[0]
    start = lax.axis_index(row_axis) * here
    log_mass = log_mass_ref[pl.ds(start, here), :]
    out_ref[...] = (log_mass - log_sum(parts_of(parts_ref, row_devices))) * from_log2


def per_device(
    coupling,
    coupling_index,
    near_cost,
    near_index,
    source_weights,
    target_cost,
    target_index,
    target_weights,
):
    rows_here = coupling.shape[0]
    slots = coupling.shape[2]
    width = coupling.shape[3]
    near_count = near_cost.shape[1]
    group_blocks = target_index.shape[1]
    link_count = target_index.shape[2]
    target_here = target_cost.shape[1]
    row_devices = lax.axis_size("rows")
    col_devices = lax.axis_size("cols")
    source_count = rows_here * row_devices * width
    target_count = group_blocks * width * col_devices
    f32 = jnp.float32
    half = row_devices // 2
    arrived = {0: target_cost}
    for mask in range(1, half + 1):
        arrived[mask] = send(target_cost, "rows", mask)

    near_t = in_hbm(near_index.T)
    slot_t = in_hbm(coupling_index[:, 0, :].T)
    link_t = in_hbm(jnp.transpose(target_index, (2, 0, 1)))
    mass = in_hbm(source_weights.reshape(rows_here, width))
    small = pltpu.CompilerParams(vmem_limit_bytes=4 * mib)

    pack_rows = 1 + target_here
    devices = row_devices * col_devices
    handed = [near_t, slot_t, link_t, mass]
    pack, near_t, slot_t, link_t, mass = pl.pallas_call(
        functools.partial(pack_kernel, devices),
        in_specs=[VMEM] * (2 + len(handed)),
        out_specs=[VMEM] * (1 + len(handed)),
        out_shape=[jax.ShapeDtypeStruct((devices * pack_rows, width), f32)]
        + [jax.ShapeDtypeStruct(a.shape, a.dtype) for a in handed],
        compiler_params=small,
        name="pack",
    )(mass, in_hbm(target_weights.reshape(target_here, width)), *handed)
    packs = exchange(pack, ("rows", "cols"))

    direct = list(range(1, half + 1))
    passed = pl.pallas_call(
        relay_kernel,
        in_specs=[ANY] * half,
        out_specs=[ANY] * half,
        out_shape=[jax.ShapeDtypeStruct(target_cost.shape, f32)] * half,
        input_output_aliases={e: e for e in range(half)},
        compiler_params=small,
        cost_estimate=pl.CostEstimate(flops=10**11, bytes_accessed=256 * mib, transcendentals=0),
        name="relay",
    )(*[arrived[mask] for mask in direct])
    arrived.update(zip(direct, passed))
    for mask in range(half + 1, row_devices):
        arrived[mask] = send(arrived[half], "rows", mask - half)
    cost_parts = [arrived[s] for s in range(row_devices)]

    wide = near_count * slots * width
    groups = rows_here // SUB
    step_rows = 2 * SUB if groups % 2 == 0 else SUB
    x, term = pl.pallas_call(
        near_kernel,
        grid=(rows_here // step_rows,),
        in_specs=[
            SMEM,
            pl.BlockSpec((step_rows, near_count, width, width), lambda g: (g, 0, 0, 0)),
            pl.BlockSpec((step_rows, 1, slots, width, width), lambda g: (g, 0, 0, 0, 0)),
            whole((rows_here, width)),
            ANY,
        ],
        out_specs=[VMEM, VMEM],
        out_shape=[
            pltpu.VMEM((rows_here, 2 * width, wide), jnp.bfloat16),
            pltpu.VMEM((groups, width, SUB), f32),
        ],
        scratch_shapes=[pltpu.VMEM((step_rows, 3 * width, slots * width), jnp.bfloat16)],
        compiler_params=pltpu.CompilerParams(vmem_limit_bytes=12 * mib),
        cost_estimate=pl.CostEstimate(
            flops=6 * rows_here * wide * width * width,
            bytes_accessed=4 * rows_here * width * (near_count + slots) * width,
            transcendentals=0,
        ),
        name="near_product",
    )(near_t, in_hbm(near_cost), in_hbm(coupling), mass, packs)

    far_bytes = group_blocks * link_count * width * width * 4
    far_rows = 2 * step_rows if rows_here % (2 * step_rows) == 0 else step_rows
    steps = rows_here // far_rows
    work_shape = pltpu.VMEM((rows_here, slots, width, width), f32)
    cost_blocks, work, tall, row_part, log_source, log_target, select = pl.pallas_call(
        functools.partial(
            far_kernel,
            (row_devices, col_devices, target_here, source_count, target_count, group_blocks, link_count),
            "rows",
            "cols",
        ),
        grid=(steps,),
        in_specs=[SMEM, SMEM, SMEM, VMEM, VMEM, whole((rows_here, width))]
        + [VMEM] * row_devices
        + [whole(packs.shape)],
        out_specs=[
            ANY,
            VMEM,
            VMEM,
            whole((rows_here, width)),
            whole((rows_here, width)),
            whole((group_blocks, width)),
            whole((rows_here * slots, width)),
        ],
        out_shape=[
            pltpu.HBM(coupling.shape, f32),
            work_shape,
            work_shape,
            jax.ShapeDtypeStruct((rows_here, width), f32),
            jax.ShapeDtypeStruct((rows_here, width), f32),
            jax.ShapeDtypeStruct((group_blocks, width), f32),
            jax.ShapeDtypeStruct((rows_here * slots, width), jnp.int32),
        ],
        scratch_shapes=[
            pltpu.VMEM((group_blocks * link_count + 1, width, width), jnp.bfloat16),
            pltpu.VMEM((group_blocks * link_count + 1, width, width), jnp.bfloat16),
            pltpu.SMEM((group_blocks * group_blocks,), jnp.int32),
            pltpu.VMEM((group_blocks, width), f32),
            pltpu.VMEM((1, width), f32),
            pltpu.VMEM((slots * rows_here, width), f32),
            pltpu.VMEM((slots * rows_here, width), f32),
            pltpu.VMEM(coupling.shape, f32),
            pltpu.SemaphoreType.DMA((rows_here,)),
        ],
        compiler_params=pltpu.CompilerParams(vmem_limit_bytes=12 * mib + 2 * far_bytes),
        name="far_product",
    )(near_t, slot_t, link_t, in_vmem(x), in_vmem(term), mass, *cost_parts, packs)

    pass_params = pltpu.CompilerParams(vmem_limit_bytes=12 * mib)

    def column_step(row_parts, copies):
        return pl.pallas_call(
            functools.partial(column_kernel, copies),
            in_specs=[VMEM] * (3 + len(row_parts)),
            out_specs=[VMEM, VMEM],
            out_shape=[
                jax.ShapeDtypeStruct((copies * group_blocks, width), f32),
                jax.ShapeDtypeStruct((rows_here, width), f32),
            ],
            scratch_shapes=[
                pltpu.VMEM((rows_here, width), f32),
                pltpu.VMEM((rows_here * slots, width), f32),
                pltpu.VMEM((rows_here * slots, width), f32),
            ],
            compiler_params=pass_params,
            name="column_pass",
        )(in_vmem(work), select, log_source, *row_parts)

    def row_step(column_parts):
        return pl.pallas_call(
            functools.partial(row_kernel, row_devices),
            in_specs=[ANY, VMEM, VMEM, VMEM],
            out_specs=VMEM,
            out_shape=jax.ShapeDtypeStruct((rows_here, width), f32),
            scratch_shapes=[
                pltpu.VMEM((group_blocks, width, width), f32),
                pltpu.VMEM((slots * rows_here, width), f32),
                pltpu.VMEM((slots * rows_here, width), f32),
                pltpu.SMEM((slots, rows_here), jnp.int32),
                pltpu.SemaphoreType.DMA,
            ],
            compiler_params=pass_params,
            name="row_pass",
        )(slot_t, in_vmem(tall), log_target, column_parts)

    for step in range(ITERS):
        last = step == ITERS - 1
        column_part, source_potential = column_step(
            from_all(row_part, "cols"), 1 if last else row_devices
        )
        column_parts = exchange(column_part, "rows")
        if not last:
            row_part = row_step(column_parts)
    own_target = pl.pallas_call(
        functools.partial(last_kernel, row_devices, "rows"),
        out_shape=jax.ShapeDtypeStruct((target_here, width), f32),
        compiler_params=small,
        name="last_potential",
    )(log_target, column_parts)
    return (
        cost_blocks,
        source_potential.reshape(rows_here * width),
        own_target.reshape(1, target_here * width),
    )


def solution(mesh):
    placed = (
        P("rows", "cols", None, None, None),
        P("rows", "cols", None),
        P("rows", None, None, None),
        P("rows", None),
        P("rows"),
        P("cols", "rows", None, None, None),
        P("cols", None, None),
        P("cols", "rows"),
    )
    return jax.shard_map(
        per_device,
        mesh=mesh,
        in_specs=placed,
        out_specs=(P("rows", "cols", None, None, None), P("rows"), P("cols", "rows")),
        check_vma=False,
    )
```

```python
import functools
import math

import jax
import jax.numpy as jnp
from jax import lax
from jax.experimental import pallas as pl
from jax.experimental.pallas import tpu as pltpu
from jax.sharding import PartitionSpec as P

ITERS = 3
SUB = 4

entropy = 0.01
to_log2 = math.log2(math.e) / entropy
from_log2 = entropy * math.log(2.0)
very_low = -1e30
mib = 1024 * 1024

SMEM = pl.BlockSpec(memory_space=pltpu.SMEM)
VMEM = pl.BlockSpec(memory_space=pltpu.VMEM)
ANY = pl.BlockSpec(memory_space=pl.ANY)


def in_hbm(x):
    return pltpu.with_memory_space_constraint(x, pltpu.HBM)


def in_vmem(x):
    return pltpu.with_memory_space_constraint(x, pltpu.VMEM)


def whole(shape):
    return pl.BlockSpec(shape, lambda *_: (0,) * len(shape))


def split(x):
    high = x.astype(jnp.bfloat16)
    return high, (x - high.astype(jnp.float32)).astype(jnp.bfloat16)


def tree(parts, op):
    while len(parts) > 1:
        half = len(parts) // 2
        parts = [op(parts[s], parts[s + half]) for s in range(half)]
    return parts[0]


def log_sum(parts):
    peak = tree(parts, jnp.maximum)
    return peak + jnp.log2(tree([jnp.exp2(p - peak) for p in parts], jnp.add))


def parts_of(ref, devices):
    rows = ref.shape[0] // devices
    return [ref[d * rows : (d + 1) * rows, :] for d in range(devices)]


def put_copies(ref, devices, value):
    rows = value.shape[0]
    for d in range(devices):
        ref[d * rows : (d + 1) * rows, :] = value


def send(x, axis, mask):
    size = lax.axis_size(axis)
    return lax.ppermute(x, axis, [(d, d ^ mask) for d in range(size)])


def from_all(x, axis):
    return [x] + [send(x, axis, s) for s in range(1, lax.axis_size(axis))]


def exchange(copies, axis):
    return lax.all_to_all(copies, axis, 0, 0, tiled=True)


def pack_kernel(devices, source_ref, target_ref, *refs):
    small = (len(refs) - 1) // 2
    out_ref = refs[small]
    rows = out_ref.shape[0] // devices
    total = jnp.sum(source_ref[...].astype(jnp.float32), axis=(0, 1), keepdims=True)
    target = target_ref[...].astype(jnp.float32)
    for d in range(devices):
        out_ref[d * rows : d * rows + 1, :] = jnp.broadcast_to(total, (1, out_ref.shape[1]))
        out_ref[d * rows + 1 : d * rows + 1 + target.shape[0], :] = target
    for from_ref, to_ref in zip(refs[:small], refs[small + 1 :]):
        to_ref[...] = from_ref[...]


def near_kernel(
    near_any, cost_ref, plan_ref, mass_ref, totals_ref, x_ref, term_ref, plan_scr, near_index_ref, sem
):
    index_copy = pltpu.make_async_copy(near_any, near_index_ref, sem)
    pl.when(pl.program_id(0) == 0)(index_copy.start)
    rows = cost_ref.shape[0]
    first = pl.program_id(0) * rows
    near_count = cost_ref.shape[1]
    width = cost_ref.shape[2]
    slots = plan_ref.shape[2]
    wide = slots * width
    for a in range(rows):
        plan = jnp.concatenate([plan_ref[a, 0, q] for q in range(slots)], axis=1)
        high, low = split(plan)
        plan_scr[a, 0:width, :] = high
        plan_scr[a, width : 2 * width, :] = low
        plan_scr[a, 2 * width : 3 * width, :] = high
    pl.when(pl.program_id(0) == 0)(index_copy.wait)
    lanes = lax.broadcasted_iota(jnp.int32, (width, SUB), 1)
    for group in range(rows // SUB):
        terms = jnp.zeros((width, SUB), jnp.float32)
        for i in range(group * SUB, (group + 1) * SUB):
            acc = None
            for k in range(near_count):
                a = group * SUB + (near_index_ref[k, first + i] & (SUB - 1))
                cost = cost_ref[i, k]
                high, low = split(cost)
                x = jnp.dot(
                    jnp.concatenate([high, high, low], axis=1),
                    plan_scr[a],
                    preferred_element_type=jnp.float32,
                )
                x_high, x_low = split(x)
                x_ref[first + i, 0:width, k * wide : (k + 1) * wide] = x_high
                x_ref[first + i, width : 2 * width, k * wide : (k + 1) * wide] = x_low
                weighted = cost * cost * mass_ref[pl.ds(first + a, 1), :].astype(jnp.float32)
                acc = weighted if acc is None else acc + weighted
            terms = jnp.where(lanes == i % SUB, jnp.sum(acc, axis=1, keepdims=True), terms)
        term_ref[first // SUB + group] = terms


def relay_kernel(*refs):
    pass


def far_kernel(counts, row_axis, col_axis, *refs):
    row_devices, col_devices, target_here, source_count, target_count, group_blocks, link_count = counts
    tables, (x_ref, term_ref, mass_ref) = refs[:3], refs[3:6]
    cost_parts = refs[6 : 6 + row_devices]
    pack_ref, out_ref, work_ref, tall_ref, part_ref, log_source_ref, log_target_ref, select_ref = refs[
        6 + row_devices : 14 + row_devices
    ]
    far_high, far_low, table, column_scr, scale_scr, peak_scr, sum_scr, cost_scr, sems = refs[14 + row_devices : -4]
    near_index_ref, slot_ref, link_ref, table_sems = refs[-4:]
    g = pl.program_id(0)
    near_count = near_index_ref.shape[0]
    slots = slot_ref.shape[0]
    all_rows = out_ref.shape[0]
    rows = all_rows // pl.num_programs(0)
    width = out_ref.shape[3]
    zero_block = group_blocks * link_count

    @pl.when(g == 0)
    def _():
        table_copies = [
            pltpu.make_async_copy(table_any, table_ref, table_sems.at[e])
            for e, (table_any, table_ref) in enumerate(zip(tables, (near_index_ref, slot_ref, link_ref)))
        ]
        for copy in table_copies:
            copy.start()
        me = lax.axis_index(row_axis)
        col = lax.axis_index(col_axis)
        far_high[zero_block] = jnp.zeros((width, width), jnp.bfloat16)
        far_low[zero_block] = jnp.zeros((width, width), jnp.bfloat16)

        def clear(e, _):
            table[e] = zero_block
            return 0

        lax.fori_loop(0, group_blocks * group_blocks, clear, 0)

        pack_rows = pack_ref.shape[0] // (row_devices * col_devices)
        total_source = functools.reduce(
            jnp.add,
            [pack_ref[r * col_devices * pack_rows : r * col_devices * pack_rows + 1, :] for r in range(row_devices)],
        )
        targets = functools.reduce(
            jnp.add,
            [
                pack_ref[d * pack_rows + 1 + h : d * pack_rows + 2 + h, :]
                for d in range(row_devices * col_devices)
                for h in range(target_here)
            ],
        )
        total_target = jnp.sum(targets, axis=1, keepdims=True)
        log_source_ref[...] = jnp.log2(source_count * mass_ref[...].astype(jnp.float32) / total_source)
        scale_scr[...] = source_count / (total_source * (near_count * width))
        column_scr[...] = jnp.zeros_like(column_scr)
        for copy in table_copies:
            copy.wait()

        def mark(j, _):
            for m in range(link_count):
                table[j * group_blocks + link_ref[m, 0, j]] = j * link_count + m
            return 0

        lax.fori_loop(0, group_blocks, mark, 0)
        for s in range(row_devices):
            for h in range(target_here):
                j = (me ^ s) * target_here + h
                place = ((me ^ s) * col_devices + col) * pack_rows + 1 + h
                mass = target_count * pack_ref[pl.ds(place, 1), :] / total_target
                log_target_ref[pl.ds(j, 1), :] = jnp.log2(mass)
                tall = jnp.broadcast_to(mass, (width, width)).T
                for m in range(link_count):
                    block = cost_parts[s][0, h, m]
                    high, low = split(block)
                    far_high[j * link_count + m] = high
                    far_low[j * link_count + m] = low
                    spread = jnp.sum(tall * (block * block), axis=0, keepdims=True)
                    t = link_ref[m, 0, j]
                    column_scr[pl.ds(t, 1), :] += spread * (1.0 / (link_count * width))

    def out_copy(row):
        return pltpu.make_async_copy(cost_scr.at[row], out_ref.at[row], sems.at[row])

    group_devices = target_count // (group_blocks * width)
    coef = 2.0 * (1.0 / (near_count * width)) * (1.0 / (slots * group_devices * width))
    scale = scale_scr[0:1, 0:1]
    for i in range(rows):
        row = g * rows + i
        group = row - lax.rem(row, SUB)
        targets = [slot_ref[l, row] for l in range(slots)]
        far_rows = []
        for k in range(near_count):
            a = group + (near_index_ref[k, row] & (SUB - 1))
            for q in range(slots):
                j = slot_ref[q, a]
                far_rows.append([table[j * group_blocks + t] for t in targets])
        right_high = jnp.concatenate(
            [jnp.concatenate([far_high[e] for e in r], axis=1) for r in far_rows], axis=0
        )
        right_low = jnp.concatenate(
            [jnp.concatenate([far_low[e] for e in r], axis=1) for r in far_rows], axis=0
        )
        both = jnp.dot(x_ref[row], right_high, preferred_element_type=jnp.float32)
        rest = jnp.dot(x_ref[row, 0:width, :], right_low, preferred_element_type=jnp.float32)
        product = both[0:width] + (both[width:] + rest)
        tall = term_ref[row // SUB, :, i % SUB : i % SUB + 1] * scale
        scores = []
        for l in range(slots):
            cost = tall + column_scr[pl.ds(targets[l], 1), :] - coef * product[:, l * width : (l + 1) * width]
            cost_scr[row, 0, l] = cost
            select_ref[pl.ds(row * slots + l, 1), :] = jnp.full((1, width), targets[l], jnp.int32)
            scaled = cost * -to_log2
            work_ref[row, l] = scaled
            turned = scaled.T
            tall_ref[row, l] = turned
            scores.append(turned)
        out_copy(row).start()
        row_pass(scores, row, part_ref.shape[0], peak_scr, sum_scr)

    @pl.when(g == pl.num_programs(0) - 1)
    def _():
        part_ref[...] = row_sums(part_ref.shape[0], peak_scr, sum_scr)
        for row in range(all_rows):
            out_copy(row).wait()


def row_pass(scores, row, rows, peak_scr, sum_scr):
    for l, score in enumerate(scores):
        peak = jnp.max(score, axis=0, keepdims=True)
        peak_scr[pl.ds(l * rows + row, 1), :] = peak
        sum_scr[pl.ds(l * rows + row, 1), :] = jnp.sum(jnp.exp2(score - peak), axis=0, keepdims=True)


def row_sums(rows, peak_scr, sum_scr):
    slots = peak_scr.shape[0] // rows
    peaks = [peak_scr[l * rows : (l + 1) * rows, :] for l in range(slots)]
    sums = [sum_scr[l * rows : (l + 1) * rows, :] for l in range(slots)]
    peak = functools.reduce(jnp.maximum, peaks)
    total = functools.reduce(jnp.add, [t * jnp.exp2(p - peak) for p, t in zip(peaks, sums)])
    return peak + jnp.log2(total)


def column_kernel(copies, work_ref, select_ref, log_mass_ref, *refs):
    parts = refs[:-5]
    out_ref, potential_ref, potential_scr, peak_scr, sum_scr = refs[-5:]
    rows, slots, width, _ = work_ref.shape
    together = math.gcd(rows, 8)
    scaled = log_mass_ref[...] - log_sum([p[...] for p in parts])
    potential_scr[...] = scaled
    potential_ref[...] = scaled * from_log2

    for first in range(0, rows, together):
        tall = potential_scr[first : first + together, :].T
        for i in range(together):
            for l in range(slots):
                score = tall[:, i : i + 1] + work_ref[first + i, l]
                peak = jnp.max(score, axis=0, keepdims=True)
                total = jnp.sum(jnp.exp2(score - peak), axis=0, keepdims=True)
                place = (first + i) * slots + l
                peak_scr[place : place + 1, :] = peak
                sum_scr[place : place + 1, :] = total
    select = select_ref[...]
    peaks = peak_scr[...]
    sums = sum_scr[...]
    blocks = out_ref.shape[0] // copies
    for t in range(blocks):
        chosen = select == t
        peak = jnp.max(jnp.where(chosen, peaks, very_low), axis=0, keepdims=True)
        shifted = jnp.where(chosen, sums * jnp.exp2(jnp.minimum(peaks - peak, 0.0)), 0.0)
        total = jnp.sum(shifted, axis=0, keepdims=True)
        some = total > 0.0
        out_ref[t : t + 1, :] = jnp.where(
            some, peak + jnp.log2(jnp.where(some, total, 1.0)), very_low
        )
    if copies > 1:
        put_copies(out_ref, copies, out_ref[0:blocks, :])


def row_kernel(
    row_devices, slot_any, tall_ref, log_mass_ref, parts_ref, out_ref, wide_scr, peak_scr, sum_scr, slot_ref, sem
):
    rows, slots, width, _ = tall_ref.shape
    slot_copy = pltpu.make_async_copy(slot_any, slot_ref, sem)
    slot_copy.start()
    potential = (log_mass_ref[...] - log_sum(parts_of(parts_ref, row_devices))).T
    for t in range(wide_scr.shape[0]):
        wide_scr[t] = jnp.broadcast_to(potential[:, t : t + 1], (width, width))

    slot_copy.wait()
    for row in range(rows):
        scores = [wide_scr[slot_ref[l, row]] + tall_ref[row, l] for l in range(slots)]
        row_pass(scores, row, rows, peak_scr, sum_scr)
    out_ref[...] = row_sums(rows, peak_scr, sum_scr)


def last_kernel(row_devices, row_axis, log_mass_ref, parts_ref, out_ref):
    here = out_ref.shape[0]
    start = lax.axis_index(row_axis) * here
    log_mass = log_mass_ref[pl.ds(start, here), :]
    out_ref[...] = (log_mass - log_sum(parts_of(parts_ref, row_devices))) * from_log2


def per_device(
    coupling,
    coupling_index,
    near_cost,
    near_index,
    source_weights,
    target_cost,
    target_index,
    target_weights,
):
    rows_here = coupling.shape[0]
    slots = coupling.shape[2]
    width = coupling.shape[3]
    near_count = near_cost.shape[1]
    group_blocks = target_index.shape[1]
    link_count = target_index.shape[2]
    target_here = target_cost.shape[1]
    row_devices = lax.axis_size("rows")
    col_devices = lax.axis_size("cols")
    source_count = rows_here * row_devices * width
    target_count = group_blocks * width * col_devices
    f32 = jnp.float32
    half = row_devices // 2
    arrived = {0: target_cost}
    for mask in range(1, half + 1):
        arrived[mask] = send(target_cost, "rows", mask)

    near_t = in_hbm(near_index.T)
    slot_t = in_hbm(coupling_index[:, 0, :].T)
    link_t = in_hbm(jnp.transpose(target_index, (2, 0, 1)))
    mass = in_hbm(source_weights.reshape(rows_here, width))
    small = pltpu.CompilerParams(vmem_limit_bytes=4 * mib)

    pack_rows = 1 + target_here
    devices = row_devices * col_devices
    handed = [near_t, slot_t, link_t, mass]
    pack, near_t, slot_t, link_t, mass = pl.pallas_call(
        functools.partial(pack_kernel, devices),
        in_specs=[VMEM] * (2 + len(handed)),
        out_specs=[VMEM] * (1 + len(handed)),
        out_shape=[jax.ShapeDtypeStruct((devices * pack_rows, width), f32)]
        + [jax.ShapeDtypeStruct(a.shape, a.dtype) for a in handed],
        compiler_params=small,
        name="pack",
    )(mass, in_hbm(target_weights.reshape(target_here, width)), *handed)
    packs = exchange(pack, ("rows", "cols"))

    direct = list(range(1, half + 1))
    passed = pl.pallas_call(
        relay_kernel,
        in_specs=[ANY] * half,
        out_specs=[ANY] * half,
        out_shape=[jax.ShapeDtypeStruct(target_cost.shape, f32)] * half,
        input_output_aliases={e: e for e in range(half)},
        compiler_params=small,
        cost_estimate=pl.CostEstimate(flops=10**11, bytes_accessed=256 * mib, transcendentals=0),
        name="relay",
    )(*[arrived[mask] for mask in direct])
    arrived.update(zip(direct, passed))
    for mask in range(half + 1, row_devices):
        arrived[mask] = send(arrived[half], "rows", mask - half)
    cost_parts = [arrived[s] for s in range(row_devices)]

    wide = near_count * slots * width
    groups = rows_here // SUB
    step_rows = 2 * SUB if groups % 2 == 0 else SUB
    x, term = pl.pallas_call(
        near_kernel,
        grid=(rows_here // step_rows,),
        in_specs=[
            ANY,
            pl.BlockSpec((step_rows, near_count, width, width), lambda g: (g, 0, 0, 0)),
            pl.BlockSpec((step_rows, 1, slots, width, width), lambda g: (g, 0, 0, 0, 0)),
            whole((rows_here, width)),
            ANY,
        ],
        out_specs=[VMEM, VMEM],
        out_shape=[
            pltpu.VMEM((rows_here, 2 * width, wide), jnp.bfloat16),
            pltpu.VMEM((groups, width, SUB), f32),
        ],
        scratch_shapes=[
            pltpu.VMEM((step_rows, 3 * width, slots * width), jnp.bfloat16),
            pltpu.SMEM(near_t.shape, jnp.int32),
            pltpu.SemaphoreType.DMA,
        ],
        compiler_params=pltpu.CompilerParams(vmem_limit_bytes=12 * mib),
        cost_estimate=pl.CostEstimate(
            flops=6 * rows_here * wide * width * width,
            bytes_accessed=4 * rows_here * width * (near_count + slots) * width,
            transcendentals=0,
        ),
        name="near_product",
    )(near_t, in_hbm(near_cost), in_hbm(coupling), mass, packs)

    far_bytes = group_blocks * link_count * width * width * 4
    far_rows = 2 * step_rows if rows_here % (2 * step_rows) == 0 else step_rows
    steps = rows_here // far_rows
    work_shape = pltpu.VMEM((rows_here, slots, width, width), f32)
    cost_blocks, work, tall, row_part, log_source, log_target, select = pl.pallas_call(
        functools.partial(
            far_kernel,
            (row_devices, col_devices, target_here, source_count, target_count, group_blocks, link_count),
            "rows",
            "cols",
        ),
        grid=(steps,),
        in_specs=[ANY, ANY, ANY, VMEM, VMEM, whole((rows_here, width))]
        + [VMEM] * row_devices
        + [whole(packs.shape)],
        out_specs=[
            ANY,
            VMEM,
            VMEM,
            whole((rows_here, width)),
            whole((rows_here, width)),
            whole((group_blocks, width)),
            whole((rows_here * slots, width)),
        ],
        out_shape=[
            pltpu.HBM(coupling.shape, f32),
            work_shape,
            work_shape,
            jax.ShapeDtypeStruct((rows_here, width), f32),
            jax.ShapeDtypeStruct((rows_here, width), f32),
            jax.ShapeDtypeStruct((group_blocks, width), f32),
            jax.ShapeDtypeStruct((rows_here * slots, width), jnp.int32),
        ],
        scratch_shapes=[
            pltpu.VMEM((group_blocks * link_count + 1, width, width), jnp.bfloat16),
            pltpu.VMEM((group_blocks * link_count + 1, width, width), jnp.bfloat16),
            pltpu.SMEM((group_blocks * group_blocks,), jnp.int32),
            pltpu.VMEM((group_blocks, width), f32),
            pltpu.VMEM((1, width), f32),
            pltpu.VMEM((slots * rows_here, width), f32),
            pltpu.VMEM((slots * rows_here, width), f32),
            pltpu.VMEM(coupling.shape, f32),
            pltpu.SemaphoreType.DMA((rows_here,)),
            pltpu.SMEM(near_t.shape, jnp.int32),
            pltpu.SMEM(slot_t.shape, jnp.int32),
            pltpu.SMEM(link_t.shape, jnp.int32),
            pltpu.SemaphoreType.DMA((3,)),
        ],
        compiler_params=pltpu.CompilerParams(vmem_limit_bytes=12 * mib + 2 * far_bytes),
        name="far_product",
    )(near_t, slot_t, link_t, in_vmem(x), in_vmem(term), mass, *cost_parts, packs)

    pass_params = pltpu.CompilerParams(vmem_limit_bytes=12 * mib)

    def column_step(row_parts, copies):
        return pl.pallas_call(
            functools.partial(column_kernel, copies),
            in_specs=[VMEM] * (3 + len(row_parts)),
            out_specs=[VMEM, VMEM],
            out_shape=[
                jax.ShapeDtypeStruct((copies * group_blocks, width), f32),
                jax.ShapeDtypeStruct((rows_here, width), f32),
            ],
            scratch_shapes=[
                pltpu.VMEM((rows_here, width), f32),
                pltpu.VMEM((rows_here * slots, width), f32),
                pltpu.VMEM((rows_here * slots, width), f32),
            ],
            compiler_params=pass_params,
            name="column_pass",
        )(in_vmem(work), select, log_source, *row_parts)

    def row_step(column_parts):
        return pl.pallas_call(
            functools.partial(row_kernel, row_devices),
            in_specs=[ANY, VMEM, VMEM, VMEM],
            out_specs=VMEM,
            out_shape=jax.ShapeDtypeStruct((rows_here, width), f32),
            scratch_shapes=[
                pltpu.VMEM((group_blocks, width, width), f32),
                pltpu.VMEM((slots * rows_here, width), f32),
                pltpu.VMEM((slots * rows_here, width), f32),
                pltpu.SMEM((slots, rows_here), jnp.int32),
                pltpu.SemaphoreType.DMA,
            ],
            compiler_params=pass_params,
            name="row_pass",
        )(slot_t, in_vmem(tall), log_target, column_parts)

    for step in range(ITERS):
        last = step == ITERS - 1
        column_part, source_potential = column_step(
            from_all(row_part, "cols"), 1 if last else row_devices
        )
        column_parts = exchange(column_part, "rows")
        if not last:
            row_part = row_step(column_parts)
    own_target = pl.pallas_call(
        functools.partial(last_kernel, row_devices, "rows"),
        out_shape=jax.ShapeDtypeStruct((target_here, width), f32),
        compiler_params=small,
        name="last_potential",
    )(log_target, column_parts)
    return (
        cost_blocks,
        source_potential.reshape(rows_here * width),
        own_target.reshape(1, target_here * width),
    )


def solution(mesh):
    placed = (
        P("rows", "cols", None, None, None),
        P("rows", "cols", None),
        P("rows", None, None, None),
        P("rows", None),
        P("rows"),
        P("cols", "rows", None, None, None),
        P("cols", None, None),
        P("cols", "rows"),
    )
    return jax.shard_map(
        per_device,
        mesh=mesh,
        in_specs=placed,
        out_specs=(P("rows", "cols", None, None, None), P("rows"), P("cols", "rows")),
        check_vma=False,
    )
```

```python
import functools
import math

import jax
import jax.numpy as jnp
from jax import lax
from jax.experimental import pallas as pl
from jax.experimental.pallas import tpu as pltpu
from jax.sharding import PartitionSpec as P

ITERS = 3
SUB = 4

entropy = 0.01
to_log2 = math.log2(math.e) / entropy
from_log2 = entropy * math.log(2.0)
very_low = -1e30
mib = 1024 * 1024

SMEM = pl.BlockSpec(memory_space=pltpu.SMEM)
VMEM = pl.BlockSpec(memory_space=pltpu.VMEM)
ANY = pl.BlockSpec(memory_space=pl.ANY)


def in_hbm(x):
    return pltpu.with_memory_space_constraint(x, pltpu.HBM)


def in_vmem(x):
    return pltpu.with_memory_space_constraint(x, pltpu.VMEM)


def whole(shape):
    return pl.BlockSpec(shape, lambda *_: (0,) * len(shape))


def split(x):
    high = x.astype(jnp.bfloat16)
    return high, (x - high.astype(jnp.float32)).astype(jnp.bfloat16)


def tree(parts, op):
    while len(parts) > 1:
        half = len(parts) // 2
        parts = [op(parts[s], parts[s + half]) for s in range(half)]
    return parts[0]


def log_sum(parts):
    peak = tree(parts, jnp.maximum)
    return peak + jnp.log2(tree([jnp.exp2(p - peak) for p in parts], jnp.add))


def parts_of(ref, devices):
    rows = ref.shape[0] // devices
    return [ref[d * rows : (d + 1) * rows, :] for d in range(devices)]


def put_copies(ref, devices, value):
    rows = value.shape[0]
    for d in range(devices):
        ref[d * rows : (d + 1) * rows, :] = value


def send(x, axis, mask):
    size = lax.axis_size(axis)
    return lax.ppermute(x, axis, [(d, d ^ mask) for d in range(size)])


def from_all(x, axis):
    return [x] + [send(x, axis, s) for s in range(1, lax.axis_size(axis))]


def exchange(copies, axis):
    return lax.all_to_all(copies, axis, 0, 0, tiled=True)


def pack_kernel(devices, source_ref, target_ref, *refs):
    small = (len(refs) - 1) // 2
    out_ref = refs[small]
    rows = out_ref.shape[0] // devices
    total = jnp.sum(source_ref[...].astype(jnp.float32), axis=(0, 1), keepdims=True)
    target = target_ref[...].astype(jnp.float32)
    for d in range(devices):
        out_ref[d * rows : d * rows + 1, :] = jnp.broadcast_to(total, (1, out_ref.shape[1]))
        out_ref[d * rows + 1 : d * rows + 1 + target.shape[0], :] = target
    for from_ref, to_ref in zip(refs[:small], refs[small + 1 :]):
        to_ref[...] = from_ref[...]


def near_kernel(
    near_any, cost_ref, plan_ref, mass_ref, totals_ref, x_ref, term_ref, plan_scr, near_index_ref, sem
):
    index_copy = pltpu.make_async_copy(near_any, near_index_ref, sem)
    pl.when(pl.program_id(0) == 0)(index_copy.start)
    rows = cost_ref.shape[0]
    first = pl.program_id(0) * rows
    near_count = cost_ref.shape[1]
    width = cost_ref.shape[2]
    slots = plan_ref.shape[2]
    wide = slots * width
    for a in range(rows):
        plan = jnp.concatenate([plan_ref[a, 0, q] for q in range(slots)], axis=1)
        high, low = split(plan)
        plan_scr[a, 0:width, :] = high
        plan_scr[a, width : 2 * width, :] = low
        plan_scr[a, 2 * width : 3 * width, :] = high
    pl.when(pl.program_id(0) == 0)(index_copy.wait)
    lanes = lax.broadcasted_iota(jnp.int32, (width, SUB), 1)
    for group in range(rows // SUB):
        terms = jnp.zeros((width, SUB), jnp.float32)
        for i in range(group * SUB, (group + 1) * SUB):
            acc = None
            for k in range(near_count):
                a = group * SUB + (near_index_ref[k, first + i] & (SUB - 1))
                cost = cost_ref[i, k]
                high, low = split(cost)
                x = jnp.dot(
                    jnp.concatenate([high, high, low], axis=1),
                    plan_scr[a],
                    preferred_element_type=jnp.float32,
                )
                x_high, x_low = split(x)
                x_ref[first + i, 0:width, k * wide : (k + 1) * wide] = x_high
                x_ref[first + i, width : 2 * width, k * wide : (k + 1) * wide] = x_low
                weighted = cost * cost * mass_ref[pl.ds(first + a, 1), :].astype(jnp.float32)
                acc = weighted if acc is None else acc + weighted
            terms = jnp.where(lanes == i % SUB, jnp.sum(acc, axis=1, keepdims=True), terms)
        term_ref[first // SUB + group] = terms


def relay_kernel(*refs):
    pass


def far_kernel(counts, row_axis, col_axis, *refs):
    row_devices, col_devices, target_here, source_count, target_count, group_blocks, link_count = counts
    tables, (x_ref, term_ref, mass_ref) = refs[:3], refs[3:6]
    cost_parts = refs[6 : 6 + row_devices]
    pack_ref, out_ref, work_ref, tall_ref, part_ref, log_source_ref, log_target_ref, select_ref = refs[
        6 + row_devices : 14 + row_devices
    ]
    far_high, far_low, table, column_scr, scale_scr, peak_scr, sum_scr, cost_scr, sems = refs[14 + row_devices : -4]
    near_index_ref, slot_ref, link_ref, table_sems = refs[-4:]
    g = pl.program_id(0)
    near_count = near_index_ref.shape[0]
    slots = slot_ref.shape[0]
    all_rows = out_ref.shape[0]
    rows = all_rows // pl.num_programs(0)
    width = out_ref.shape[3]
    zero_block = group_blocks * link_count

    @pl.when(g == 0)
    def _():
        table_copies = [
            pltpu.make_async_copy(table_any, table_ref, table_sems.at[e])
            for e, (table_any, table_ref) in enumerate(zip(tables, (near_index_ref, slot_ref, link_ref)))
        ]
        for copy in table_copies:
            copy.start()
        me = lax.axis_index(row_axis)
        col = lax.axis_index(col_axis)
        far_high[zero_block] = jnp.zeros((width, width), jnp.bfloat16)
        far_low[zero_block] = jnp.zeros((width, width), jnp.bfloat16)

        def clear(e, _):
            table[e] = zero_block
            return 0

        lax.fori_loop(0, group_blocks * group_blocks, clear, 0)

        pack_rows = pack_ref.shape[0] // (row_devices * col_devices)
        total_source = functools.reduce(
            jnp.add,
            [pack_ref[r * col_devices * pack_rows : r * col_devices * pack_rows + 1, :] for r in range(row_devices)],
        )
        targets = functools.reduce(
            jnp.add,
            [
                pack_ref[d * pack_rows + 1 + h : d * pack_rows + 2 + h, :]
                for d in range(row_devices * col_devices)
                for h in range(target_here)
            ],
        )
        total_target = jnp.sum(targets, axis=1, keepdims=True)
        log_source_ref[...] = jnp.log2(source_count * mass_ref[...].astype(jnp.float32) / total_source)
        scale_scr[...] = source_count / (total_source * (near_count * width))
        column_scr[...] = jnp.zeros_like(column_scr)
        for copy in table_copies:
            copy.wait()

        def mark(j, _):
            for m in range(link_count):
                table[j * group_blocks + link_ref[m, 0, j]] = j * link_count + m
            return 0

        lax.fori_loop(0, group_blocks, mark, 0)
        for s in range(row_devices):
            for h in range(target_here):
                j = (me ^ s) * target_here + h
                place = ((me ^ s) * col_devices + col) * pack_rows + 1 + h
                mass = target_count * pack_ref[pl.ds(place, 1), :] / total_target
                log_target_ref[pl.ds(j, 1), :] = jnp.log2(mass)
                tall = jnp.broadcast_to(mass, (width, width)).T
                for m in range(link_count):
                    block = cost_parts[s][0, h, m]
                    high, low = split(block)
                    far_high[j * link_count + m] = high
                    far_low[j * link_count + m] = low
                    spread = jnp.sum(tall * (block * block), axis=0, keepdims=True)
                    t = link_ref[m, 0, j]
                    column_scr[pl.ds(t, 1), :] += spread * (1.0 / (link_count * width))

    def out_copy(row):
        return pltpu.make_async_copy(cost_scr.at[row], out_ref.at[row], sems.at[row])

    group_devices = target_count // (group_blocks * width)
    coef = 2.0 * (1.0 / (near_count * width)) * (1.0 / (slots * group_devices * width))
    scale = scale_scr[0:1, 0:1]
    for i in range(rows):
        row = g * rows + i
        group = row - lax.rem(row, SUB)
        targets = [slot_ref[l, row] for l in range(slots)]
        far_rows = []
        for k in range(near_count):
            a = group + (near_index_ref[k, row] & (SUB - 1))
            for q in range(slots):
                j = slot_ref[q, a]
                far_rows.append([table[j * group_blocks + t] for t in targets])
        right_high = jnp.concatenate(
            [jnp.concatenate([far_high[e] for e in r], axis=1) for r in far_rows], axis=0
        )
        right_low = jnp.concatenate(
            [jnp.concatenate([far_low[e] for e in r], axis=1) for r in far_rows], axis=0
        )
        both = jnp.dot(x_ref[row], right_high, preferred_element_type=jnp.float32)
        rest = jnp.dot(x_ref[row, 0:width, :], right_low, preferred_element_type=jnp.float32)
        product = both[0:width] + (both[width:] + rest)
        tall = term_ref[row // SUB, :, i % SUB : i % SUB + 1] * scale
        scores = []
        for l in range(slots):
            cost = tall + column_scr[pl.ds(targets[l], 1), :] - coef * product[:, l * width : (l + 1) * width]
            cost_scr[row, 0, l] = cost
            select_ref[pl.ds(row * slots + l, 1), :] = jnp.full((1, width), targets[l], jnp.int32)
            scaled = cost * -to_log2
            work_ref[row, l] = scaled
            turned = scaled.T
            tall_ref[row, l] = turned
            scores.append(turned)
        out_copy(row).start()
        row_pass(scores, row, part_ref.shape[0], peak_scr, sum_scr)

    @pl.when(g == pl.num_programs(0) - 1)
    def _():
        part_ref[...] = row_sums(part_ref.shape[0], peak_scr, sum_scr)
        for row in range(all_rows):
            out_copy(row).wait()


def row_pass(scores, row, rows, peak_scr, sum_scr):
    for l, score in enumerate(scores):
        peak = jnp.max(score, axis=0, keepdims=True)
        peak_scr[pl.ds(l * rows + row, 1), :] = peak
        sum_scr[pl.ds(l * rows + row, 1), :] = jnp.sum(jnp.exp2(score - peak), axis=0, keepdims=True)


def row_sums(rows, peak_scr, sum_scr):
    slots = peak_scr.shape[0] // rows
    peaks = [peak_scr[l * rows : (l + 1) * rows, :] for l in range(slots)]
    sums = [sum_scr[l * rows : (l + 1) * rows, :] for l in range(slots)]
    peak = functools.reduce(jnp.maximum, peaks)
    total = functools.reduce(jnp.add, [t * jnp.exp2(p - peak) for p, t in zip(peaks, sums)])
    return peak + jnp.log2(total)


def column_kernel(copies, work_ref, select_ref, log_mass_ref, *refs):
    parts = refs[:-5]
    out_ref, potential_ref, potential_scr, peak_scr, sum_scr = refs[-5:]
    rows, slots, width, _ = work_ref.shape
    together = math.gcd(rows, 8)
    scaled = log_mass_ref[...] - log_sum([p[...] for p in parts])
    potential_scr[...] = scaled
    potential_ref[...] = scaled * from_log2

    for first in range(0, rows, together):
        tall = potential_scr[first : first + together, :].T
        for i in range(together):
            for l in range(slots):
                score = tall[:, i : i + 1] + work_ref[first + i, l]
                peak = jnp.max(score, axis=0, keepdims=True)
                total = jnp.sum(jnp.exp2(score - peak), axis=0, keepdims=True)
                place = (first + i) * slots + l
                peak_scr[place : place + 1, :] = peak
                sum_scr[place : place + 1, :] = total
    select = select_ref[...]
    peaks = peak_scr[...]
    sums = sum_scr[...]
    blocks = out_ref.shape[0] // copies
    for t in range(blocks):
        chosen = select == t
        peak = jnp.max(jnp.where(chosen, peaks, very_low), axis=0, keepdims=True)
        shifted = jnp.where(chosen, sums * jnp.exp2(jnp.minimum(peaks - peak, 0.0)), 0.0)
        total = jnp.sum(shifted, axis=0, keepdims=True)
        some = total > 0.0
        out_ref[t : t + 1, :] = jnp.where(
            some, peak + jnp.log2(jnp.where(some, total, 1.0)), very_low
        )
    if copies > 1:
        put_copies(out_ref, copies, out_ref[0:blocks, :])


def row_kernel(
    row_devices, slot_any, tall_ref, log_mass_ref, parts_ref, out_ref, wide_scr, peak_scr, sum_scr, slot_ref, sem
):
    rows, slots, width, _ = tall_ref.shape
    slot_copy = pltpu.make_async_copy(slot_any, slot_ref, sem)
    slot_copy.start()
    potential = (log_mass_ref[...] - log_sum(parts_of(parts_ref, row_devices))).T
    for t in range(wide_scr.shape[0]):
        wide_scr[t] = jnp.broadcast_to(potential[:, t : t + 1], (width, width))

    slot_copy.wait()
    for row in range(rows):
        scores = [wide_scr[slot_ref[l, row]] + tall_ref[row, l] for l in range(slots)]
        row_pass(scores, row, rows, peak_scr, sum_scr)
    out_ref[...] = row_sums(rows, peak_scr, sum_scr)


def last_kernel(row_devices, row_axis, log_mass_ref, parts_ref, out_ref):
    here = out_ref.shape[0]
    start = lax.axis_index(row_axis) * here
    log_mass = log_mass_ref[pl.ds(start, here), :]
    out_ref[...] = (log_mass - log_sum(parts_of(parts_ref, row_devices))) * from_log2


def per_device(
    coupling,
    coupling_index,
    near_cost,
    near_index,
    source_weights,
    target_cost,
    target_index,
    target_weights,
):
    rows_here = coupling.shape[0]
    slots = coupling.shape[2]
    width = coupling.shape[3]
    near_count = near_cost.shape[1]
    group_blocks = target_index.shape[1]
    link_count = target_index.shape[2]
    target_here = target_cost.shape[1]
    row_devices = lax.axis_size("rows")
    col_devices = lax.axis_size("cols")
    source_count = rows_here * row_devices * width
    target_count = group_blocks * width * col_devices
    f32 = jnp.float32
    half = row_devices // 2
    arrived = {0: target_cost}
    for mask in range(1, half + 1):
        arrived[mask] = send(target_cost, "rows", mask)

    near_t = in_hbm(near_index.T)
    slot_t = in_hbm(coupling_index[:, 0, :].T)
    link_t = in_hbm(jnp.transpose(target_index, (2, 0, 1)))
    mass = in_hbm(source_weights.reshape(rows_here, width))
    small = pltpu.CompilerParams(vmem_limit_bytes=4 * mib)

    pack_rows = 1 + target_here
    devices = row_devices * col_devices
    handed = [near_t, slot_t, link_t, mass]
    pack, near_t, slot_t, link_t, mass = pl.pallas_call(
        functools.partial(pack_kernel, devices),
        in_specs=[VMEM] * (2 + len(handed)),
        out_specs=[VMEM] * (1 + len(handed)),
        out_shape=[jax.ShapeDtypeStruct((devices * pack_rows, width), f32)]
        + [jax.ShapeDtypeStruct(a.shape, a.dtype) for a in handed],
        compiler_params=small,
        name="pack",
    )(mass, in_hbm(target_weights.reshape(target_here, width)), *handed)
    packs = exchange(pack, ("rows", "cols"))

    direct = list(range(1, half + 1))
    passed = pl.pallas_call(
        relay_kernel,
        in_specs=[ANY] * half,
        out_specs=[ANY] * half,
        out_shape=[jax.ShapeDtypeStruct(target_cost.shape, f32)] * half,
        input_output_aliases={e: e for e in range(half)},
        compiler_params=small,
        cost_estimate=pl.CostEstimate(flops=10**11, bytes_accessed=256 * mib, transcendentals=0),
        name="relay",
    )(*[arrived[mask] for mask in direct])
    arrived.update(zip(direct, passed))
    for mask in range(half + 1, row_devices):
        arrived[mask] = send(arrived[half], "rows", mask - half)
    cost_parts = [arrived[s] for s in range(row_devices)]

    wide = near_count * slots * width
    groups = rows_here // SUB
    step_rows = 2 * SUB if groups % 2 == 0 else SUB
    x, term = pl.pallas_call(
        near_kernel,
        grid=(rows_here // step_rows,),
        in_specs=[
            ANY,
            pl.BlockSpec((step_rows, near_count, width, width), lambda g: (g, 0, 0, 0)),
            pl.BlockSpec((step_rows, 1, slots, width, width), lambda g: (g, 0, 0, 0, 0)),
            whole((rows_here, width)),
            ANY,
        ],
        out_specs=[VMEM, VMEM],
        out_shape=[
            pltpu.VMEM((rows_here, 2 * width, wide), jnp.bfloat16),
            pltpu.VMEM((groups, width, SUB), f32),
        ],
        scratch_shapes=[
            pltpu.VMEM((step_rows, 3 * width, slots * width), jnp.bfloat16),
            pltpu.SMEM(near_t.shape, jnp.int32),
            pltpu.SemaphoreType.DMA,
        ],
        compiler_params=pltpu.CompilerParams(vmem_limit_bytes=12 * mib),
        cost_estimate=pl.CostEstimate(
            flops=6 * rows_here * wide * width * width,
            bytes_accessed=4 * rows_here * width * (near_count + slots) * width,
            transcendentals=0,
        ),
        name="near_product",
    )(near_t, in_hbm(near_cost), in_hbm(coupling), mass, packs)

    far_bytes = group_blocks * link_count * width * width * 4
    far_rows = rows_here
    steps = rows_here // far_rows
    work_shape = pltpu.VMEM((rows_here, slots, width, width), f32)
    cost_blocks, work, tall, row_part, log_source, log_target, select = pl.pallas_call(
        functools.partial(
            far_kernel,
            (row_devices, col_devices, target_here, source_count, target_count, group_blocks, link_count),
            "rows",
            "cols",
        ),
        grid=(steps,),
        in_specs=[ANY, ANY, ANY, VMEM, VMEM, whole((rows_here, width))]
        + [VMEM] * row_devices
        + [whole(packs.shape)],
        out_specs=[
            ANY,
            VMEM,
            VMEM,
            whole((rows_here, width)),
            whole((rows_here, width)),
            whole((group_blocks, width)),
            whole((rows_here * slots, width)),
        ],
        out_shape=[
            pltpu.HBM(coupling.shape, f32),
            work_shape,
            work_shape,
            jax.ShapeDtypeStruct((rows_here, width), f32),
            jax.ShapeDtypeStruct((rows_here, width), f32),
            jax.ShapeDtypeStruct((group_blocks, width), f32),
            jax.ShapeDtypeStruct((rows_here * slots, width), jnp.int32),
        ],
        scratch_shapes=[
            pltpu.VMEM((group_blocks * link_count + 1, width, width), jnp.bfloat16),
            pltpu.VMEM((group_blocks * link_count + 1, width, width), jnp.bfloat16),
            pltpu.SMEM((group_blocks * group_blocks,), jnp.int32),
            pltpu.VMEM((group_blocks, width), f32),
            pltpu.VMEM((1, width), f32),
            pltpu.VMEM((slots * rows_here, width), f32),
            pltpu.VMEM((slots * rows_here, width), f32),
            pltpu.VMEM(coupling.shape, f32),
            pltpu.SemaphoreType.DMA((rows_here,)),
            pltpu.SMEM(near_t.shape, jnp.int32),
            pltpu.SMEM(slot_t.shape, jnp.int32),
            pltpu.SMEM(link_t.shape, jnp.int32),
            pltpu.SemaphoreType.DMA((3,)),
        ],
        compiler_params=pltpu.CompilerParams(vmem_limit_bytes=12 * mib + 2 * far_bytes),
        name="far_product",
    )(near_t, slot_t, link_t, in_vmem(x), in_vmem(term), mass, *cost_parts, packs)

    pass_params = pltpu.CompilerParams(vmem_limit_bytes=12 * mib)

    def column_step(row_parts, copies):
        return pl.pallas_call(
            functools.partial(column_kernel, copies),
            in_specs=[VMEM] * (3 + len(row_parts)),
            out_specs=[VMEM, VMEM],
            out_shape=[
                jax.ShapeDtypeStruct((copies * group_blocks, width), f32),
                jax.ShapeDtypeStruct((rows_here, width), f32),
            ],
            scratch_shapes=[
                pltpu.VMEM((rows_here, width), f32),
                pltpu.VMEM((rows_here * slots, width), f32),
                pltpu.VMEM((rows_here * slots, width), f32),
            ],
            compiler_params=pass_params,
            name="column_pass",
        )(in_vmem(work), select, log_source, *row_parts)

    def row_step(column_parts):
        return pl.pallas_call(
            functools.partial(row_kernel, row_devices),
            in_specs=[ANY, VMEM, VMEM, VMEM],
            out_specs=VMEM,
            out_shape=jax.ShapeDtypeStruct((rows_here, width), f32),
            scratch_shapes=[
                pltpu.VMEM((group_blocks, width, width), f32),
                pltpu.VMEM((slots * rows_here, width), f32),
                pltpu.VMEM((slots * rows_here, width), f32),
                pltpu.SMEM((slots, rows_here), jnp.int32),
                pltpu.SemaphoreType.DMA,
            ],
            compiler_params=pass_params,
            name="row_pass",
        )(slot_t, in_vmem(tall), log_target, column_parts)

    for step in range(ITERS):
        last = step == ITERS - 1
        column_part, source_potential = column_step(
            from_all(row_part, "cols"), 1 if last else row_devices
        )
        column_parts = exchange(column_part, "rows")
        if not last:
            row_part = row_step(column_parts)
    own_target = pl.pallas_call(
        functools.partial(last_kernel, row_devices, "rows"),
        out_shape=jax.ShapeDtypeStruct((target_here, width), f32),
        compiler_params=small,
        name="last_potential",
    )(log_target, column_parts)
    return (
        cost_blocks,
        source_potential.reshape(rows_here * width),
        own_target.reshape(1, target_here * width),
    )


def solution(mesh):
    placed = (
        P("rows", "cols", None, None, None),
        P("rows", "cols", None),
        P("rows", None, None, None),
        P("rows", None),
        P("rows"),
        P("cols", "rows", None, None, None),
        P("cols", None, None),
        P("cols", "rows"),
    )
    return jax.shard_map(
        per_device,
        mesh=mesh,
        in_specs=placed,
        out_specs=(P("rows", "cols", None, None, None), P("rows"), P("cols", "rows")),
        check_vma=False,
    )
```
